128 devices in a mesh: section: 2 (over x_hi), dp: 4 (over y), ctx: 16 (over x_lo, z, core).
Axes of the slice: x: 4 (x_hi: 2, x_lo: 2; x = x_hi * 2 + x_lo), y: 4, z: 4, core: 2. Of those that a mesh axis runs over, the one named last changes fastest.
Arguments:
- inputs: bfloat16 [2, 8192, 512], P(None, ('dp', 'ctx')), may hold values from -6 to 6
- lengths: int32 [4, 2, 3], P('dp'), may hold values from 1 to 2046, as said below
- norm_gain: bfloat16 [2, 2, 512], P('section'), may hold values from 0.5 to 1.5
- norm_bias: bfloat16 [2, 2, 512], P('section'), may hold values from -1 to 1
- qkv_weight: bfloat16 [2, 512, 1536], P('section'), may hold values from -0.25 to 0.25
- qkv_bias: bfloat16 [2, 1536], P('section'), may hold values from -1 to 1
- proj_weight: bfloat16 [2, 512, 512], P('section'), may hold values from -2 to 2
- up_weight: bfloat16 [2, 512, 2048], P('section'), may hold values from -0.25 to 0.25
- up_bias: bfloat16 [2, 2048], P('section'), may hold values from -1 to 1
- down_weight: bfloat16 [2, 2048, 512], P('section'), may hold values from -0.125 to 0.125
- branch_bias: bfloat16 [2, 2, 512], P('section'), may hold values from -1 to 1
- cotangent: bfloat16 [2, 8192, 512], P(None, ('dp', 'ctx')), may hold values from -6 to 6
Outputs:
- block_out: bfloat16 [2, 2, 8192, 512], P('section', None, ('dp', 'ctx'))
- input_grads: bfloat16 [2, 2, 8192, 512], P('section', None, ('dp', 'ctx'))
- norm_gain_grad: float32 [2, 2, 512], P('section')
- norm_bias_grad: float32 [2, 2, 512], P('section')
- qkv_weight_grad: float32 [2, 512, 1536], P('section')
- qkv_bias_grad: float32 [2, 1536], P('section')
- proj_weight_grad: float32 [2, 512, 512], P('section')
- up_weight_grad: float32 [2, 512, 2048], P('section')
- up_bias_grad: float32 [2, 2048], P('section')
- down_weight_grad: float32 [2, 2048, 512], P('section')
- branch_bias_grad: float32 [2, 2, 512], P('section')
The draws below stay inside these ranges and needn't reach their ends.
Inputs may be any that keep to these rules, and one draw needn't show every extreme that they name: lengths[g, m, :] holds 3 sequence lengths that sum to 2048.
All inputs are finite; a program needn't handle non-finite values.
Results may differ from the reference program's by a relative error of at most 0.02.
Values may be sent and summed in bfloat16 or wider, within the bound.
No kernel may reach another device: no remote copies, remote signals or barrier semaphores. Data moves between devices by JAX's collectives and lax.ppermute only.
A program may use at most 192 MiB of HBM per device.

```python
import math
import jax
import jax.numpy as jnp
from jax import lax

D = 512
HEADS = 8
FF = 2048
MICRO = 2
SEQS = 3
GROUP = 2048
TOKENS = 8192
N_DP = 4
N_CTX = 16


def draw_lengths(key, part):
    key = jax.random.fold_in(key, 11)
    span_rows = GROUP // N_CTX
    row_keys = jax.random.split(key, N_DP * MICRO)
    micro_index = jnp.tile(jnp.arange(MICRO, dtype=jnp.int32), N_DP)
    row_number = jnp.arange(N_DP * MICRO, dtype=jnp.int32)

    def one_row(row_key, batch_index, row_id):
        first_key, second_key, third_key = jax.random.split(row_key, 3)
        narrow = jax.random.randint(first_key, (2,), 1, (span_rows - 1) // 2 + 1).astype(jnp.int32)
        broad = jax.random.randint(third_key, (2,), 1, GROUP // 4 + 1).astype(jnp.int32)
        sides = jnp.where(batch_index == 0, narrow, broad).astype(jnp.int32)
        sides = jnp.where(row_id == 0, jnp.ones((2,), jnp.int32), sides).astype(jnp.int32)
        longest = GROUP - sides[0] - sides[1]
        slot = jax.random.randint(second_key, (), 0, 3)
        placed = jnp.where(slot == 0, jnp.stack([longest, sides[0], sides[1]]), jnp.where(slot == 1, jnp.stack([sides[0], longest, sides[1]]), jnp.stack([sides[0], sides[1], longest])))
        return placed.astype(jnp.int32)
    rows_all = jax.vmap(one_row)(row_keys, micro_index, row_number)
    return rows_all.reshape(N_DP, MICRO, SEQS).astype(jnp.int32)


def level_of(stream_key, extent, pieces, low, high):
    factor_of, own = 1.0, jax.random.fold_in(stream_key, 6)
    for axis_at, blocks in pieces:
        steps = jnp.exp(jax.random.uniform(jax.random.fold_in(own, axis_at), (blocks,), jnp.float32, low / len(pieces), high / len(pieces)))
        factor_of = factor_of * jnp.repeat(steps, extent[axis_at] // blocks).reshape([-1 if axis == axis_at else 1 for axis in range(len(extent))])
    return factor_of


def bell_draw(key, shape, width, limit, pieces=(), kind=jnp.bfloat16):
    level = level_of(key, shape, pieces, -0.22, 0.18) if pieces else 1.0
    entries = jax.random.normal(key, shape, jnp.float32) * width * level
    return jnp.minimum(jnp.maximum(entries, -limit), limit).astype(kind)


def setup_inputs(seed: int = 0) -> dict:
    key_of = jax.random.split(jax.random.key(seed), 13)
    inputs = bell_draw(key_of[0], (MICRO, TOKENS, D), 1.0, 6.0, ((1, 64),))
    lengths = draw_lengths(jax.random.fold_in(key_of[12], 71), 0)
    norm_gain = jnp.clip(1.0 + 0.1 * jax.random.normal(key_of[2], (2, 2, D), jnp.float32), 0.5, 1.5).astype(jnp.bfloat16)
    norm_bias = bell_draw(key_of[3], (2, 2, D), 0.2, 1.0, ((0, 2),))
    qkv_weight = bell_draw(key_of[4], (2, D, 3 * D), D ** -0.5, 0.25, ((0, 2),))
    qkv_bias = bell_draw(key_of[5], (2, 3 * D), 0.2, 1.0, ((0, 2),))
    proj_weight = bell_draw(key_of[6], (2, D, D), (max(D // 64, 1)) ** -0.5, 2.0, ((0, 2),))
    up_weight = bell_draw(key_of[7], (2, D, FF), D ** -0.5, 0.25, ((0, 2),))
    up_bias = bell_draw(key_of[8], (2, FF), 0.2, 1.0, ((0, 2),))
    down_weight = bell_draw(key_of[9], (2, FF, D), FF ** -0.5, 0.125, ((0, 2),))
    branch_bias = bell_draw(key_of[10], (2, 2, D), 0.2, 1.0, ((0, 2),))
    cotangent = bell_draw(key_of[11], (MICRO, TOKENS, D), 1.0, 6.0, ((1, 64),))
    return dict(inputs=inputs, lengths=lengths, norm_gain=norm_gain, norm_bias=norm_bias, qkv_weight=qkv_weight, qkv_bias=qkv_bias, proj_weight=proj_weight, up_weight=up_weight, up_bias=up_bias, down_weight=down_weight, branch_bias=branch_bias, cotangent=cotangent)


@jax.custom_vjp
def low(v):
    return lax.optimization_barrier(v.astype(jnp.bfloat16)).astype(jnp.float32)

@jax.custom_vjp
def low_back(v):
    return v

def low_keep(v):
    return (low(v), None)

def low_pass(kept, grad):
    return (grad,)

def back_keep(v):
    return (v, None)

def back_low(kept, grad):
    return (low(grad),)
low.defvjp(low_keep, low_pass)
low_back.defvjp(back_keep, back_low)
EPS = 1e-05
PRECISE = lax.Precision.HIGHEST

def layer_norm(values, gain_row, bias_row):
    row_mean = lax.optimization_barrier(jnp.mean(values, -1, keepdims=True))
    centred = values - row_mean
    spread = lax.optimization_barrier(jnp.mean(centred * centred, -1, keepdims=True))
    return centred * lax.rsqrt(spread + EPS) * gain_row + bias_row

def rotary(values, position, turn):
    head_dim = values.shape[-1] // HEADS
    quarter = head_dim // 4
    half_rot = quarter // 2
    shaped = values.reshape(values.shape[:-1] + (HEADS, head_dim))
    ladder = jnp.arange(half_rot, dtype=jnp.float32) * (2.0 / quarter)
    frequency = jnp.exp(-math.log(10000.0) * ladder)
    angle = position.astype(jnp.float32)[..., None] * frequency
    cosine = jnp.cos(angle)[..., None, :]
    sine = turn * jnp.sin(angle)[..., None, :]
    first = shaped[..., :half_rot]
    second = shaped[..., half_rot:quarter]
    turned = jnp.concatenate([first * cosine - second * sine, second * cosine + first * sine, shaped[..., quarter:]], -1)
    return turned.reshape(values.shape)

def places(seq_lengths):
    row_index = jnp.arange(GROUP, dtype=jnp.int32)
    ends = jnp.cumsum(seq_lengths, -1).astype(jnp.int32)
    after = row_index[:, None] >= ends[..., None, :]
    segment = lax.optimization_barrier(jnp.sum(after.astype(jnp.int32), -1)).astype(jnp.int32)
    begin = lax.optimization_barrier(jnp.sum(jnp.where(after, seq_lengths[..., None, :], 0), -1)).astype(jnp.int32)
    return (segment, row_index - begin)

def attend(packed):
    queries, key_rows, value_rows, segment = packed
    head_dim = D // HEADS
    row_index = jnp.arange(GROUP, dtype=jnp.int32)
    query_heads = queries.reshape(GROUP, HEADS, head_dim)
    key_heads = key_rows.reshape(GROUP, HEADS, head_dim)
    value_heads = value_rows.reshape(GROUP, HEADS, head_dim)
    scores = jnp.einsum('qhd,khd->hqk', query_heads, key_heads, precision=PRECISE) * (1.0 / math.sqrt(head_dim))
    scores = low_back(scores)
    allowed = (segment[:, None] == segment[None, :]) & (row_index[:, None] >= row_index[None, :])
    scores = jnp.where(allowed[None], scores, -1e+30)
    row_max = lax.optimization_barrier(jnp.max(scores, -1, keepdims=True))
    weights = jnp.exp(scores - row_max)
    probs = low(weights / lax.optimization_barrier(jnp.sum(weights, -1, keepdims=True)))
    return jnp.einsum('hqk,khd->qhd', probs, value_heads, precision=PRECISE).reshape(GROUP, D)

def residual_block(hidden, params, segment, position):
    gains, shifts, w_qkv, b_qkv, w_proj, w_up, b_up, w_down, b_branch = params
    normed = low(layer_norm(hidden, gains[0], shifts[0]))
    qkv_pre = low_back(jnp.dot(normed, w_qkv, precision=PRECISE) + b_qkv)
    queries = low(rotary(qkv_pre[..., :D], position, 1.0))
    key_rows = low(rotary(qkv_pre[..., D:2 * D], position, 1.0))
    value_rows = low(qkv_pre[..., 2 * D:])
    flat_count = MICRO * N_DP
    attn_out = lax.map(jax.checkpoint(attend), (queries.reshape(flat_count, GROUP, D), key_rows.reshape(flat_count, GROUP, D), value_rows.reshape(flat_count, GROUP, D), segment.reshape(flat_count, GROUP)))
    attn_out = low(low_back(attn_out.reshape(hidden.shape)))
    attn = low_back(jnp.dot(attn_out, w_proj, precision=PRECISE) + b_branch[0])
    second = low(layer_norm(hidden, gains[1], shifts[1]))
    up_pre = low_back(jnp.dot(second, w_up, precision=PRECISE) + b_up)
    active = low(jax.nn.gelu(up_pre, approximate=False))
    mlp = low_back(jnp.dot(active, w_down, precision=PRECISE) + b_branch[1])
    return hidden + attn + mlp

def reference(inputs, lengths, norm_gain, norm_bias, qkv_weight, qkv_bias, proj_weight, up_weight, up_bias, down_weight, branch_bias, cotangent):
    segment, position = places(lengths)
    segment = jnp.transpose(segment, (1, 0, 2))
    position = jnp.transpose(position, (1, 0, 2))
    start = inputs.astype(jnp.float32).reshape(MICRO, N_DP, GROUP, D)
    params = [norm_gain, norm_bias, qkv_weight, qkv_bias, proj_weight, up_weight, up_bias, down_weight, branch_bias]
    params = [item.astype(jnp.float32) for item in params]
    first_params = tuple((item[0] for item in params))
    second_params = tuple((item[1] for item in params))

    def sectioned(entry, first_set, second_set, offset):
        sent = low(low_back(residual_block(entry, first_set, segment, position))) + offset
        return (sent, residual_block(sent, second_set, segment, position))
    offset = jnp.zeros_like(start)
    (sent, final), pullback = jax.vjp(sectioned, start, first_params, second_params, offset)
    incoming = cotangent.astype(jnp.float32).reshape(MICRO, N_DP, GROUP, D)
    grad_start, grad_first, grad_second, grad_sent = pullback((jnp.zeros_like(sent), incoming))
    block_out = jnp.stack([sent, final]).reshape(2, MICRO, N_DP * GROUP, D).astype(jnp.bfloat16)
    input_grads = jnp.stack([grad_start, grad_sent]).reshape(2, MICRO, N_DP * GROUP, D).astype(jnp.bfloat16)
    grads = [jnp.stack([left, right]).astype(jnp.float32) for left, right in zip(grad_first, grad_second)]
    return (block_out, input_grads, grads[0], grads[1], grads[2], grads[3], grads[4], grads[5], grads[6], grads[7], grads[8])
```

```python
from functools import partial
import math

import jax
import jax.numpy as jnp
from jax import lax
from jax.experimental import pallas as pl
from jax.experimental.pallas import tpu as pltpu
from jax.sharding import Mesh, PartitionSpec as P

HEADS = 8
EPS = 1e-05
F32 = jnp.float32
BF16 = jnp.bfloat16
XZ = ("xl", "z")
LOG2E = math.log2(math.e)
SPAN = 128
HEAD = 64
TILE = 256
SCALE = 1.0 / math.sqrt(HEAD)


def dot(a, b, dims):
    return lax.dot_general(a, b, (dims, ((), ())), preferred_element_type=F32)


NN = ((1,), (0,))
NT = ((1,), (1,))
TN = ((0,), (0,))


def lanes_of(ref, block, at, micro):
    lanes = slice(micro * SPAN, (micro + 1) * SPAN)
    return jnp.concatenate(
        [ref[2 * block, at : at + HEAD, lanes], ref[2 * block + 1, at : at + HEAD, lanes]], axis=1
    )


def key_offsets():
    row = lax.broadcasted_iota(jnp.int32, (TILE, TILE), 0)
    return row + jnp.where(row >= SPAN, SPAN, 0)


def allowed_in(offsets, low, high, chunk, core, tile):
    side = core if chunk % 2 == 0 else 1 - core
    base = (chunk // 2) * (2 * TILE) + side * SPAN
    seen = offsets >= low - base
    if chunk // 2 == tile:
        seen = seen & (offsets <= high - base)
    return seen


def attend_kernel(core_ref, mine_ref, other_ref, low_ref, high_ref, out_ref, lse_ref, keys, scores):
    core = core_ref[0]
    offsets = key_offsets()
    for micro in range(2):
        for chunk in range(8):
            ref, at = (mine_ref, HEAD) if chunk % 2 == 0 else (other_ref, 0)
            keys[chunk * TILE : (chunk + 1) * TILE, :] = lanes_of(ref, chunk // 2, at, micro).T
        for tile in range(4):
            row = micro * 4 + tile
            low, high = low_ref[row : row + 1, :], high_ref[row : row + 1, :]
            query = lanes_of(mine_ref, tile, 0, micro)
            top = jnp.full((1, TILE), -1e30, F32)
            for chunk in range(2 * tile + 2):
                rows = slice(chunk * TILE, (chunk + 1) * TILE)
                raw = dot(keys[rows, :], query, NN) * (SCALE * LOG2E)
                raw = jnp.where(allowed_in(offsets, low, high, chunk, core, tile), raw, -1e30)
                scores[rows, :] = raw
                top = jnp.maximum(top, jnp.max(raw, axis=0, keepdims=True))
            total = jnp.zeros((1, TILE), F32)
            heard = jnp.zeros((HEAD, TILE), F32)
            for chunk in range(2 * tile + 2):
                rows = slice(chunk * TILE, (chunk + 1) * TILE)
                weight = jnp.exp2(scores[rows, :] - top)
                total = total + jnp.sum(weight, axis=0, keepdims=True)
                ref, at = (mine_ref, 2 * HEAD) if chunk % 2 == 0 else (other_ref, HEAD)
                value = lanes_of(ref, chunk // 2, at, micro)
                heard = heard + dot(value, weight.astype(BF16), NN)
            heard = (heard / total).astype(BF16)
            lanes = slice(micro * SPAN, (micro + 1) * SPAN)
            out_ref[2 * tile, :, lanes] = heard[:, :SPAN]
            out_ref[2 * tile + 1, :, lanes] = heard[:, SPAN:]
            lse_ref[row : row + 1, :] = top + jnp.log2(total)


def attend_back_kernel(
    core_ref,
    mine_ref,
    other_ref,
    low_ref,
    high_ref,
    out_ref,
    lse_ref,
    grad_ref,
    gmine_ref,
    gother_ref,
    keys,
    values,
    gkeys,
    gvalues,
):
    core = core_ref[0]
    offsets = key_offsets()
    for micro in range(2):
        lanes = slice(micro * SPAN, (micro + 1) * SPAN)
        for chunk in range(8):
            rows = slice(chunk * TILE, (chunk + 1) * TILE)
            ref, at = (mine_ref, HEAD) if chunk % 2 == 0 else (other_ref, 0)
            keys[rows, :] = lanes_of(ref, chunk // 2, at, micro).T
            values[rows, :] = lanes_of(ref, chunk // 2, at + HEAD, micro).T
        gkeys[...] = jnp.zeros_like(gkeys)
        gvalues[...] = jnp.zeros_like(gvalues)
        for tile in range(4):
            row = micro * 4 + tile
            low, high = low_ref[row : row + 1, :], high_ref[row : row + 1, :]
            lse = lse_ref[row : row + 1, :]
            query = lanes_of(mine_ref, tile, 0, micro)
            grad = lanes_of(grad_ref, tile, 0, micro)
            heard = lanes_of(out_ref, tile, 0, micro)
            centre = jnp.sum(grad.astype(F32) * heard.astype(F32), axis=0, keepdims=True)
            gquery = jnp.zeros((HEAD, TILE), F32)
            for chunk in range(2 * tile + 2):
                rows = slice(chunk * TILE, (chunk + 1) * TILE)
                raw = dot(keys[rows, :], query, NN) * (SCALE * LOG2E)
                seen = allowed_in(offsets, low, high, chunk, core, tile)
                prob = jnp.exp2(jnp.where(seen, raw - lse, -1e30))
                gprob = dot(values[rows, :], grad, NN)
                gscore = (prob * (gprob - centre)).astype(BF16)
                ref, at = (mine_ref, HEAD) if chunk % 2 == 0 else (other_ref, 0)
                gquery = gquery + dot(lanes_of(ref, chunk // 2, at, micro), gscore, NN)
                gkeys[:, rows] += dot(query, gscore, NT)
                gvalues[:, rows] += dot(grad, prob.astype(BF16), NT)
            gquery = (gquery * SCALE).astype(BF16)
            gmine_ref[2 * tile, :HEAD, lanes] = gquery[:, :SPAN]
            gmine_ref[2 * tile + 1, :HEAD, lanes] = gquery[:, SPAN:]
        for chunk in range(8):
            ref, at = (gmine_ref, HEAD) if chunk % 2 == 0 else (gother_ref, 0)
            for half in range(2):
                cols = slice(chunk * TILE + half * SPAN, chunk * TILE + (half + 1) * SPAN)
                block = 2 * (chunk // 2) + half
                ref[block, at : at + HEAD, lanes] = (gkeys[:, cols] * SCALE).astype(BF16)
                ref[block, at + HEAD : at + 2 * HEAD, lanes] = gvalues[:, cols].astype(BF16)


VMEM = pl.BlockSpec(memory_space=pltpu.VMEM)
SMEM = pl.BlockSpec(memory_space=pltpu.SMEM)
LIMIT = 40 * 1024 * 1024


def attend(core, mine, other, low, high):
    return pl.pallas_call(
        attend_kernel,
        out_shape=(
            jax.ShapeDtypeStruct((8, HEAD, 2 * SPAN), BF16),
            jax.ShapeDtypeStruct((8, TILE), F32),
        ),
        in_specs=[SMEM, VMEM, VMEM, VMEM, VMEM],
        out_specs=(VMEM, VMEM),
        scratch_shapes=[pltpu.VMEM((2048, HEAD), BF16), pltpu.VMEM((2048, TILE), F32)],
        compiler_params=pltpu.CompilerParams(vmem_limit_bytes=LIMIT),
        cost_estimate=pl.CostEstimate(
            flops=700_000_000, bytes_accessed=2_000_000, transcendentals=2_600_000
        ),
        name="attend",
    )(core, mine, other, low, high)


def attend_back(core, mine, other, low, high, out, lse, grad):
    return pl.pallas_call(
        attend_back_kernel,
        out_shape=(
            jax.ShapeDtypeStruct((8, 3 * HEAD, 2 * SPAN), BF16),
            jax.ShapeDtypeStruct((8, 2 * HEAD, 2 * SPAN), BF16),
        ),
        in_specs=[SMEM] + [VMEM] * 7,
        out_specs=(VMEM, VMEM),
        scratch_shapes=[
            pltpu.VMEM((2048, HEAD), BF16),
            pltpu.VMEM((2048, HEAD), BF16),
            pltpu.VMEM((HEAD, 2048), F32),
            pltpu.VMEM((HEAD, 2048), F32),
        ],
        compiler_params=pltpu.CompilerParams(vmem_limit_bytes=LIMIT),
        cost_estimate=pl.CostEstimate(
            flops=1_700_000_000, bytes_accessed=3_000_000, transcendentals=2_600_000
        ),
        name="attend_back",
    )(core, mine, other, low, high, out, lse, grad)


def swap(array, axis):
    return lax.ppermute(array, axis, [(0, 1), (1, 0)])


def normed_of(hidden):
    centred = hidden - jnp.mean(hidden, -1, keepdims=True)
    inv = lax.rsqrt(jnp.mean(centred * centred, -1, keepdims=True) + EPS)
    return centred * inv, inv


def turned(tiles, cosine, sine):
    first, second = tiles[:, :8], tiles[:, 8:16]
    return jnp.concatenate(
        [first * cosine - second * sine, second * cosine + first * sine, tiles[:, 16:]], 1
    )


def per_device(
    inputs,
    lengths,
    norm_gain,
    norm_bias,
    qkv_weight,
    qkv_bias,
    proj_weight,
    up_weight,
    up_bias,
    down_weight,
    branch_bias,
    cotangent,
):
    section = lax.axis_index("section")
    core = lax.axis_index("core")
    block = lax.axis_index(XZ)
    micros, span, width = inputs.shape
    rows = micros * span
    gains = norm_gain[0].astype(F32)
    shifts = norm_bias[0].astype(F32)
    w_qkv, w_proj, w_up, w_down = qkv_weight[0], proj_weight[0], up_weight[0], down_weight[0]
    b_qkv = qkv_bias[0].astype(F32)
    b_up = up_bias[0].astype(F32)
    b_branch = jnp.sum(branch_bias[0].astype(F32), 0)
    core_word = core.astype(jnp.int32).reshape(1)

    ends = jnp.cumsum(lengths[0], -1)

    def begin_of(row):
        after = row[None, :, None] >= ends[:, None, :]
        return jnp.sum(jnp.where(after, lengths[0][:, None, :], 0), -1)

    heard_rows = (
        (2 * jnp.arange(8, dtype=jnp.int32)[:, None] + core) * span
        + jnp.arange(span, dtype=jnp.int32)[None]
    ).reshape(-1)
    low = begin_of(heard_rows).reshape(8, TILE)
    high = jnp.broadcast_to(heard_rows[None], (micros, 8 * span)).reshape(8, TILE)
    own_rows = (2 * block + core) * span + jnp.arange(span, dtype=jnp.int32)
    position = (own_rows[None] - begin_of(own_rows)).reshape(1, rows).astype(F32)
    ladder = jnp.arange(8, dtype=F32) * (2.0 / 16)
    angle = jnp.exp(-math.log(10000.0) * ladder)[:, None] * position
    cosine, sine = jnp.cos(angle), jnp.sin(angle)

    def front(hidden):
        xhat, _ = normed_of(hidden)
        first = (xhat * gains[0] + shifts[0]).astype(BF16)
        second = (xhat * gains[1] + shifts[1]).astype(BF16)
        qkv = (dot(first, w_qkv, NN) + b_qkv).T.reshape(3, HEADS, HEAD, rows)
        tiles = jnp.concatenate(
            [turned(qkv[0], cosine, sine), turned(qkv[1], cosine, sine), qkv[2]], 1
        ).astype(BF16)
        mine = lax.all_to_all(tiles, XZ, 0, 0, tiled=True)
        other = swap(mine[:, HEAD:], "core")
        return first, second, mine, other

    def mlp_of(second):
        up = dot(second, w_up, NN) + b_up
        phi = 0.5 * (1.0 + lax.erf(up * (1.0 / math.sqrt(2.0))))
        bell = jnp.exp(-0.5 * up * up) * (1.0 / math.sqrt(2.0 * math.pi))
        active = (up * phi).astype(BF16)
        slope = (phi + up * bell).astype(BF16)
        return active, slope

    def forward(hidden):
        first, second, mine, other = front(hidden)
        active, slope = mlp_of(second)
        base = hidden + dot(active, w_down, NN) + b_branch
        heard, lse = attend(core_word, mine, other, low, high)
        heard_rows = lax.all_to_all(heard, XZ, 0, 0, tiled=True).reshape(width, rows)
        result = (base + dot(heard_rows, w_proj, TN)).astype(BF16)
        kept = (first, second, mine, other, active, slope, heard, lse, heard_rows)
        return result, kept

    def norm_back(grad, gain, xhat, inv):
        e = grad * gain
        return inv * (
            e - jnp.mean(e, -1, keepdims=True) - xhat * jnp.mean(e * xhat, -1, keepdims=True)
        )

    def backward(grad_in, hidden, kept, want_terms):
        first, second, mine, other, active, slope, heard, lse, heard_rows = kept
        grad = grad_in.astype(F32)
        ggo = dot(w_proj, grad_in, NT).astype(BF16).reshape(HEADS, HEAD, rows)
        ggo = lax.all_to_all(ggo, XZ, 0, 0, tiled=True)
        gup = (dot(grad_in, w_down, NT) * slope.astype(F32)).astype(BF16)
        gsecond = dot(gup, w_up, NT)
        gmine, gother = attend_back(core_word, mine, other, low, high, heard, lse, ggo)
        gother = swap(gother, "core")
        gmine = jnp.concatenate(
            [gmine[:, :HEAD], (gmine[:, HEAD:].astype(F32) + gother.astype(F32)).astype(BF16)], 1
        )
        back = lax.all_to_all(gmine, XZ, 0, 0, tiled=True).astype(F32)
        back = jnp.stack(
            [
                turned(back[:, :HEAD], cosine, -sine),
                turned(back[:, HEAD : 2 * HEAD], cosine, -sine),
                back[:, 2 * HEAD :],
            ]
        )
        gqkv = back.astype(BF16).reshape(3 * width, rows)
        gfirst = dot(gqkv, w_qkv, ((0,), (1,)))
        xhat, inv = normed_of(hidden)
        ghidden = (
            grad
            + norm_back(gfirst, gains[0], xhat, inv)
            + norm_back(gsecond, gains[1], xhat, inv)
        ).astype(BF16)
        if not want_terms:
            return ghidden, None
        total = lambda v: jnp.sum(v, 0)
        terms = dict(
            qkv=dot(first, gqkv, ((0,), (1,))),
            proj=dot(heard_rows, grad_in, NN),
            up=dot(second, gup, TN),
            down=dot(active, grad_in, TN),
            small=jnp.concatenate(
                [
                    total(gfirst * xhat),
                    total(gsecond * xhat),
                    total(gfirst),
                    total(gsecond),
                    jnp.sum(gqkv.astype(F32), 1),
                    total(gup.astype(F32)),
                    total(grad),
                ]
            ),
        )
        return ghidden, terms

    entry = inputs.reshape(rows, width)
    loss_grad = cotangent.reshape(rows, width)
    sent, _ = forward(entry.astype(F32))
    received = lax.ppermute(sent, "section", [(0, 1)])
    entry = jnp.where(section == 1, received, entry)
    hidden = entry.astype(F32)
    result, kept = forward(hidden)
    sent_back, _ = backward(loss_grad, hidden, kept, False)
    received = lax.ppermute(sent_back, "section", [(1, 0)])
    grad_in = jnp.where(section == 1, loss_grad, received)
    ghidden, terms = backward(grad_in, hidden, kept, True)

    blocks = [terms["qkv"][:, i * width : (i + 1) * width] for i in range(3)]
    blocks += [terms["proj"]]
    blocks += [terms["up"][:, i * width : (i + 1) * width] for i in range(4)]
    blocks += [terms["down"]]
    line = jnp.concatenate([b.astype(BF16) for b in blocks], 0).reshape(2, -1, width)
    small = jnp.pad(terms["small"].astype(BF16).reshape(-1, width), ((0, 4), (0, 0)))
    half = line.shape[1]
    theirs = lax.dynamic_index_in_dim(line, 1 - core, 0, keepdims=False)
    ours = lax.dynamic_index_in_dim(line, core, 0, keepdims=False)
    got = swap(jnp.concatenate([theirs, small]), "core")
    summed = (jnp.concatenate([ours, small]).astype(F32) + got.astype(F32)).astype(BF16)
    shares = 4 * 8
    share = half // shares
    parts = jnp.concatenate(
        [
            summed[:half].reshape(shares, share, width),
            jnp.broadcast_to(summed[half:][None], (shares, 16, width)),
        ],
        1,
    )
    parts = lax.all_to_all(parts, XZ + ("dp",), 0, 0, tiled=True)
    part = jnp.sum(parts.astype(F32), 0)
    small = part[share:].reshape(-1)
    part = lax.all_gather(part[:share].astype(BF16), "dp", tiled=True)
    part = lax.all_gather(part, XZ, tiled=True)
    partner = swap(part, "core")
    whole = jnp.where(core == 0, jnp.stack([part, partner]), jnp.stack([partner, part]))
    whole = whole.reshape(-1, width).astype(F32)

    def beside(at, count):
        return jnp.concatenate(
            [whole[at + i * width : at + (i + 1) * width] for i in range(count)], 1
        )

    return (
        result.reshape(1, micros, span, width),
        ghidden.reshape(1, micros, span, width),
        small[:1024].reshape(1, 2, width),
        small[1024:2048].reshape(1, 2, width),
        beside(0, 3)[None],
        small[2048:3584][None],
        whole[3 * width : 4 * width][None],
        beside(4 * width, 4)[None],
        small[3584:5632][None],
        whole[8 * width :][None],
        jnp.broadcast_to(small[5632:6144].reshape(1, 1, width), (1, 2, width)),
    )


def solution(mesh):
    axes = ("section", "dp", "xl", "z", "core")
    fine = Mesh(mesh.devices.reshape(2, 4, 2, 4, 2), axes)
    spread = P(None, ("dp", "xl", "z", "core"), None)
    three, two = P("section", None, None), P("section", None)
    kept = P("section", None, ("dp", "xl", "z", "core"), None)
    in_specs = (
        spread, P("dp", None, None), three, three, three, two, three, three, two, three, three, spread,
    )
    out_specs = (kept, kept, three, three, three, two, three, three, two, three, three)
    return jax.shard_map(
        per_device, mesh=fine, in_specs=in_specs, out_specs=out_specs, check_vma=False
    )
```

```python
from functools import partial
import math

import jax
import jax.numpy as jnp
from jax import lax
from jax.experimental import pallas as pl
from jax.experimental.pallas import tpu as pltpu
from jax.sharding import Mesh, PartitionSpec as P

HEADS = 8
EPS = 1e-05
F32 = jnp.float32
BF16 = jnp.bfloat16
XZ = ("xl", "z")
LOG2E = math.log2(math.e)
SPAN = 128
HEAD = 64
TILE = 256
SCALE = 1.0 / math.sqrt(HEAD)


def dot(a, b, dims):
    return lax.dot_general(a, b, (dims, ((), ())), preferred_element_type=F32)


NN = ((1,), (0,))
NT = ((1,), (1,))
TN = ((0,), (0,))


def lanes_of(ref, block, at, micro):
    lanes = slice(micro * SPAN, (micro + 1) * SPAN)
    return jnp.concatenate(
        [ref[2 * block, at : at + HEAD, lanes], ref[2 * block + 1, at : at + HEAD, lanes]], axis=1
    )


def key_offsets():
    row = lax.broadcasted_iota(jnp.int32, (TILE, TILE), 0)
    return row + jnp.where(row >= SPAN, SPAN, 0)


def allowed_in(offsets, low, high, chunk, core, tile):
    side = core if chunk % 2 == 0 else 1 - core
    base = (chunk // 2) * (2 * TILE) + side * SPAN
    seen = offsets >= low - base
    if chunk // 2 == tile:
        seen = seen & (offsets <= high - base)
    return seen


def attend_kernel(core_ref, mine_ref, other_ref, low_ref, high_ref, out_ref, lse_ref, keys, scores):
    core = core_ref[0]
    offsets = key_offsets()
    for micro in range(2):
        for chunk in range(8):
            ref, at = (mine_ref, HEAD) if chunk % 2 == 0 else (other_ref, 0)
            keys[chunk * TILE : (chunk + 1) * TILE, :] = lanes_of(ref, chunk // 2, at, micro).T
        for tile in range(4):
            row = micro * 4 + tile
            low, high = low_ref[row : row + 1, :], high_ref[row : row + 1, :]
            query = lanes_of(mine_ref, tile, 0, micro)
            top = jnp.full((1, TILE), -1e30, F32)
            for chunk in range(2 * tile + 2):
                rows = slice(chunk * TILE, (chunk + 1) * TILE)
                raw = dot(keys[rows, :], query, NN) * (SCALE * LOG2E)
                raw = jnp.where(allowed_in(offsets, low, high, chunk, core, tile), raw, -1e30)
                scores[rows, :] = raw
                top = jnp.maximum(top, jnp.max(raw, axis=0, keepdims=True))
            total = jnp.zeros((1, TILE), F32)
            heard = jnp.zeros((HEAD, TILE), F32)
            for chunk in range(2 * tile + 2):
                rows = slice(chunk * TILE, (chunk + 1) * TILE)
                weight = jnp.exp2(scores[rows, :] - top)
                total = total + jnp.sum(weight, axis=0, keepdims=True)
                ref, at = (mine_ref, 2 * HEAD) if chunk % 2 == 0 else (other_ref, HEAD)
                value = lanes_of(ref, chunk // 2, at, micro)
                heard = heard + dot(value, weight.astype(BF16), NN)
            heard = (heard / total).astype(BF16)
            lanes = slice(micro * SPAN, (micro + 1) * SPAN)
            out_ref[2 * tile, :, lanes] = heard[:, :SPAN]
            out_ref[2 * tile + 1, :, lanes] = heard[:, SPAN:]
            lse_ref[row : row + 1, :] = top + jnp.log2(total)


def attend_back_kernel(
    core_ref,
    mine_ref,
    other_ref,
    low_ref,
    high_ref,
    out_ref,
    lse_ref,
    grad_ref,
    gmine_ref,
    gother_ref,
    keys,
    values,
    gkeys,
    gvalues,
):
    core = core_ref[0]
    offsets = key_offsets()
    for micro in range(2):
        lanes = slice(micro * SPAN, (micro + 1) * SPAN)
        for chunk in range(8):
            rows = slice(chunk * TILE, (chunk + 1) * TILE)
            ref, at = (mine_ref, HEAD) if chunk % 2 == 0 else (other_ref, 0)
            keys[rows, :] = lanes_of(ref, chunk // 2, at, micro).T
            values[rows, :] = lanes_of(ref, chunk // 2, at + HEAD, micro).T
        gkeys[...] = jnp.zeros_like(gkeys)
        gvalues[...] = jnp.zeros_like(gvalues)
        for tile in range(4):
            row = micro * 4 + tile
            low, high = low_ref[row : row + 1, :], high_ref[row : row + 1, :]
            lse = lse_ref[row : row + 1, :]
            query = lanes_of(mine_ref, tile, 0, micro)
            grad = lanes_of(grad_ref, tile, 0, micro)
            heard = lanes_of(out_ref, tile, 0, micro)
            centre = jnp.sum(grad.astype(F32) * heard.astype(F32), axis=0, keepdims=True)
            gquery = jnp.zeros((HEAD, TILE), F32)
            for chunk in range(2 * tile + 2):
                rows = slice(chunk * TILE, (chunk + 1) * TILE)
                raw = dot(keys[rows, :], query, NN) * (SCALE * LOG2E)
                seen = allowed_in(offsets, low, high, chunk, core, tile)
                prob = jnp.exp2(jnp.where(seen, raw - lse, -1e30))
                gprob = dot(values[rows, :], grad, NN)
                gscore = (prob * (gprob - centre)).astype(BF16)
                ref, at = (mine_ref, HEAD) if chunk % 2 == 0 else (other_ref, 0)
                gquery = gquery + dot(lanes_of(ref, chunk // 2, at, micro), gscore, NN)
                gkeys[:, rows] += dot(query, gscore, NT)
                gvalues[:, rows] += dot(grad, prob.astype(BF16), NT)
            gquery = (gquery * SCALE).astype(BF16)
            gmine_ref[2 * tile, :HEAD, lanes] = gquery[:, :SPAN]
            gmine_ref[2 * tile + 1, :HEAD, lanes] = gquery[:, SPAN:]
        for chunk in range(8):
            ref, at = (gmine_ref, HEAD) if chunk % 2 == 0 else (gother_ref, 0)
            for half in range(2):
                cols = slice(chunk * TILE + half * SPAN, chunk * TILE + (half + 1) * SPAN)
                block = 2 * (chunk // 2) + half
                ref[block, at : at + HEAD, lanes] = (gkeys[:, cols] * SCALE).astype(BF16)
                ref[block, at + HEAD : at + 2 * HEAD, lanes] = gvalues[:, cols].astype(BF16)


def front_kernel(
    hidden_ref, gain_ref, shift_ref, weight_ref, bias_ref, cos_ref, sin_ref, tiles_ref, first_ref, second_ref
):
    xhat, _ = normed_of(hidden_ref[...].astype(F32))
    first = (xhat * gain_ref[0:1, :] + shift_ref[0:1, :]).astype(BF16)
    first_ref[...] = first
    second_ref[...] = (xhat * gain_ref[1:2, :] + shift_ref[1:2, :]).astype(BF16)
    width = first.shape[1]
    cosine, sine = cos_ref[...], sin_ref[...]
    for part in range(3):
        cols = slice(part * width, (part + 1) * width)
        made = (dot(first, weight_ref[:, cols], NN) + bias_ref[:, cols]).T
        for head in range(HEADS):
            tile = made[head * HEAD : (head + 1) * HEAD]
            if part < 2:
                tile = turned(tile, cosine, sine)
            tiles_ref[head, part * HEAD : (part + 1) * HEAD, :] = tile.astype(BF16)


def back_kernel(
    back_ref,
    hidden_ref,
    grad_ref,
    gsecond_ref,
    gain_ref,
    weight_ref,
    cos_ref,
    sin_ref,
    ghidden_ref,
    gqkv_ref,
    sums_ref,
    bias_ref,
):
    width = hidden_ref.shape[1]
    rows = hidden_ref.shape[0]
    cosine, sine = cos_ref[...], -sin_ref[...]
    gfirst = jnp.zeros((rows, width), F32)
    ones = jnp.ones((8, rows), BF16)
    for part in range(3):
        cols = slice(part * width, (part + 1) * width)
        for head in range(HEADS):
            tile = back_ref[head, part * HEAD : (part + 1) * HEAD, :]
            if part < 2:
                tile = turned(tile.astype(F32), cosine, sine).astype(BF16)
            at = part * width + head * HEAD
            gqkv_ref[at : at + HEAD, :] = tile
        made = gqkv_ref[cols, :]
        gfirst = gfirst + dot(made.T, weight_ref[:, cols], NT)
        bias_ref[:, cols] = dot(ones, made, NT)
    xhat, inv = normed_of(hidden_ref[...].astype(F32))
    gsecond = gsecond_ref[...]
    total = grad_ref[...].astype(F32)
    for which, grad in ((0, gfirst), (1, gsecond)):
        e = grad * gain_ref[which : which + 1, :]
        total = total + inv * (
            e - jnp.mean(e, -1, keepdims=True) - xhat * jnp.mean(e * xhat, -1, keepdims=True)
        )
        sums_ref[which : which + 1, :] = jnp.sum(grad * xhat, 0, keepdims=True)
        sums_ref[which + 2 : which + 3, :] = jnp.sum(grad, 0, keepdims=True)
    sums_ref[4:8, :] = jnp.zeros((4, width), F32)
    ghidden_ref[...] = total.astype(BF16)


def mlp_terms_kernel(core_ref, second_ref, gup_ref, active_ref, grad_ref, ours_ref, theirs_ref):
    core = core_ref[0]
    width = second_ref.shape[1]
    turned_second = second_ref[...].T
    for block in range(4):
        cols = slice(block * width, (block + 1) * width)
        up = dot(turned_second, gup_ref[:, cols], NN).astype(BF16)
        down = dot(active_ref[:, cols].T, grad_ref[...], NN).astype(BF16)
        ours_ref[block] = jnp.where(core == 0, up, down)
        theirs_ref[block] = jnp.where(core == 0, down, up)


def mix_terms_kernel(core_ref, first_ref, gqkv_ref, heard_ref, grad_ref, ours_ref, theirs_ref):
    core = core_ref[0]
    width = first_ref.shape[1]
    turned_first = first_ref[...].T
    made = [
        dot(turned_first, gqkv_ref[block * width : (block + 1) * width, :], NT).astype(BF16)
        for block in range(3)
    ]
    made.append(dot(heard_ref[...], grad_ref[...], NN).astype(BF16))
    for block in range(2):
        low, high = made[block], made[block + 2]
        ours_ref[block] = jnp.where(core == 0, low, high)
        theirs_ref[block] = jnp.where(core == 0, high, low)


def split_kernel(count, pieces, at_ref, *refs):
    sources, targets = refs[:count], refs[count:]
    extent = targets[0].shape[0]
    at = at_ref[0]
    for step in range(pieces):
        start = pl.multiple_of(lax.rem(at + step, pieces) * extent, extent)
        total = sources[0][pl.ds(start, extent), :].astype(F32)
        for source in sources[1:]:
            total = total + source[pl.ds(start, extent), :].astype(F32)
        targets[step][...] = total.astype(BF16)


def place_kernel(at_ref, *refs):
    sources, target = refs[:-1], refs[-1]
    count, extent, at = len(sources), sources[0].shape[0], at_ref[0]
    for step, source in enumerate(sources):
        start = pl.multiple_of(lax.rem(at + count - step, count) * extent, extent)
        target[pl.ds(start, extent), :] = source[...]


def mlp_out_kernel(core_ref, mine_ref, other_ref, up_ref, down_ref):
    core = core_ref[0]
    mine, other = mine_ref[...].astype(F32), other_ref[...].astype(F32)
    up_ref[...] = jnp.where(core == 0, mine, other)
    down_ref[...] = jnp.where(core == 0, other, mine)


def mix_out_kernel(core_ref, mine_ref, other_ref, qkv_ref, proj_ref):
    core = core_ref[0]
    width = proj_ref.shape[0]
    mine, other = mine_ref[...].astype(F32), other_ref[...].astype(F32)
    low, high = jnp.where(core == 0, mine, other), jnp.where(core == 0, other, mine)
    qkv_ref[:, :width] = low[:width]
    qkv_ref[:, width : 2 * width] = low[width:]
    qkv_ref[:, 2 * width :] = high[:width]
    proj_ref[...] = high[width:]


VMEM = pl.BlockSpec(memory_space=pltpu.VMEM)
SMEM = pl.BlockSpec(memory_space=pltpu.SMEM)
MIB = 1024 * 1024


def shaped(shape, dtype):
    return jax.ShapeDtypeStruct(shape, dtype)


def call(kernel, outs, *args, words=0, flops=0, moved=1_000_000, exps=0, limit=40, scratch=(), name=None):
    single = not isinstance(outs, tuple)
    shapes = (outs,) if single else outs
    made = pl.pallas_call(
        kernel,
        out_shape=shapes,
        in_specs=[SMEM] * words + [VMEM] * (len(args) - words),
        out_specs=tuple(VMEM for _ in shapes),
        scratch_shapes=list(scratch),
        compiler_params=pltpu.CompilerParams(vmem_limit_bytes=limit * MIB),
        cost_estimate=pl.CostEstimate(flops=flops, bytes_accessed=moved, transcendentals=exps),
        name=name,
    )(*args)
    return made[0] if single else made


def attend(core, mine, other, low, high):
    return call(
        attend_kernel,
        (shaped((8, HEAD, 2 * SPAN), BF16), shaped((8, TILE), F32)),
        core, mine, other, low, high,
        words=1, flops=2_800_000_000, moved=2_000_000, exps=2_600_000,
        scratch=[pltpu.VMEM((2048, HEAD), BF16), pltpu.VMEM((2048, TILE), F32)],
        name="attend",
    )


def attend_back(core, mine, other, low, high, out, lse, grad):
    return call(
        attend_back_kernel,
        (shaped((8, 3 * HEAD, 2 * SPAN), BF16), shaped((8, 2 * HEAD, 2 * SPAN), BF16)),
        core, mine, other, low, high, out, lse, grad,
        words=1, flops=7_000_000_000, moved=3_000_000, exps=2_600_000,
        scratch=[
            pltpu.VMEM((2048, HEAD), BF16),
            pltpu.VMEM((2048, HEAD), BF16),
            pltpu.VMEM((HEAD, 2048), F32),
            pltpu.VMEM((HEAD, 2048), F32),
        ],
        name="attend_back",
    )


def swap(array, axis):
    return lax.ppermute(array, axis, [(0, 1), (1, 0)])


def word(value):
    return value.astype(jnp.int32).reshape(1)


def spread_from(pieces, axis):
    count = len(pieces)
    return [pieces[0]] + [
        lax.ppermute(pieces[s], axis, [(i, (i + s) % count) for i in range(count)])
        for s in range(1, count)
    ]


def split(arrays, axis, pieces):
    extent = arrays[0].shape[0] // pieces
    shapes = tuple(shaped((extent, arrays[0].shape[1]), BF16) for _ in range(pieces))
    return call(
        partial(split_kernel, len(arrays), pieces), shapes, word(lax.axis_index(axis)), *arrays,
        words=1, moved=2 * arrays[0].size * (len(arrays) + 1), limit=16, name="split",
    )


def summed_over(arrays, axes):
    for axis in axes:
        arrays = spread_from(split(arrays, axis, lax.axis_size(axis)), axis)
    total = arrays[0].astype(F32)
    for array in arrays[1:]:
        total = total + array.astype(F32)
    return total.astype(BF16)


def gathered_over(array, axes):
    for axis in axes:
        count = lax.axis_size(axis)
        pieces = spread_from([array] * count, axis)
        array = call(
            place_kernel, shaped((count * array.shape[0], array.shape[1]), BF16),
            word(lax.axis_index(axis)), *pieces,
            words=1, moved=4 * count * array.size, limit=16, name="place",
        )
    return array


def normed_of(hidden):
    centred = hidden - jnp.mean(hidden, -1, keepdims=True)
    inv = lax.rsqrt(jnp.mean(centred * centred, -1, keepdims=True) + EPS)
    return centred * inv, inv


def turned(tile, cosine, sine):
    first, second = tile[:8], tile[8:16]
    return jnp.concatenate(
        [first * cosine - second * sine, second * cosine + first * sine, tile[16:]], 0
    )


def per_device(
    inputs,
    lengths,
    norm_gain,
    norm_bias,
    qkv_weight,
    qkv_bias,
    proj_weight,
    up_weight,
    up_bias,
    down_weight,
    branch_bias,
    cotangent,
):
    section = lax.axis_index("section")
    core = lax.axis_index("core")
    block = lax.axis_index(XZ)
    micros, span, width = inputs.shape
    rows = micros * span
    gains = norm_gain[0].astype(F32)
    shifts = norm_bias[0].astype(F32)
    w_qkv, w_proj, w_up, w_down = qkv_weight[0], proj_weight[0], up_weight[0], down_weight[0]
    b_qkv = qkv_bias.astype(F32)
    b_up = up_bias[0].astype(F32)
    b_branch = jnp.sum(branch_bias[0].astype(F32), 0)
    core_word = word(core)

    ends = jnp.cumsum(lengths[0], -1)

    def begin_of(row):
        after = row[None, :, None] >= ends[:, None, :]
        return jnp.sum(jnp.where(after, lengths[0][:, None, :], 0), -1)

    heard_rows = (
        (2 * jnp.arange(8, dtype=jnp.int32)[:, None] + core) * span
        + jnp.arange(span, dtype=jnp.int32)[None]
    ).reshape(-1)
    low = begin_of(heard_rows).reshape(8, TILE)
    high = jnp.broadcast_to(heard_rows[None], (micros, 8 * span)).reshape(8, TILE)
    own_rows = (2 * block + core) * span + jnp.arange(span, dtype=jnp.int32)
    position = (own_rows[None] - begin_of(own_rows)).reshape(1, rows).astype(F32)
    ladder = jnp.arange(8, dtype=F32) * (2.0 / 16)
    angle = jnp.exp(-math.log(10000.0) * ladder)[:, None] * position
    cosine, sine = jnp.cos(angle), jnp.sin(angle)

    def front(hidden):
        tiles, first, second = call(
            front_kernel,
            (
                shaped((HEADS, 3 * HEAD, rows), BF16),
                shaped((rows, width), BF16),
                shaped((rows, width), BF16),
            ),
            hidden, gains, shifts, w_qkv, b_qkv, cosine, sine,
            flops=400_000_000, moved=4_000_000, limit=24, name="front",
        )
        mine = lax.all_to_all(tiles, XZ, 0, 0, tiled=True)
        other = swap(mine[:, HEAD:], "core")
        return first, second, mine, other

    def mlp_of(second):
        up = dot(second, w_up, NN) + b_up
        phi = 0.5 * (1.0 + lax.erf(up * (1.0 / math.sqrt(2.0))))
        bell = jnp.exp(-0.5 * up * up) * (1.0 / math.sqrt(2.0 * math.pi))
        active = (up * phi).astype(BF16)
        slope = (phi + up * bell).astype(BF16)
        return active, slope

    def forward(hidden):
        first, second, mine, other = front(hidden)
        active, slope = mlp_of(second)
        base = hidden.astype(F32) + dot(active, w_down, NN) + b_branch
        heard, lse = attend(core_word, mine, other, low, high)
        heard_rows = lax.all_to_all(heard, XZ, 0, 0, tiled=True).reshape(width, rows)
        result = (base + dot(heard_rows, w_proj, TN)).astype(BF16)
        kept = (first, second, mine, other, active, slope, heard, lse, heard_rows)
        return result, kept

    def backward(grad_in, hidden, kept, want_terms):
        first, second, mine, other, active, slope, heard, lse, heard_rows = kept
        ggo = dot(w_proj, grad_in, NT).astype(BF16).reshape(HEADS, HEAD, rows)
        ggo = lax.all_to_all(ggo, XZ, 0, 0, tiled=True)
        gup = (dot(grad_in, w_down, NT) * slope.astype(F32)).astype(BF16)
        gsecond = dot(gup, w_up, NT)
        mlp = None
        if want_terms:
            mlp = call(
                mlp_terms_kernel,
                (shaped((4, width, width), BF16), shaped((4, width, width), BF16)),
                core_word, second, gup, active, grad_in,
                words=1, flops=1_100_000_000, moved=6_000_000, limit=32, name="mlp_terms",
            )
            mlp = [v.reshape(4 * width, width) for v in mlp]
            mlp = summed_over([mlp[0], swap(mlp[1], "core")], ("dp", "z", "xl"))
            mlp = gathered_over(mlp, ("xl", "z", "dp"))
        gmine, gother = attend_back(core_word, mine, other, low, high, heard, lse, ggo)
        gother = swap(gother, "core")
        gmine = jnp.concatenate(
            [gmine[:, :HEAD], (gmine[:, HEAD:].astype(F32) + gother.astype(F32)).astype(BF16)], 1
        )
        back = lax.all_to_all(gmine, XZ, 0, 0, tiled=True)
        ghidden, gqkv, sums, bias_sums = call(
            back_kernel,
            (
                shaped((rows, width), BF16),
                shaped((3 * width, rows), BF16),
                shaped((8, width), F32),
                shaped((8, 3 * width), F32),
            ),
            back, hidden, grad_in, gsecond, gains, w_qkv, cosine, sine,
            flops=500_000_000, moved=4_000_000, limit=24, name="back",
        )
        if not want_terms:
            return ghidden, None
        mix = call(
            mix_terms_kernel,
            (shaped((2, width, width), BF16), shaped((2, width, width), BF16)),
            core_word, first, gqkv, heard_rows, grad_in,
            words=1, flops=600_000_000, moved=3_000_000, limit=24, name="mix_terms",
        )
        small = jnp.concatenate(
            [
                sums[:4].reshape(-1),
                bias_sums[0],
                jnp.sum(gup.astype(F32), 0),
                jnp.sum(grad_in.astype(F32), 0),
            ]
        ).astype(BF16)
        small = jnp.pad(small.reshape(-1, width), ((0, 4), (0, 0)))
        return ghidden, (mlp, [v.reshape(2 * width, width) for v in mix], small)

    entry = inputs.reshape(rows, width)
    loss_grad = cotangent.reshape(rows, width)
    sent, _ = forward(entry)
    received = lax.ppermute(sent, "section", [(0, 1)])
    entry = jnp.where(section == 1, received, entry)
    result, kept = forward(entry)
    sent_back, _ = backward(loss_grad, entry, kept, False)
    received = lax.ppermute(sent_back, "section", [(1, 0)])
    grad_in = jnp.where(section == 1, loss_grad, received)
    ghidden, (mlp, mix, small) = backward(grad_in, entry, kept, True)

    got = swap(jnp.concatenate([mix[1], small]), "core")
    summed = (jnp.concatenate([mix[0], small]).astype(F32) + got.astype(F32)).astype(BF16)
    shares, half = 32, 2 * width
    parts = jnp.concatenate(
        [
            summed[:half].reshape(shares, half // shares, width),
            jnp.broadcast_to(summed[half:][None], (shares, 16, width)),
        ],
        1,
    )
    parts = lax.all_to_all(parts, ("z", "dp", "xl"), 0, 0, tiled=True)
    part = jnp.sum(parts.astype(F32), 0)
    small = part[half // shares :].reshape(-1)
    mix = gathered_over(part[: half // shares].astype(BF16), ("xl", "dp", "z"))
    qkv, proj = call(
        mix_out_kernel,
        (shaped((width, 3 * width), F32), shaped((width, width), F32)),
        core_word, mix, swap(mix, "core"),
        words=1, moved=6_000_000, limit=32, name="mix_out",
    )
    block_spec = pl.BlockSpec((width, width), lambda i: (i, 0))
    up, down = pl.pallas_call(
        mlp_out_kernel,
        grid=(4,),
        out_shape=(shaped((width, 4 * width), F32), shaped((4 * width, width), F32)),
        in_specs=[SMEM, block_spec, block_spec],
        out_specs=(pl.BlockSpec((width, width), lambda i: (0, i)), block_spec),
        compiler_params=pltpu.CompilerParams(vmem_limit_bytes=24 * MIB),
        cost_estimate=pl.CostEstimate(flops=0, bytes_accessed=12_000_000, transcendentals=0),
        name="mlp_out",
    )(core_word, mlp, swap(mlp, "core"))

    return (
        result.reshape(1, micros, span, width),
        ghidden.reshape(1, micros, span, width),
        small[:1024].reshape(1, 2, width),
        small[1024:2048].reshape(1, 2, width),
        qkv[None],
        small[2048:3584][None],
        proj[None],
        up[None],
        small[3584:5632][None],
        down[None],
        jnp.broadcast_to(small[5632:6144].reshape(1, 1, width), (1, 2, width)),
    )


def solution(mesh):
    axes = ("section", "dp", "xl", "z", "core")
    fine = Mesh(mesh.devices.reshape(2, 4, 2, 4, 2), axes)
    spread = P(None, ("dp", "xl", "z", "core"), None)
    three, two = P("section", None, None), P("section", None)
    kept = P("section", None, ("dp", "xl", "z", "core"), None)
    in_specs = (
        spread, P("dp", None, None), three, three, three, two, three, three, two, three, three, spread,
    )
    out_specs = (kept, kept, three, three, three, two, three, three, two, three, three)
    return jax.shard_map(
        per_device, mesh=fine, in_specs=in_specs, out_specs=out_specs, check_vma=False
    )
```

```python
from functools import partial
import math

import jax
import jax.numpy as jnp
from jax import lax
from jax.experimental import pallas as pl
from jax.experimental.pallas import tpu as pltpu
from jax.sharding import Mesh, PartitionSpec as P

HEADS = 8
EPS = 1e-05
F32 = jnp.float32
BF16 = jnp.bfloat16
XZ = ("xl", "z")
LOG2E = math.log2(math.e)
SPAN = 128
HEAD = 64
TILE = 256
SCALE = 1.0 / math.sqrt(HEAD)
LAST = 32


def dot(a, b, dims):
    return lax.dot_general(a, b, (dims, ((), ())), preferred_element_type=F32)


NN = ((1,), (0,))
NT = ((1,), (1,))
TN = ((0,), (0,))


def lanes_of(ref, block, at, lanes):
    return jnp.concatenate(
        [ref[2 * block, at : at + HEAD, lanes], ref[2 * block + 1, at : at + HEAD, lanes]], axis=1
    )


def lanes_at(micro):
    return pl.ds(pl.multiple_of(micro * SPAN, SPAN), SPAN)


def key_offsets():
    row = lax.broadcasted_iota(jnp.int32, (TILE, TILE), 0)
    return row + jnp.where(row >= SPAN, SPAN, 0)


def allowed_in(offsets, low, high, chunk, core, tile):
    side = core if chunk % 2 == 0 else 1 - core
    base = (chunk // 2) * (2 * TILE) + side * SPAN
    seen = offsets >= low - base
    if chunk // 2 == tile:
        seen = seen & (offsets <= high - base)
    return seen


def attend_kernel(core_ref, mine_ref, other_ref, low_ref, high_ref, out_ref, lse_ref, keys, scores):
    core = core_ref[0]
    offsets = key_offsets()

    def one_micro(micro, carry):
        lanes = lanes_at(micro)
        for chunk in range(8):
            ref, at = (mine_ref if chunk % 2 == 0 else other_ref), HEAD
            keys[chunk * TILE : (chunk + 1) * TILE, :] = lanes_of(ref, chunk // 2, at, lanes).T
        for tile in range(4):
            row = pl.ds(micro * 4 + tile, 1)
            low, high = low_ref[row, :], high_ref[row, :]
            query = lanes_of(mine_ref, tile, 0, lanes)
            top = jnp.full((1, TILE), -1e30, F32)
            for chunk in range(2 * tile + 2):
                rows = slice(chunk * TILE, (chunk + 1) * TILE)
                raw = dot(keys[rows, :], query, NN) * (SCALE * LOG2E)
                raw = jnp.where(allowed_in(offsets, low, high, chunk, core, tile), raw, -1e30)
                scores[rows, :] = raw
                top = jnp.maximum(top, jnp.max(raw, axis=0, keepdims=True))
            total = jnp.zeros((1, TILE), F32)
            heard = jnp.zeros((HEAD, TILE), F32)
            for chunk in range(2 * tile + 2):
                rows = slice(chunk * TILE, (chunk + 1) * TILE)
                weight = jnp.exp2(scores[rows, :] - top)
                total = total + jnp.sum(weight, axis=0, keepdims=True)
                ref, at = (mine_ref if chunk % 2 == 0 else other_ref), 2 * HEAD
                value = lanes_of(ref, chunk // 2, at, lanes)
                heard = heard + dot(value, weight.astype(BF16), NN)
            heard = (heard / total).astype(BF16)
            out_ref[2 * tile, :, lanes] = heard[:, :SPAN]
            out_ref[2 * tile + 1, :, lanes] = heard[:, SPAN:]
            lse_ref[row, :] = top + jnp.log2(total)
        return carry

    lax.fori_loop(0, 2, one_micro, 0)


def attend_back_kernel(
    core_ref,
    mine_ref,
    other_ref,
    low_ref,
    high_ref,
    out_ref,
    lse_ref,
    grad_ref,
    gmine_ref,
    gother_ref,
    keys,
    values,
    gkeys,
    gvalues,
):
    core = core_ref[0]
    offsets = key_offsets()

    def one_micro(micro, carry):
        lanes = lanes_at(micro)
        for chunk in range(8):
            rows = slice(chunk * TILE, (chunk + 1) * TILE)
            ref, at = (mine_ref if chunk % 2 == 0 else other_ref), HEAD
            keys[rows, :] = lanes_of(ref, chunk // 2, at, lanes).T
            values[rows, :] = lanes_of(ref, chunk // 2, at + HEAD, lanes).T
        gkeys[...] = jnp.zeros_like(gkeys)
        gvalues[...] = jnp.zeros_like(gvalues)
        for tile in range(4):
            row = pl.ds(micro * 4 + tile, 1)
            low, high, lse = low_ref[row, :], high_ref[row, :], lse_ref[row, :]
            query = lanes_of(mine_ref, tile, 0, lanes)
            grad = lanes_of(grad_ref, tile, 0, lanes)
            heard = lanes_of(out_ref, tile, 0, lanes)
            centre = jnp.sum(grad.astype(F32) * heard.astype(F32), axis=0, keepdims=True)
            gquery = jnp.zeros((HEAD, TILE), F32)
            for chunk in range(2 * tile + 2):
                rows = slice(chunk * TILE, (chunk + 1) * TILE)
                raw = dot(keys[rows, :], query, NN) * (SCALE * LOG2E)
                seen = allowed_in(offsets, low, high, chunk, core, tile)
                prob = jnp.exp2(jnp.where(seen, raw - lse, -1e30))
                gprob = dot(values[rows, :], grad, NN)
                gscore = (prob * (gprob - centre)).astype(BF16)
                ref, at = (mine_ref if chunk % 2 == 0 else other_ref), HEAD
                gquery = gquery + dot(lanes_of(ref, chunk // 2, at, lanes), gscore, NN)
                gkeys[:, rows] += dot(query, gscore, NT)
                gvalues[:, rows] += dot(grad, prob.astype(BF16), NT)
            gquery = (gquery * SCALE).astype(BF16)
            gmine_ref[2 * tile, :HEAD, lanes] = gquery[:, :SPAN]
            gmine_ref[2 * tile + 1, :HEAD, lanes] = gquery[:, SPAN:]
        for chunk in range(8):
            ref, at = (gmine_ref, HEAD) if chunk % 2 == 0 else (gother_ref, 0)
            for half in range(2):
                cols = slice(chunk * TILE + half * SPAN, chunk * TILE + (half + 1) * SPAN)
                block = 2 * (chunk // 2) + half
                ref[block, at : at + HEAD, lanes] = (gkeys[:, cols] * SCALE).astype(BF16)
                ref[block, at + HEAD : at + 2 * HEAD, lanes] = gvalues[:, cols].astype(BF16)
        return carry

    lax.fori_loop(0, 2, one_micro, 0)


def front_kernel(
    hidden_ref, gain_ref, shift_ref, weight_ref, bias_ref, cos_ref, sin_ref, tiles_ref, first_ref, second_ref
):
    xhat, _ = normed_of(hidden_ref[...].astype(F32))
    first = (xhat * gain_ref[0:1, :] + shift_ref[0:1, :]).astype(BF16)
    first_ref[...] = first
    second_ref[...] = (xhat * gain_ref[1:2, :] + shift_ref[1:2, :]).astype(BF16)
    width = first.shape[1]
    cosine, sine = cos_ref[...], sin_ref[...]
    for part in range(3):
        cols = slice(part * width, (part + 1) * width)
        made = (dot(first, weight_ref[:, cols], NN) + bias_ref[:, cols]).T
        for head in range(HEADS):
            tile = made[head * HEAD : (head + 1) * HEAD]
            if part < 2:
                tile = turned(tile, cosine, sine)
            tiles_ref[head, part * HEAD : (part + 1) * HEAD, :] = tile.astype(BF16)


def back_kernel(
    back_ref, hidden_ref, grad_ref, gsecond_ref, gain_ref, weight_ref, ghidden_ref, sums_ref, bias_ref, gqkv
):
    width = hidden_ref.shape[1]
    rows = hidden_ref.shape[0]
    gfirst = jnp.zeros((rows, width), F32)
    ones = jnp.ones((8, rows), BF16)
    for part in range(3):
        cols = slice(part * width, (part + 1) * width)
        for head in range(HEADS):
            gqkv[head * HEAD : (head + 1) * HEAD, :] = back_ref[head, part * HEAD : (part + 1) * HEAD, :]
        made = gqkv[...]
        gfirst = gfirst + dot(made.T, weight_ref[:, cols], NT)
        bias_ref[:, cols] = dot(ones, made, NT)
    xhat, inv = normed_of(hidden_ref[...].astype(F32))
    gsecond = gsecond_ref[...]
    total = grad_ref[...].astype(F32)
    for which, grad in ((0, gfirst), (1, gsecond)):
        e = grad * gain_ref[which : which + 1, :]
        total = total + inv * (
            e - jnp.mean(e, -1, keepdims=True) - xhat * jnp.mean(e * xhat, -1, keepdims=True)
        )
        sums_ref[which : which + 1, :] = jnp.sum(grad * xhat, 0, keepdims=True)
        sums_ref[which + 2 : which + 3, :] = jnp.sum(grad, 0, keepdims=True)
    sums_ref[4:8, :] = jnp.zeros((4, width), F32)
    ghidden_ref[...] = total.astype(BF16)


def join_kernel(mine_ref, other_ref, cos_ref, sin_ref, out_ref):
    for block in range(8):
        cosine, sine = cos_ref[block], -sin_ref[block]
        for part in range(3):
            rows = slice(part * HEAD, (part + 1) * HEAD)
            tile = mine_ref[block, rows, :].astype(F32)
            if part > 0:
                at = (part - 1) * HEAD
                tile = tile + other_ref[block, at : at + HEAD, :].astype(F32)
            if part < 2:
                tile = turned(tile, cosine, sine)
            out_ref[block, rows, :] = tile.astype(BF16)


def grad_kernel(section_ref, received_ref, own_ref, weight_ref, grad_ref, heard_ref):
    grad = jnp.where(section_ref[0] == 1, own_ref[...], received_ref[...])
    grad_ref[...] = grad
    made = dot(weight_ref[...], grad, NT).astype(BF16)
    for head in range(HEADS):
        heard_ref[head] = made[head * HEAD : (head + 1) * HEAD]


def early_terms_kernel(
    core_ref,
    second_ref,
    slope_ref,
    active_ref,
    grad_ref,
    heard_ref,
    down_ref,
    gup_ref,
    ours_ref,
    theirs_ref,
):
    core = core_ref[0]
    width = second_ref.shape[1]
    turned_second = second_ref[...].T
    grad = grad_ref[...]
    proj = dot(heard_ref[...], grad, NN).astype(BF16)
    for block in range(4):
        cols = slice(block * width, (block + 1) * width)
        gup = (dot(grad, down_ref[cols, :], NT) * slope_ref[:, cols].astype(F32)).astype(BF16)
        gup_ref[:, cols] = gup
        up = dot(turned_second, gup, NN).astype(BF16)
        down = dot(active_ref[:, cols].T, grad, NN).astype(BF16)
        first = proj[block * 64 : (block + 1) * 64]
        last = proj[256 + block * 64 : 256 + (block + 1) * 64]
        ours_ref[block, :width, :] = jnp.where(core == 0, up, down)
        theirs_ref[block, :width, :] = jnp.where(core == 0, down, up)
        ours_ref[block, width:, :] = jnp.where(core == 0, first, last)
        theirs_ref[block, width:, :] = jnp.where(core == 0, last, first)


def second_grad_kernel(gup_ref, up_ref, gsecond_ref):
    gsecond_ref[...] = dot(gup_ref[...], up_ref[...], NT)


def late_terms_kernel(core_ref, gqkv_ref, first_ref, ours_ref, theirs_ref):
    core = core_ref[0]
    total = jnp.zeros((3 * HEAD, first_ref.shape[2]), F32)
    for block in range(8):
        total = total + dot(gqkv_ref[block], first_ref[block], NN)
    total = jnp.concatenate([total, jnp.zeros((HEAD, total.shape[1]), F32)], 0).T
    half = total.shape[0] // 2
    upper, lower = total[:half].astype(BF16), total[half:].astype(BF16)
    ours_ref[...] = jnp.where(core == 0, upper, lower)
    theirs_ref[...] = jnp.where(core == 0, lower, upper)


def split_kernel(count, pieces, at_ref, *refs):
    sources, targets = refs[:count], refs[count:]
    extent = targets[0].shape[0]
    at = at_ref[0]
    for step in range(pieces):
        start = pl.multiple_of(lax.rem(at + step, pieces) * extent, extent)
        total = sources[0][pl.ds(start, extent), :].astype(F32)
        for source in sources[1:]:
            total = total + source[pl.ds(start, extent), :].astype(F32)
        targets[step][...] = total.astype(BF16)


def place_kernel(at_ref, *refs):
    sources, target = refs[:-1], refs[-1]
    count, extent, at = len(sources), sources[0].shape[0], at_ref[0]
    for step, source in enumerate(sources):
        start = pl.multiple_of(lax.rem(at + count - step, count) * extent, extent)
        target[pl.ds(start, extent), :] = source[...]


def columns_kernel(at_ref, *refs):
    sources, (ours_ref, theirs_ref) = refs[:-2], refs[-2:]
    total = sources[0][...].astype(F32)
    for source in sources[1:]:
        total = total + source[...].astype(F32)
    half = total.shape[1] // 2
    left, right = total[:, :half].astype(BF16), total[:, half:].astype(BF16)
    ours_ref[...] = jnp.where(at_ref[0] == 0, left, right)
    theirs_ref[...] = jnp.where(at_ref[0] == 0, right, left)


def out_kernel(core_ref, a_ref, b_ref, other_a_ref, other_b_ref, up_ref, down_ref, qkv_ref, proj_ref):
    core = core_ref[0]
    width = down_ref.shape[1]

    def parts(first_ref, second_ref):
        early, late = [], []
        for z in range(4):
            first = jnp.concatenate([first_ref[0, z, 0], first_ref[0, z, 1]], 1)
            second = jnp.concatenate([second_ref[z, 0, 0, :LAST], second_ref[z, 0, 1, :LAST]], 1)
            early += [first, second]
        for half in range(2):
            late += [second_ref[z, 0, half, LAST:] for z in range(4)]
        return jnp.concatenate(early, 0).astype(F32), [v.astype(F32) for v in late]

    mine, late = parts(a_ref, b_ref)
    other, other_late = parts(other_a_ref, other_b_ref)
    low, high = jnp.where(core == 0, mine, other), jnp.where(core == 0, other, mine)
    up_ref[...] = low[:width]
    down_ref[...] = high[:width]
    proj_ref[0] = low[width:]
    proj_ref[1] = high[width:]
    for head in range(HEADS):
        low = jnp.where(core == 0, late[head], other_late[head])
        high = jnp.where(core == 0, other_late[head], late[head])
        for part in range(3):
            at = part * width + head * HEAD
            qkv_ref[0, :, at : at + HEAD] = low[:, part * HEAD : (part + 1) * HEAD]
            qkv_ref[1, :, at : at + HEAD] = high[:, part * HEAD : (part + 1) * HEAD]


def halves_kernel(at_ref, mine_ref, other_ref, a_ref, b_ref):
    at = at_ref[0]
    first, last = a_ref.shape[0] // 2, b_ref.shape[0] // 2
    for source, to in ((mine_ref, at), (other_ref, 1 - at)):
        a_ref[pl.ds(pl.multiple_of(to * first, 16), first), :] = source[:first, :]
        b_ref[pl.ds(pl.multiple_of(to * last, 16), last), :] = source[first:, :]


VMEM = pl.BlockSpec(memory_space=pltpu.VMEM)
SMEM = pl.BlockSpec(memory_space=pltpu.SMEM)
MIB = 1024 * 1024


def shaped(shape, dtype):
    return jax.ShapeDtypeStruct(shape, dtype)


def call(kernel, outs, *args, words=0, limit=12, scratch=(), name=None):
    single = not isinstance(outs, tuple)
    shapes = (outs,) if single else outs
    made = pl.pallas_call(
        kernel,
        out_shape=shapes,
        in_specs=[SMEM] * words + [VMEM] * (len(args) - words),
        out_specs=tuple(VMEM for _ in shapes),
        scratch_shapes=list(scratch),
        compiler_params=pltpu.CompilerParams(vmem_limit_bytes=limit * MIB),
        cost_estimate=pl.CostEstimate(flops=0, bytes_accessed=1024, transcendentals=0),
        name=name,
    )(*args)
    return made[0] if single else made


def attend(core, mine, other, low, high):
    return call(
        attend_kernel,
        (shaped((8, HEAD, 2 * SPAN), BF16), shaped((8, TILE), F32)),
        core, mine, other, low, high,
        words=1, limit=10,
        scratch=[pltpu.VMEM((2048, HEAD), BF16), pltpu.VMEM((2048, TILE), F32)],
        name="attend",
    )


def attend_back(core, mine, other, low, high, out, lse, grad):
    return call(
        attend_back_kernel,
        (shaped((8, 3 * HEAD, 2 * SPAN), BF16), shaped((8, 2 * HEAD, 2 * SPAN), BF16)),
        core, mine, other, low, high, out, lse, grad,
        words=1, limit=10,
        scratch=[
            pltpu.VMEM((2048, HEAD), BF16),
            pltpu.VMEM((2048, HEAD), BF16),
            pltpu.VMEM((HEAD, 2048), F32),
            pltpu.VMEM((HEAD, 2048), F32),
        ],
        name="attend_back",
    )


def swap(array, axis):
    return lax.ppermute(array, axis, [(0, 1), (1, 0)])


def word(value):
    return value.astype(jnp.int32).reshape(1)


def spread_from(pieces, axis):
    count = len(pieces)
    return [pieces[0]] + [
        lax.ppermute(pieces[s], axis, [(i, (i + s) % count) for i in range(count)])
        for s in range(1, count)
    ]


def split(arrays, axis, pieces):
    extent = arrays[0].shape[0] // pieces
    shapes = tuple(shaped((extent, arrays[0].shape[1]), BF16) for _ in range(pieces))
    return call(
        partial(split_kernel, len(arrays), pieces), shapes, word(lax.axis_index(axis)), *arrays,
        words=1, limit=10, name="split",
    )


def placed(pieces, axis):
    extent, width = pieces[0].shape
    return call(
        place_kernel, shaped((len(pieces) * extent, width), BF16),
        word(lax.axis_index(axis)), *pieces,
        words=1, limit=8, name="place",
    )


def normed_of(hidden):
    centred = hidden - jnp.mean(hidden, -1, keepdims=True)
    inv = lax.rsqrt(jnp.mean(centred * centred, -1, keepdims=True) + EPS)
    return centred * inv, inv


def turned(tile, cosine, sine):
    first, second = tile[:8], tile[8:16]
    return jnp.concatenate(
        [first * cosine - second * sine, second * cosine + first * sine, tile[16:]], 0
    )


def per_device(
    inputs,
    lengths,
    norm_gain,
    norm_bias,
    qkv_weight,
    qkv_bias,
    proj_weight,
    up_weight,
    up_bias,
    down_weight,
    branch_bias,
    cotangent,
):
    section = lax.axis_index("section")
    core = lax.axis_index("core")
    block = lax.axis_index(XZ)
    micros, span, width = inputs.shape
    rows = micros * span
    gains = norm_gain[0].astype(F32)
    shifts = norm_bias[0].astype(F32)
    w_qkv, w_proj, w_up, w_down = qkv_weight[0], proj_weight[0], up_weight[0], down_weight[0]
    b_qkv = qkv_bias.astype(F32)
    b_up = up_bias[0].astype(F32)
    b_branch = jnp.sum(branch_bias[0].astype(F32), 0)
    core_word = word(core)

    ends = jnp.cumsum(lengths[0], -1)

    def begin_of(row):
        after = row[None, :, None] >= ends[:, None, :]
        return jnp.sum(jnp.where(after, lengths[0][:, None, :], 0), -1)

    heard_rows = (
        (2 * jnp.arange(8, dtype=jnp.int32)[:, None] + core) * span
        + jnp.arange(span, dtype=jnp.int32)[None]
    ).reshape(-1)
    low = begin_of(heard_rows).reshape(8, TILE)
    high = jnp.broadcast_to(heard_rows[None], (micros, 8 * span)).reshape(8, TILE)
    own_rows = (2 * block + core) * span + jnp.arange(span, dtype=jnp.int32)
    position = (own_rows[None] - begin_of(own_rows)).reshape(1, rows).astype(F32)
    ladder = jnp.exp(-math.log(10000.0) * (jnp.arange(8, dtype=F32) * (2.0 / 16)))
    angle = ladder[:, None] * position
    cosine, sine = jnp.cos(angle), jnp.sin(angle)
    heard_position = (heard_rows[None] - begin_of(heard_rows)).reshape(micros, 8, span)
    heard_position = jnp.moveaxis(heard_position, 0, 1).reshape(8, 1, rows).astype(F32)
    heard_angle = ladder[None, :, None] * heard_position
    heard_cosine, heard_sine = jnp.cos(heard_angle), jnp.sin(heard_angle)

    def front(hidden):
        tiles, first, second = call(
            front_kernel,
            (
                shaped((HEADS, 3 * HEAD, rows), BF16),
                shaped((rows, width), BF16),
                shaped((rows, width), BF16),
            ),
            hidden, gains, shifts, w_qkv, b_qkv, cosine, sine,
            limit=12, name="front",
        )
        mine = lax.all_to_all(tiles, XZ, 0, 0, tiled=True)
        other = swap(mine, "core")
        return first, second, mine, other

    def mlp_of(second):
        up = dot(second, w_up, NN) + b_up
        phi = 0.5 * (1.0 + lax.erf(up * (1.0 / math.sqrt(2.0))))
        bell = jnp.exp(-0.5 * up * up) * (1.0 / math.sqrt(2.0 * math.pi))
        active = (up * phi).astype(BF16)
        slope = (phi + up * bell).astype(BF16)
        return active, slope

    def forward(hidden):
        first, second, mine, other = front(hidden)
        active, slope = mlp_of(second)
        base = hidden.astype(F32) + dot(active, w_down, NN) + b_branch
        heard, lse = attend(core_word, mine, other, low, high)
        return base, first, second, mine, other, active, slope, heard, lse

    def finish(base, heard):
        heard_rows = lax.all_to_all(heard, XZ, 0, 0, tiled=True).reshape(width, rows)
        return (base + dot(heard_rows, w_proj, TN)).astype(BF16), heard_rows

    def heard_grad(received, own):
        grad_in, ggo = call(
            grad_kernel,
            (shaped((rows, width), BF16), shaped((HEADS, HEAD, rows), BF16)),
            word(section), received, own, w_proj,
            words=1, name="grad",
        )
        return grad_in, lax.all_to_all(ggo, XZ, 0, 0, tiled=True)

    def joined(gmine, gother):
        return call(
            join_kernel, shaped(gmine.shape, BF16),
            gmine, swap(gother, "core"), heard_cosine, heard_sine, name="join",
        )

    def rows_back(back, hidden, grad_in, gsecond):
        return call(
            back_kernel,
            (shaped((rows, width), BF16), shaped((8, width), F32), shaped((8, 3 * width), F32)),
            back, hidden, grad_in, gsecond, gains, w_qkv,
            scratch=[pltpu.VMEM((width, rows), BF16)], name="back",
        )

    def mlp_back(grad_in, slope):
        gup = (dot(grad_in, w_down, NT) * slope.astype(F32)).astype(BF16)
        return gup, dot(gup, w_up, NT)

    entry = inputs.reshape(rows, width)
    loss_grad = cotangent.reshape(rows, width)
    base, *_, heard, _ = forward(entry)
    sent, _ = finish(base, heard)
    received = lax.ppermute(sent, "section", [(0, 1)])
    entry = jnp.where(section == 1, received, entry)
    base, first, second, mine, other, active, slope, heard, lse = forward(entry)
    mine, first = lax.optimization_barrier((mine, first))
    first_all = lax.all_gather(first, XZ)
    grad_in, ggo = heard_grad(loss_grad, loss_grad)
    _, gsecond = mlp_back(grad_in, slope)
    gmine, gother = attend_back(core_word, mine, other, low, high, heard, lse, ggo)
    result, heard_rows = finish(base, heard)
    gother, heard_rows = lax.optimization_barrier((gother, heard_rows))
    back = lax.all_to_all(joined(gmine, gother), XZ, 0, 0, tiled=True)
    sent_back, _, _ = rows_back(back, entry, grad_in, gsecond)
    received = lax.ppermute(sent_back, "section", [(1, 0)])
    received, result, heard_rows = lax.optimization_barrier((received, result, heard_rows))
    grad_in, ggo = heard_grad(received, loss_grad)
    gup, *early = call(
        early_terms_kernel,
        (shaped((rows, 4 * width), BF16),) + (shaped((4, width + 64, width), BF16),) * 2,
        core_word, second, slope, active, grad_in, heard_rows, w_down,
        words=1, limit=24, name="early_terms",
    )
    ggo, early = lax.optimization_barrier((ggo, early))
    early = [v.reshape(-1, width) for v in early]
    pieces = split([early[0], swap(early[1], "core")], "dp", 4)
    ggo, pieces = lax.optimization_barrier((ggo, pieces))
    pieces = spread_from(pieces, "dp")
    gmine, gother = attend_back(core_word, mine, other, low, high, heard, lse, ggo)
    gmine = joined(gmine, gother)
    gmine, pieces[1], pieces[3] = lax.optimization_barrier((gmine, pieces[1], pieces[3]))
    late = call(
        late_terms_kernel,
        (shaped((width // 2, width // 2), BF16),) * 2,
        core_word, gmine, first_all,
        words=1, name="late_terms",
    )
    gsecond = call(second_grad_kernel, shaped((rows, width), F32), gup, w_up, name="second_grad")
    back = lax.all_to_all(gmine, XZ, 0, 0, tiled=True)
    pieces = spread_from(split(pieces, "z", 4), "z")
    back, pieces, late = lax.optimization_barrier((back, pieces, late))
    late = spread_from(split([late[0], swap(late[1], "core")], "dp", 4), "dp")
    ghidden, sums, bias_sums = rows_back(back, entry, grad_in, gsecond)
    ours, theirs = call(
        columns_kernel,
        (shaped((pieces[0].shape[0], width // 2), BF16),) * 2,
        word(lax.axis_index("xl")), *pieces,
        words=1, limit=8, name="columns",
    )
    early = ours.astype(F32) + swap(theirs, "xl").astype(F32)
    late = sum(v.astype(F32) for v in late)
    share = jnp.concatenate([early.astype(BF16), late.astype(BF16)])
    extent = share.shape[0]

    small = jnp.concatenate(
        [
            sums[:4].reshape(-1),
            bias_sums[0],
            jnp.sum(gup.astype(F32), 0),
            jnp.sum(grad_in.astype(F32), 0),
        ]
    ).astype(BF16)
    small = jnp.pad(small.reshape(2, -1), ((0, 0), (0, 1024))).reshape(2, 16, width // 2)
    of_core = lambda c: lax.dynamic_index_in_dim(small, c, 0, keepdims=False)
    small = of_core(core).astype(F32) + swap(of_core(1 - core), "core").astype(F32)
    share, small, ghidden = lax.optimization_barrier((share, small.astype(BF16), ghidden))
    small = jnp.broadcast_to(small[None], (32, 16, width // 2))
    small = lax.all_to_all(small, ("dp",) + XZ, 0, 0, tiled=True)
    a, b = call(
        halves_kernel,
        (shaped((2 * 112, width // 2), BF16), shaped((2 * (extent - 112), width // 2), BF16)),
        word(lax.axis_index("xl")), share, swap(share, "xl"),
        words=1, limit=8, name="halves",
    )
    a_pieces, b_pieces = spread_from([a] * 4, "z"), spread_from([b] * 4, "dp")
    a, b, small = lax.optimization_barrier((placed(a_pieces, "z"), placed(b_pieces, "dp"), small))
    a_pieces, b_pieces = spread_from([a] * 4, "dp"), spread_from([b] * 4, "z")
    a, b = placed(a_pieces, "dp"), placed(b_pieces, "z")
    small = jnp.sum(small.astype(F32), 0).reshape(-1)[:3072]
    partner = swap(small, "core")
    small = jnp.where(core == 0, jnp.stack([small, partner]), jnp.stack([partner, small]))
    small = small.reshape(-1)

    other_a, other_b = swap(a, "core"), swap(b, "core")
    a_spec = pl.BlockSpec((1, 4, 2, 112, width // 2), lambda i: (i, 0, 0, 0, 0))
    b_spec = pl.BlockSpec((4, 1, 2, 96, width // 2), lambda i: (0, i, 0, 0, 0))
    a, other_a = [v.reshape(4, 4, 2, 112, width // 2) for v in (a, other_a)]
    b, other_b = [v.reshape(4, 4, 2, 96, width // 2) for v in (b, other_b)]
    up, down, qkv, proj = pl.pallas_call(
        out_kernel,
        grid=(4,),
        out_shape=(
            shaped((width, 4 * width), F32),
            shaped((4 * width, width), F32),
            shaped((2, width // 2, 3 * width), F32),
            shaped((2, width // 2, width), F32),
        ),
        in_specs=[SMEM, a_spec, b_spec, a_spec, b_spec],
        out_specs=(
            pl.BlockSpec((width, width), lambda i: (0, i)),
            pl.BlockSpec((width, width), lambda i: (i, 0)),
            pl.BlockSpec((2, 64, 3 * width), lambda i: (0, i, 0)),
            pl.BlockSpec((2, 64, width), lambda i: (0, i, 0)),
        ),
        compiler_params=pltpu.CompilerParams(vmem_limit_bytes=32 * MIB),
        cost_estimate=pl.CostEstimate(flops=0, bytes_accessed=1024, transcendentals=0),
        name="out",
    )(core_word, a, b, other_a, other_b)
    qkv, proj = qkv.reshape(width, 3 * width), proj.reshape(width, width)

    return (
        result.reshape(1, micros, span, width),
        ghidden.reshape(1, micros, span, width),
        small[:1024].reshape(1, 2, width),
        small[1024:2048].reshape(1, 2, width),
        qkv[None],
        small[2048:3584][None],
        proj[None],
        up[None],
        small[3584:5632][None],
        down[None],
        jnp.broadcast_to(small[5632:6144].reshape(1, 1, width), (1, 2, width)),
    )


def solution(mesh):
    axes = ("section", "dp", "xl", "z", "core")
    fine = Mesh(mesh.devices.reshape(2, 4, 2, 4, 2), axes)
    spread = P(None, ("dp", "xl", "z", "core"), None)
    three, two = P("section", None, None), P("section", None)
    kept = P("section", None, ("dp", "xl", "z", "core"), None)
    in_specs = (
        spread, P("dp", None, None), three, three, three, two, three, three, two, three, three, spread,
    )
    out_specs = (kept, kept, three, three, three, two, three, three, two, three, three)
    return jax.shard_map(
        per_device, mesh=fine, in_specs=in_specs, out_specs=out_specs, check_vma=False
    )
```

```python
from functools import partial
import math

import jax
import jax.numpy as jnp
from jax import lax
from jax.experimental import pallas as pl
from jax.experimental.pallas import tpu as pltpu
from jax.sharding import Mesh, PartitionSpec as P

HEADS = 8
EPS = 1e-05
F32 = jnp.float32
BF16 = jnp.bfloat16
XZ = ("xl", "z")
LOG2E = math.log2(math.e)
SPAN = 128
HEAD = 64
TILE = 256
SCALE = 1.0 / math.sqrt(HEAD)
LAST = 32
HALF = 112


def dot(a, b, dims):
    return lax.dot_general(a, b, (dims, ((), ())), preferred_element_type=F32)


NN = ((1,), (0,))
NT = ((1,), (1,))
TN = ((0,), (0,))


def lanes_of(ref, block, at, lanes):
    return jnp.concatenate(
        [ref[2 * block, at : at + HEAD, lanes], ref[2 * block + 1, at : at + HEAD, lanes]], axis=1
    )


def lanes_at(micro):
    return pl.ds(pl.multiple_of(micro * SPAN, SPAN), SPAN)


def key_offsets():
    row = lax.broadcasted_iota(jnp.int32, (TILE, TILE), 0)
    return row + jnp.where(row >= SPAN, SPAN, 0)


def allowed_in(offsets, low, high, chunk, core, tile):
    side = core if chunk % 2 == 0 else 1 - core
    base = (chunk // 2) * (2 * TILE) + side * SPAN
    seen = offsets >= low - base
    if chunk // 2 == tile:
        seen = seen & (offsets <= high - base)
    return seen


def attend_kernel(core_ref, mine_ref, other_ref, low_ref, high_ref, out_ref, lse_ref, keys, scores):
    core = core_ref[0]
    offsets = key_offsets()

    def one_micro(micro, carry):
        lanes = lanes_at(micro)
        for chunk in range(8):
            ref, at = (mine_ref if chunk % 2 == 0 else other_ref), HEAD
            keys[chunk * TILE : (chunk + 1) * TILE, :] = lanes_of(ref, chunk // 2, at, lanes).T
        for tile in range(4):
            row = pl.ds(micro * 4 + tile, 1)
            low, high = low_ref[row, :], high_ref[row, :]
            query = lanes_of(mine_ref, tile, 0, lanes)
            top = jnp.full((1, TILE), -1e30, F32)
            for chunk in range(2 * tile + 2):
                rows = slice(chunk * TILE, (chunk + 1) * TILE)
                raw = dot(keys[rows, :], query, NN) * (SCALE * LOG2E)
                raw = jnp.where(allowed_in(offsets, low, high, chunk, core, tile), raw, -1e30)
                scores[rows, :] = raw
                top = jnp.maximum(top, jnp.max(raw, axis=0, keepdims=True))
            total = jnp.zeros((1, TILE), F32)
            heard = jnp.zeros((HEAD, TILE), F32)
            for chunk in range(2 * tile + 2):
                rows = slice(chunk * TILE, (chunk + 1) * TILE)
                weight = jnp.exp2(scores[rows, :] - top)
                total = total + jnp.sum(weight, axis=0, keepdims=True)
                ref, at = (mine_ref if chunk % 2 == 0 else other_ref), 2 * HEAD
                value = lanes_of(ref, chunk // 2, at, lanes)
                heard = heard + dot(value, weight.astype(BF16), NN)
            heard = (heard / total).astype(BF16)
            out_ref[2 * tile, :, lanes] = heard[:, :SPAN]
            out_ref[2 * tile + 1, :, lanes] = heard[:, SPAN:]
            lse_ref[row, :] = top + jnp.log2(total)
        return carry

    lax.fori_loop(0, 2, one_micro, 0)


def attend_back_kernel(
    core_ref,
    mine_ref,
    other_ref,
    low_ref,
    high_ref,
    out_ref,
    lse_ref,
    grad_ref,
    gmine_ref,
    gother_ref,
    keys,
    values,
    gkeys,
    gvalues,
):
    core = core_ref[0]
    offsets = key_offsets()

    def one_micro(micro, carry):
        lanes = lanes_at(micro)
        for chunk in range(8):
            rows = slice(chunk * TILE, (chunk + 1) * TILE)
            ref, at = (mine_ref if chunk % 2 == 0 else other_ref), HEAD
            keys[rows, :] = lanes_of(ref, chunk // 2, at, lanes).T
            values[rows, :] = lanes_of(ref, chunk // 2, at + HEAD, lanes).T
        gkeys[...] = jnp.zeros_like(gkeys)
        gvalues[...] = jnp.zeros_like(gvalues)
        for tile in range(4):
            row = pl.ds(micro * 4 + tile, 1)
            low, high, lse = low_ref[row, :], high_ref[row, :], lse_ref[row, :]
            query = lanes_of(mine_ref, tile, 0, lanes)
            grad = lanes_of(grad_ref, tile, 0, lanes)
            heard = lanes_of(out_ref, tile, 0, lanes)
            centre = jnp.sum(grad.astype(F32) * heard.astype(F32), axis=0, keepdims=True)
            gquery = jnp.zeros((HEAD, TILE), F32)
            for chunk in range(2 * tile + 2):
                rows = slice(chunk * TILE, (chunk + 1) * TILE)
                raw = dot(keys[rows, :], query, NN) * (SCALE * LOG2E)
                seen = allowed_in(offsets, low, high, chunk, core, tile)
                prob = jnp.exp2(jnp.where(seen, raw - lse, -1e30))
                gprob = dot(values[rows, :], grad, NN)
                gscore = (prob * (gprob - centre)).astype(BF16)
                ref, at = (mine_ref if chunk % 2 == 0 else other_ref), HEAD
                gquery = gquery + dot(lanes_of(ref, chunk // 2, at, lanes), gscore, NN)
                gkeys[:, rows] += dot(query, gscore, NT)
                gvalues[:, rows] += dot(grad, prob.astype(BF16), NT)
            gquery = (gquery * SCALE).astype(BF16)
            gmine_ref[2 * tile, :HEAD, lanes] = gquery[:, :SPAN]
            gmine_ref[2 * tile + 1, :HEAD, lanes] = gquery[:, SPAN:]
        for chunk in range(8):
            ref, at = (gmine_ref, HEAD) if chunk % 2 == 0 else (gother_ref, 0)
            for half in range(2):
                cols = slice(chunk * TILE + half * SPAN, chunk * TILE + (half + 1) * SPAN)
                block = 2 * (chunk // 2) + half
                ref[block, at : at + HEAD, lanes] = (gkeys[:, cols] * SCALE).astype(BF16)
                ref[block, at + HEAD : at + 2 * HEAD, lanes] = gvalues[:, cols].astype(BF16)
        return carry

    lax.fori_loop(0, 2, one_micro, 0)


def front_kernel(
    hidden_ref, gain_ref, shift_ref, weight_ref, bias_ref, cos_ref, sin_ref, tiles_ref, first_ref, second_ref
):
    xhat, _ = normed_of(hidden_ref[...].astype(F32))
    first = (xhat * gain_ref[0:1, :] + shift_ref[0:1, :]).astype(BF16)
    first_ref[...] = first
    second_ref[...] = (xhat * gain_ref[1:2, :] + shift_ref[1:2, :]).astype(BF16)
    width = first.shape[1]
    cosine, sine = cos_ref[...], sin_ref[...]
    for part in range(3):
        cols = slice(part * width, (part + 1) * width)
        made = (dot(first, weight_ref[:, cols], NN) + bias_ref[:, cols]).T
        for head in range(HEADS):
            tile = made[head * HEAD : (head + 1) * HEAD]
            if part < 2:
                tile = turned(tile, cosine, sine)
            tiles_ref[head, part * HEAD : (part + 1) * HEAD, :] = tile.astype(BF16)


def back_kernel(
    back_ref, hidden_ref, grad_ref, gsecond_ref, gain_ref, weight_ref, ghidden_ref, sums_ref, bias_ref, gqkv
):
    width = hidden_ref.shape[1]
    rows = hidden_ref.shape[0]
    gfirst = jnp.zeros((rows, width), F32)
    ones = jnp.ones((8, rows), BF16)
    for part in range(3):
        cols = slice(part * width, (part + 1) * width)
        for head in range(HEADS):
            gqkv[head * HEAD : (head + 1) * HEAD, :] = back_ref[head, part * HEAD : (part + 1) * HEAD, :]
        made = gqkv[...]
        gfirst = gfirst + dot(made.T, weight_ref[:, cols], NT)
        bias_ref[:, cols] = dot(ones, made, NT)
    xhat, inv = normed_of(hidden_ref[...].astype(F32))
    gsecond = gsecond_ref[...]
    total = grad_ref[...].astype(F32)
    for which, grad in ((0, gfirst), (1, gsecond)):
        e = grad * gain_ref[which : which + 1, :]
        total = total + inv * (
            e - jnp.mean(e, -1, keepdims=True) - xhat * jnp.mean(e * xhat, -1, keepdims=True)
        )
        sums_ref[which : which + 1, :] = jnp.sum(grad * xhat, 0, keepdims=True)
        sums_ref[which + 2 : which + 3, :] = jnp.sum(grad, 0, keepdims=True)
    sums_ref[4:8, :] = jnp.zeros((4, width), F32)
    ghidden_ref[...] = total.astype(BF16)


def join_kernel(mine_ref, other_ref, cos_ref, sin_ref, *refs):
    out_ref = refs[-1]
    for block in range(8):
        if len(refs) > 1:
            out_ref[block, 3 * HEAD :, :] = refs[0][block]
        cosine, sine = cos_ref[block], -sin_ref[block]
        for part in range(3):
            rows = slice(part * HEAD, (part + 1) * HEAD)
            tile = mine_ref[block, rows, :].astype(F32)
            if part > 0:
                at = (part - 1) * HEAD
                tile = tile + other_ref[block, at : at + HEAD, :].astype(F32)
            if part < 2:
                tile = turned(tile, cosine, sine)
            out_ref[block, rows, :] = tile.astype(BF16)


def grad_kernel(section_ref, received_ref, own_ref, weight_ref, grad_ref, heard_ref):
    grad = jnp.where(section_ref[0] == 1, own_ref[...], received_ref[...])
    grad_ref[...] = grad
    made = dot(weight_ref[...], grad, NT).astype(BF16)
    for head in range(HEADS):
        heard_ref[head] = made[head * HEAD : (head + 1) * HEAD]


def early_terms_kernel(
    core_ref,
    second_ref,
    slope_ref,
    active_ref,
    grad_ref,
    heard_ref,
    down_ref,
    gup_ref,
    ours_ref,
    theirs_ref,
):
    core = core_ref[0]
    width = second_ref.shape[1]
    turned_second = second_ref[...].T
    grad = grad_ref[...]
    proj = dot(heard_ref[...], grad, NN).astype(BF16)
    for block in range(4):
        cols = slice(block * width, (block + 1) * width)
        gup = (dot(grad, down_ref[cols, :], NT) * slope_ref[:, cols].astype(F32)).astype(BF16)
        gup_ref[:, cols] = gup
        up = dot(turned_second, gup, NN).astype(BF16)
        down = dot(active_ref[:, cols].T, grad, NN).astype(BF16)
        first = proj[block * 64 : (block + 1) * 64]
        last = proj[256 + block * 64 : 256 + (block + 1) * 64]
        ours_ref[block, :width, :] = jnp.where(core == 0, up, down)
        theirs_ref[block, :width, :] = jnp.where(core == 0, down, up)
        ours_ref[block, width:, :] = jnp.where(core == 0, first, last)
        theirs_ref[block, width:, :] = jnp.where(core == 0, last, first)


def second_grad_kernel(gup_ref, up_ref, gsecond_ref):
    gsecond_ref[...] = dot(gup_ref[...], up_ref[...], NT)


def late_terms_kernel(core_ref, gqkv_ref, first_ref, ours_ref, theirs_ref):
    core = core_ref[0]
    total = jnp.zeros((3 * HEAD, first_ref.shape[2]), F32)
    for block in range(8):
        total = total + dot(gqkv_ref[block], first_ref[block], NN)
    total = jnp.concatenate([total, jnp.zeros((HEAD, total.shape[1]), F32)], 0).T
    half = total.shape[0] // 2
    upper, lower = total[:half].astype(BF16), total[half:].astype(BF16)
    ours_ref[...] = jnp.where(core == 0, upper, lower)
    theirs_ref[...] = jnp.where(core == 0, lower, upper)


def split_kernel(count, pieces, at_ref, *refs):
    sources, targets = refs[:count], refs[count:]
    extent = targets[0].shape[0]
    at = at_ref[0]
    for step in range(pieces):
        start = pl.multiple_of(lax.rem(at + step, pieces) * extent, extent)
        total = sources[0][pl.ds(start, extent), :].astype(F32)
        for source in sources[1:]:
            total = total + source[pl.ds(start, extent), :].astype(F32)
        targets[step][...] = total.astype(BF16)


def place_kernel(at_ref, *refs):
    sources, target = refs[:-1], refs[-1]
    count, extent, at = len(sources), sources[0].shape[0], at_ref[0]
    for step, source in enumerate(sources):
        start = pl.multiple_of(lax.rem(at + count - step, count) * extent, extent)
        target[pl.ds(start, extent), :] = source[...]


def columns_kernel(at_ref, *refs):
    sources, (ours_ref, theirs_ref) = refs[:-2], refs[-2:]
    total = sources[0][...].astype(F32)
    for source in sources[1:]:
        total = total + source[...].astype(F32)
    half = total.shape[1] // 2
    left, right = total[:, :half].astype(BF16), total[:, half:].astype(BF16)
    ours_ref[...] = jnp.where(at_ref[0] == 0, left, right)
    theirs_ref[...] = jnp.where(at_ref[0] == 0, right, left)


def out_kernel(core_ref, a_ref, b_ref, other_a_ref, other_b_ref, up_ref, down_ref, qkv_ref, proj_ref):
    core = core_ref[0]
    width = down_ref.shape[1]

    def parts(first_ref, second_ref):
        early, late = [], []
        for z in range(4):
            first = jnp.concatenate([first_ref[0, z, 0], first_ref[0, z, 1]], 1)
            second = jnp.concatenate([second_ref[z, 0, 0, :LAST], second_ref[z, 0, 1, :LAST]], 1)
            early += [first, second]
        for half in range(2):
            late += [second_ref[z, 0, half, LAST : LAST + HEAD] for z in range(4)]
        return jnp.concatenate(early, 0).astype(F32), [v.astype(F32) for v in late]

    mine, late = parts(a_ref, b_ref)
    other, other_late = parts(other_a_ref, other_b_ref)
    low, high = jnp.where(core == 0, mine, other), jnp.where(core == 0, other, mine)
    up_ref[...] = low[:width]
    down_ref[...] = high[:width]
    proj_ref[0] = low[width:]
    proj_ref[1] = high[width:]
    for head in range(HEADS):
        low = jnp.where(core == 0, late[head], other_late[head])
        high = jnp.where(core == 0, other_late[head], late[head])
        for part in range(3):
            at = part * width + head * HEAD
            qkv_ref[0, :, at : at + HEAD] = low[:, part * HEAD : (part + 1) * HEAD]
            qkv_ref[1, :, at : at + HEAD] = high[:, part * HEAD : (part + 1) * HEAD]


def halves_kernel(at_ref, mine_ref, other_ref, a_ref, b_ref):
    at = at_ref[0]
    first, last = a_ref.shape[0] // 2, b_ref.shape[0] // 2
    for source, to in ((mine_ref, at), (other_ref, 1 - at)):
        a_ref[pl.ds(pl.multiple_of(to * first, 16), first), :] = source[:first, :]
        b_ref[pl.ds(pl.multiple_of(to * last, 16), last), :] = source[first:, :]


VMEM = pl.BlockSpec(memory_space=pltpu.VMEM)
SMEM = pl.BlockSpec(memory_space=pltpu.SMEM)
MIB = 1024 * 1024


def shaped(shape, dtype):
    return jax.ShapeDtypeStruct(shape, dtype)


def call(kernel, outs, *args, words=0, limit=12, scratch=(), name=None):
    single = not isinstance(outs, tuple)
    shapes = (outs,) if single else outs
    made = pl.pallas_call(
        kernel,
        out_shape=shapes,
        in_specs=[SMEM] * words + [VMEM] * (len(args) - words),
        out_specs=tuple(VMEM for _ in shapes),
        scratch_shapes=list(scratch),
        compiler_params=pltpu.CompilerParams(vmem_limit_bytes=limit * MIB),
        cost_estimate=pl.CostEstimate(flops=0, bytes_accessed=1024, transcendentals=0),
        name=name,
    )(*args)
    return made[0] if single else made


def attend(core, mine, other, low, high):
    return call(
        attend_kernel,
        (shaped((8, HEAD, 2 * SPAN), BF16), shaped((8, TILE), F32)),
        core, mine, other, low, high,
        words=1, limit=10,
        scratch=[pltpu.VMEM((2048, HEAD), BF16), pltpu.VMEM((2048, TILE), F32)],
        name="attend",
    )


def attend_back(core, mine, other, low, high, out, lse, grad):
    return call(
        attend_back_kernel,
        (shaped((8, 3 * HEAD, 2 * SPAN), BF16), shaped((8, 2 * HEAD, 2 * SPAN), BF16)),
        core, mine, other, low, high, out, lse, grad,
        words=1, limit=10,
        scratch=[
            pltpu.VMEM((2048, HEAD), BF16),
            pltpu.VMEM((2048, HEAD), BF16),
            pltpu.VMEM((HEAD, 2048), F32),
            pltpu.VMEM((HEAD, 2048), F32),
        ],
        name="attend_back",
    )


def swap(array, axis):
    return lax.ppermute(array, axis, [(0, 1), (1, 0)])


def word(value):
    return value.astype(jnp.int32).reshape(1)


def spread_from(pieces, axis):
    count = len(pieces)
    return [pieces[0]] + [
        lax.ppermute(pieces[s], axis, [(i, (i + s) % count) for i in range(count)])
        for s in range(1, count)
    ]


def split(arrays, axis, pieces):
    extent = arrays[0].shape[0] // pieces
    shapes = tuple(shaped((extent, arrays[0].shape[1]), BF16) for _ in range(pieces))
    return call(
        partial(split_kernel, len(arrays), pieces), shapes, word(lax.axis_index(axis)), *arrays,
        words=1, limit=56, name="split",
    )


def placed(pieces, axis):
    extent, width = pieces[0].shape
    return call(
        place_kernel, shaped((len(pieces) * extent, width), BF16),
        word(lax.axis_index(axis)), *pieces,
        words=1, limit=8, name="place",
    )


def normed_of(hidden):
    centred = hidden - jnp.mean(hidden, -1, keepdims=True)
    inv = lax.rsqrt(jnp.mean(centred * centred, -1, keepdims=True) + EPS)
    return centred * inv, inv


def turned(tile, cosine, sine):
    first, second = tile[:8], tile[8:16]
    return jnp.concatenate(
        [first * cosine - second * sine, second * cosine + first * sine, tile[16:]], 0
    )


def per_device(
    inputs,
    lengths,
    norm_gain,
    norm_bias,
    qkv_weight,
    qkv_bias,
    proj_weight,
    up_weight,
    up_bias,
    down_weight,
    branch_bias,
    cotangent,
):
    section = lax.axis_index("section")
    core = lax.axis_index("core")
    block = lax.axis_index(XZ)
    micros, span, width = inputs.shape
    rows = micros * span
    gains = norm_gain[0].astype(F32)
    shifts = norm_bias[0].astype(F32)
    w_qkv, w_proj, w_up, w_down = qkv_weight[0], proj_weight[0], up_weight[0], down_weight[0]
    b_qkv = qkv_bias.astype(F32)
    b_up = up_bias[0].astype(F32)
    b_branch = jnp.sum(branch_bias[0].astype(F32), 0)
    core_word = word(core)

    ends = jnp.cumsum(lengths[0], -1)

    def begin_of(row):
        after = row[None, :, None] >= ends[:, None, :]
        return jnp.sum(jnp.where(after, lengths[0][:, None, :], 0), -1)

    heard_rows = (
        (2 * jnp.arange(8, dtype=jnp.int32)[:, None] + core) * span
        + jnp.arange(span, dtype=jnp.int32)[None]
    ).reshape(-1)
    low = begin_of(heard_rows).reshape(8, TILE)
    high = jnp.broadcast_to(heard_rows[None], (micros, 8 * span)).reshape(8, TILE)
    own_rows = (2 * block + core) * span + jnp.arange(span, dtype=jnp.int32)
    position = (own_rows[None] - begin_of(own_rows)).reshape(1, rows).astype(F32)
    ladder = jnp.exp(-math.log(10000.0) * (jnp.arange(8, dtype=F32) * (2.0 / 16)))
    angle = ladder[:, None] * position
    cosine, sine = jnp.cos(angle), jnp.sin(angle)
    heard_position = (heard_rows[None] - begin_of(heard_rows)).reshape(micros, 8, span)
    heard_position = jnp.moveaxis(heard_position, 0, 1).reshape(8, 1, rows).astype(F32)
    heard_angle = ladder[None, :, None] * heard_position
    heard_cosine, heard_sine = jnp.cos(heard_angle), jnp.sin(heard_angle)

    def front(hidden):
        tiles, first, second = call(
            front_kernel,
            (
                shaped((HEADS, 3 * HEAD, rows), BF16),
                shaped((rows, width), BF16),
                shaped((rows, width), BF16),
            ),
            hidden, gains, shifts, w_qkv, b_qkv, cosine, sine,
            limit=12, name="front",
        )
        mine = lax.all_to_all(tiles, XZ, 0, 0, tiled=True)
        other = swap(mine, "core")
        return first, second, mine, other

    def mlp_of(second):
        up = dot(second, w_up, NN) + b_up
        phi = 0.5 * (1.0 + lax.erf(up * (1.0 / math.sqrt(2.0))))
        bell = jnp.exp(-0.5 * up * up) * (1.0 / math.sqrt(2.0 * math.pi))
        active = (up * phi).astype(BF16)
        slope = (phi + up * bell).astype(BF16)
        return active, slope

    def forward(hidden):
        first, second, mine, other = front(hidden)
        active, slope = mlp_of(second)
        base = hidden.astype(F32) + dot(active, w_down, NN) + b_branch
        heard, lse = attend(core_word, mine, other, low, high)
        return base, first, second, mine, other, active, slope, heard, lse

    def finish(base, heard_rows):
        return (base + dot(heard_rows, w_proj, TN)).astype(BF16)

    def heard_grad(received, own):
        grad_in, ggo = call(
            grad_kernel,
            (shaped((rows, width), BF16), shaped((HEADS, HEAD, rows), BF16)),
            word(section), received, own, w_proj,
            words=1, name="grad",
        )
        return grad_in, lax.all_to_all(ggo, XZ, 0, 0, tiled=True)

    def joined(gmine, gother, *along):
        return call(
            join_kernel, shaped((HEADS, (3 + len(along)) * HEAD, rows), BF16),
            gmine, swap(gother, "core"), heard_cosine, heard_sine, *along, name="join",
        )

    def rows_back(back, hidden, grad_in, gsecond):
        return call(
            back_kernel,
            (shaped((rows, width), BF16), shaped((8, width), F32), shaped((8, 3 * width), F32)),
            back, hidden, grad_in, gsecond, gains, w_qkv,
            scratch=[pltpu.VMEM((width, rows), BF16)], limit=56, name="back",
        )

    def mlp_back(grad_in, slope):
        gup = (dot(grad_in, w_down, NT) * slope.astype(F32)).astype(BF16)
        return gup, dot(gup, w_up, NT)

    entry = inputs.reshape(rows, width)
    loss_grad = cotangent.reshape(rows, width)
    grad_in, ggo = heard_grad(loss_grad, loss_grad)
    base, *_, heard, _ = forward(entry)
    heard, ggo = lax.optimization_barrier((heard, ggo))
    heard_rows = lax.all_to_all(heard, XZ, 0, 0, tiled=True).reshape(width, rows)
    heard_rows, base = lax.optimization_barrier((heard_rows, base))
    sent = finish(base, heard_rows)
    received = lax.ppermute(sent, "section", [(0, 1)])
    entry = jnp.where(section == 1, received, entry)
    base, first, second, mine, other, active, slope, heard, lse = forward(entry)
    mine, first = lax.optimization_barrier((mine, first))
    first_all = jnp.broadcast_to(first[None], (8, rows, width))
    first_all = lax.all_to_all(first_all, XZ, 0, 0, tiled=True)
    _, gsecond = mlp_back(grad_in, slope)
    gmine, gother = attend_back(core_word, mine, other, low, high, heard, lse, ggo)
    gother, first_all = lax.optimization_barrier((gother, first_all))
    back = lax.all_to_all(joined(gmine, gother, heard), XZ, 0, 0, tiled=True)
    sent_back, _, _ = rows_back(back, entry, grad_in, gsecond)
    received = lax.ppermute(sent_back, "section", [(1, 0)])
    heard_rows = back[:, 3 * HEAD :].reshape(width, rows)
    result = finish(base, heard_rows)
    received, result, heard_rows = lax.optimization_barrier((received, result, heard_rows))
    grad_in, ggo = heard_grad(received, loss_grad)
    gup, *early = call(
        early_terms_kernel,
        (shaped((rows, 4 * width), BF16),) + (shaped((4, width + 64, width), BF16),) * 2,
        core_word, second, slope, active, grad_in, heard_rows, w_down,
        words=1, limit=56, name="early_terms",
    )
    ggo, early = lax.optimization_barrier((ggo, early))
    early = [v.reshape(-1, width) for v in early]
    pieces = split([early[0], swap(early[1], "core")], "dp", 4)
    ggo, pieces = lax.optimization_barrier((ggo, pieces))
    pieces = spread_from(pieces, "dp")
    gmine, gother = attend_back(core_word, mine, other, low, high, heard, lse, ggo)
    gmine = joined(gmine, gother)
    gmine, pieces[1], pieces[3] = lax.optimization_barrier((gmine, pieces[1], pieces[3]))
    late = call(
        late_terms_kernel,
        (shaped((width // 2, width // 2), BF16),) * 2,
        core_word, gmine, first_all,
        words=1, limit=56, name="late_terms",
    )
    gsecond = call(second_grad_kernel, shaped((rows, width), F32), gup, w_up, name="second_grad")
    back = lax.all_to_all(gmine, XZ, 0, 0, tiled=True)
    pieces = spread_from(split(pieces, "z", 4), "z")
    back, pieces, late = lax.optimization_barrier((back, pieces, late))
    late = spread_from(split([late[0], swap(late[1], "core")], "dp", 4), "dp")
    ghidden, sums, bias_sums = rows_back(back, entry, grad_in, gsecond)
    ours, theirs = call(
        columns_kernel,
        (shaped((pieces[0].shape[0], width // 2), BF16),) * 2,
        word(lax.axis_index("xl")), *pieces,
        words=1, limit=8, name="columns",
    )
    early = ours.astype(F32) + swap(theirs, "xl").astype(F32)
    small = jnp.concatenate(
        [
            sums[:4].reshape(-1),
            bias_sums[0],
            jnp.sum(gup.astype(F32), 0),
            jnp.sum(grad_in.astype(F32), 0),
        ]
    ).astype(BF16)
    small = jnp.pad(small.reshape(2, -1), ((0, 0), (0, 1024))).reshape(2, 16, width // 2)
    of_core = lambda c: lax.dynamic_index_in_dim(small, c, 0, keepdims=False)
    small = of_core(core).astype(F32) + swap(of_core(1 - core), "core").astype(F32)
    late = sum(v.astype(F32) for v in late)
    share = jnp.concatenate([early.astype(BF16), late.astype(BF16), small.astype(BF16)])
    share, ghidden = lax.optimization_barrier((share, ghidden))

    a, b = call(
        halves_kernel,
        (shaped((2 * HALF, width // 2), BF16),) * 2,
        word(lax.axis_index("xl")), share, swap(share, "xl"),
        words=1, limit=8, name="halves",
    )
    a_pieces, b_pieces = spread_from([a] * 4, "z"), spread_from([b] * 4, "dp")
    a_pieces, b_pieces = lax.optimization_barrier((a_pieces, b_pieces))
    a, b = lax.optimization_barrier((placed(a_pieces, "z"), placed(b_pieces, "dp")))
    a_pieces, b_pieces = spread_from([a] * 4, "dp"), spread_from([b] * 4, "z")
    a_pieces, b_pieces = lax.optimization_barrier((a_pieces, b_pieces))
    a, b = placed(a_pieces, "dp"), placed(b_pieces, "z")
    other_a, other_b = swap(a, "core"), swap(b, "core")
    a_spec = pl.BlockSpec((1, 4, 2, HALF, width // 2), lambda i: (i, 0, 0, 0, 0))
    b_spec = pl.BlockSpec((4, 1, 2, HALF, width // 2), lambda i: (0, i, 0, 0, 0))
    a, other_a, b, other_b = [v.reshape(4, 4, 2, HALF, width // 2) for v in (a, other_a, b, other_b)]
    up, down, qkv, proj = pl.pallas_call(
        out_kernel,
        grid=(4,),
        out_shape=(
            shaped((width, 4 * width), F32),
            shaped((4 * width, width), F32),
            shaped((2, width // 2, 3 * width), F32),
            shaped((2, width // 2, width), F32),
        ),
        in_specs=[SMEM, a_spec, b_spec, a_spec, b_spec],
        out_specs=(
            pl.BlockSpec((width, width), lambda i: (0, i)),
            pl.BlockSpec((width, width), lambda i: (i, 0)),
            pl.BlockSpec((2, 64, 3 * width), lambda i: (0, i, 0)),
            pl.BlockSpec((2, 64, width), lambda i: (0, i, 0)),
        ),
        compiler_params=pltpu.CompilerParams(vmem_limit_bytes=32 * MIB),
        cost_estimate=pl.CostEstimate(flops=0, bytes_accessed=1024, transcendentals=0),
        name="out",
    )(core_word, a, b, other_a, other_b)
    qkv, proj = qkv.reshape(width, 3 * width), proj.reshape(width, width)
    vectors = lambda v: jnp.sum(v[:, :, :, LAST + HEAD :].astype(F32), (0, 1, 2)).reshape(-1)[:3072]
    small, partner = vectors(b), vectors(other_b)
    small = jnp.where(core == 0, jnp.stack([small, partner]), jnp.stack([partner, small]))
    small = small.reshape(-1)

    return (
        result.reshape(1, micros, span, width),
        ghidden.reshape(1, micros, span, width),
        small[:1024].reshape(1, 2, width),
        small[1024:2048].reshape(1, 2, width),
        qkv[None],
        small[2048:3584][None],
        proj[None],
        up[None],
        small[3584:5632][None],
        down[None],
        jnp.broadcast_to(small[5632:6144].reshape(1, 1, width), (1, 2, width)),
    )


def solution(mesh):
    axes = ("section", "dp", "xl", "z", "core")
    fine = Mesh(mesh.devices.reshape(2, 4, 2, 4, 2), axes)
    spread = P(None, ("dp", "xl", "z", "core"), None)
    three, two = P("section", None, None), P("section", None)
    kept = P("section", None, ("dp", "xl", "z", "core"), None)
    in_specs = (
        spread, P("dp", None, None), three, three, three, two, three, three, two, three, three, spread,
    )
    out_specs = (kept, kept, three, three, three, two, three, three, two, three, three)
    return jax.shard_map(
        per_device, mesh=fine, in_specs=in_specs, out_specs=out_specs, check_vma=False
    )
```

```python
from functools import partial
import math

import jax
import jax.numpy as jnp
from jax import lax
from jax.experimental import pallas as pl
from jax.experimental.pallas import tpu as pltpu
from jax.sharding import Mesh, PartitionSpec as P

HEADS = 8
EPS = 1e-05
F32 = jnp.float32
BF16 = jnp.bfloat16
XZ = ("xl", "z")
LOG2E = math.log2(math.e)
SPAN = 128
HEAD = 64
TILE = 256
SCALE = 1.0 / math.sqrt(HEAD)
LAST = 32
EARLY = 144
HALF = 112


def dot(a, b, dims):
    return lax.dot_general(a, b, (dims, ((), ())), preferred_element_type=F32)


NN = ((1,), (0,))
NT = ((1,), (1,))
TN = ((0,), (0,))


def lanes_of(ref, block, at, lanes):
    return jnp.concatenate(
        [ref[2 * block, at : at + HEAD, lanes], ref[2 * block + 1, at : at + HEAD, lanes]], axis=1
    )


def both_of(mine_ref, other_ref, pair, at, lanes):
    return jnp.concatenate(
        [lanes_of(mine_ref, pair, at, lanes), lanes_of(other_ref, pair, at, lanes)], 1
    )


def lanes_at(micro):
    return pl.ds(pl.multiple_of(micro * SPAN, SPAN), SPAN)


def key_offsets():
    row = lax.broadcasted_iota(jnp.int32, (TILE, TILE), 0)
    return row + jnp.where(row >= SPAN, SPAN, 0)


def allowed_in(offsets, low, high, chunk, core, tile):
    side = core if chunk % 2 == 0 else 1 - core
    base = (chunk // 2) * (2 * TILE) + side * SPAN
    seen = offsets >= low - base
    if chunk // 2 == tile:
        seen = seen & (offsets <= high - base)
    return seen


def attend_kernel(core_ref, mine_ref, other_ref, low_ref, high_ref, out_ref, lse_ref, keys, scores):
    core = core_ref[0]
    offsets = key_offsets()

    def one_micro(micro, carry):
        lanes = lanes_at(micro)
        for chunk in range(8):
            ref, at = (mine_ref if chunk % 2 == 0 else other_ref), HEAD
            keys[chunk * TILE : (chunk + 1) * TILE, :] = lanes_of(ref, chunk // 2, at, lanes).T
        for tile in range(4):
            row = pl.ds(micro * 4 + tile, 1)
            low, high = low_ref[row, :], high_ref[row, :]
            query = lanes_of(mine_ref, tile, 0, lanes)
            top = jnp.full((8, TILE), -1e30, F32)
            for chunk in range(2 * tile + 2):
                rows = slice(chunk * TILE, (chunk + 1) * TILE)
                raw = dot(keys[rows, :], query, NN) * (SCALE * LOG2E)
                raw = jnp.where(allowed_in(offsets, low, high, chunk, core, tile), raw, -1e30)
                scores[rows, :] = raw
                top = jnp.maximum(top, jnp.max(raw.reshape(-1, 8, TILE), axis=0))
            top = jnp.max(top, axis=0, keepdims=True)
            total = jnp.zeros((8, TILE), F32)
            heard = jnp.zeros((HEAD, TILE), F32)
            for pair in range(tile + 1):
                rows = slice(2 * pair * TILE, 2 * (pair + 1) * TILE)
                weight = jnp.exp2(scores[rows, :] - top)
                total = total + jnp.sum(weight.reshape(-1, 8, TILE), axis=0)
                value = both_of(mine_ref, other_ref, pair, 2 * HEAD, lanes)
                heard = heard + dot(value, weight.astype(BF16), NN)
            total = jnp.sum(total, axis=0, keepdims=True)
            heard = (heard / total).astype(BF16)
            out_ref[2 * tile, :, lanes] = heard[:, :SPAN]
            out_ref[2 * tile + 1, :, lanes] = heard[:, SPAN:]
            lse_ref[row, :] = top + jnp.log2(total)
        return carry

    lax.fori_loop(0, 2, one_micro, 0)


def attend_back_kernel(
    core_ref,
    mine_ref,
    other_ref,
    low_ref,
    high_ref,
    out_ref,
    lse_ref,
    grad_ref,
    gmine_ref,
    gother_ref,
    keys,
    values,
    gkeys,
    gvalues,
):
    core = core_ref[0]
    offsets = key_offsets()

    def one_micro(micro, carry):
        lanes = lanes_at(micro)
        for chunk in range(8):
            rows = slice(chunk * TILE, (chunk + 1) * TILE)
            ref, at = (mine_ref if chunk % 2 == 0 else other_ref), HEAD
            keys[rows, :] = lanes_of(ref, chunk // 2, at, lanes).T
            values[rows, :] = lanes_of(ref, chunk // 2, at + HEAD, lanes).T
        for tile in range(4):
            row = pl.ds(micro * 4 + tile, 1)
            low, high, lse = low_ref[row, :], high_ref[row, :], lse_ref[row, :]
            query = lanes_of(mine_ref, tile, 0, lanes)
            grad = lanes_of(grad_ref, tile, 0, lanes)
            heard = lanes_of(out_ref, tile, 0, lanes)
            centre = jnp.sum(grad.astype(F32) * heard.astype(F32), axis=0, keepdims=True)
            gquery = jnp.zeros((HEAD, TILE), F32)
            for pair in range(tile + 1):
                rows = slice(2 * pair * TILE, 2 * (pair + 1) * TILE)
                raw = dot(keys[rows, :], query, NN) * (SCALE * LOG2E) - lse
                raws = [
                    jnp.where(
                        allowed_in(offsets, low, high, 2 * pair + side, core, tile),
                        raw[side * TILE : (side + 1) * TILE],
                        -1e30,
                    )
                    for side in range(2)
                ]
                prob = jnp.exp2(jnp.concatenate(raws, 0))
                gprob = dot(values[rows, :], grad, NN)
                gscore = (prob * (gprob - centre)).astype(BF16)
                gquery = gquery + dot(both_of(mine_ref, other_ref, pair, HEAD, lanes), gscore, NN)
                gkey = dot(query, gscore, NT)
                gvalue = dot(grad, prob.astype(BF16), NT)
                if pair == tile:
                    gkeys[:, rows], gvalues[:, rows] = gkey, gvalue
                else:
                    gkeys[:, rows] += gkey
                    gvalues[:, rows] += gvalue
            gquery = (gquery * SCALE).astype(BF16)
            gmine_ref[2 * tile, :HEAD, lanes] = gquery[:, :SPAN]
            gmine_ref[2 * tile + 1, :HEAD, lanes] = gquery[:, SPAN:]
        for chunk in range(8):
            ref, at = (gmine_ref, HEAD) if chunk % 2 == 0 else (gother_ref, 0)
            for half in range(2):
                cols = slice(chunk * TILE + half * SPAN, chunk * TILE + (half + 1) * SPAN)
                block = 2 * (chunk // 2) + half
                ref[block, at : at + HEAD, lanes] = (gkeys[:, cols] * SCALE).astype(BF16)
                ref[block, at + HEAD : at + 2 * HEAD, lanes] = gvalues[:, cols].astype(BF16)
        return carry

    lax.fori_loop(0, 2, one_micro, 0)


def front_kernel(
    hidden_ref, gain_ref, shift_ref, weight_ref, bias_ref, cos_ref, sin_ref, tiles_ref, second_ref, *copies
):
    xhat, _ = normed_of(hidden_ref[...].astype(F32))
    first = (xhat * gain_ref[0:1, :] + shift_ref[0:1, :]).astype(BF16)
    for copies_ref in copies:
        for block in range(copies_ref.shape[0]):
            copies_ref[block] = first
    second_ref[...] = (xhat * gain_ref[1:2, :] + shift_ref[1:2, :]).astype(BF16)
    width = first.shape[1]
    cosine, sine = cos_ref[...], sin_ref[...]
    for part in range(3):
        cols = slice(part * width, (part + 1) * width)
        made = (dot(first, weight_ref[:, cols], NN) + bias_ref[:, cols]).T
        for head in range(HEADS):
            tile = made[head * HEAD : (head + 1) * HEAD]
            if part < 2:
                tile = turned(tile, cosine, sine)
            tiles_ref[head, part * HEAD : (part + 1) * HEAD, :] = tile.astype(BF16)


def back_kernel(
    core_ref, back_ref, hidden_ref, grad_ref, gsecond_ref, gain_ref, weight_ref, *refs
):
    early_refs = refs[: len(refs) - 2 if len(refs) == 2 else 1]
    ghidden_ref, *vector_refs, gqkv = refs[len(early_refs) :]
    width = hidden_ref.shape[1]
    rows = hidden_ref.shape[0]
    gfirst = jnp.zeros((rows, width), F32)
    ones = jnp.ones((8, rows), BF16)
    biases, gains, shifts = [], [], []
    for part in range(3):
        cols = slice(part * width, (part + 1) * width)
        for head in range(HEADS):
            gqkv[head * HEAD : (head + 1) * HEAD, :] = back_ref[head, part * HEAD : (part + 1) * HEAD, :]
        made = gqkv[...]
        gfirst = gfirst + dot(made.T, weight_ref[:, cols], NT)
        biases.append(dot(ones, made, NT)[:1])
    xhat, inv = normed_of(hidden_ref[...].astype(F32))
    gsecond = gsecond_ref[...]
    total = grad_ref[...].astype(F32)
    for which, grad in ((0, gfirst), (1, gsecond)):
        e = grad * gain_ref[which : which + 1, :]
        total = total + inv * (
            e - jnp.mean(e, -1, keepdims=True) - xhat * jnp.mean(e * xhat, -1, keepdims=True)
        )
        gains.append(jnp.sum(grad * xhat, 0, keepdims=True))
        shifts.append(jnp.sum(grad, 0, keepdims=True))
    ghidden_ref[...] = total.astype(BF16)
    if not vector_refs:
        return
    early = jnp.sum(early_refs[0][...], 0, keepdims=True)
    wide = gains + shifts + biases + [early[:, i * width : (i + 1) * width] for i in range(5)]
    lines = [v[:, half * width // 2 : (half + 1) * width // 2] for v in wide for half in range(2)]
    blank = [jnp.zeros((4, width // 2), F32)]
    first = jnp.concatenate(lines[:12] + blank, 0).astype(BF16)
    last = jnp.concatenate(lines[12:] + blank, 0).astype(BF16)
    ours_ref, theirs_ref = vector_refs
    ours_ref[...] = jnp.where(core_ref[0] == 0, first, last)
    theirs_ref[...] = jnp.where(core_ref[0] == 0, last, first)


def join_kernel(mine_ref, other_ref, cos_ref, sin_ref, *refs):
    out_ref = refs[-1]
    for block in range(8):
        if len(refs) > 1:
            out_ref[block, 3 * HEAD :, :] = refs[0][block]
        cosine, sine = cos_ref[block], -sin_ref[block]
        for part in range(3):
            rows = slice(part * HEAD, (part + 1) * HEAD)
            tile = mine_ref[block, rows, :].astype(F32)
            if part > 0:
                at = (part - 1) * HEAD
                tile = tile + other_ref[block, at : at + HEAD, :].astype(F32)
            if part < 2:
                tile = turned(tile, cosine, sine)
            out_ref[block, rows, :] = tile.astype(BF16)


def grad_kernel(section_ref, received_ref, own_ref, weight_ref, grad_ref, heard_ref):
    grad = jnp.where(section_ref[0] == 1, own_ref[...], received_ref[...])
    grad_ref[...] = grad
    made = dot(weight_ref[...], grad, NT).astype(BF16)
    for head in range(HEADS):
        heard_ref[head] = made[head * HEAD : (head + 1) * HEAD]


def early_terms_kernel(
    core_ref,
    second_ref,
    slope_ref,
    active_ref,
    grad_ref,
    heard_ref,
    down_ref,
    gup_ref,
    ours_ref,
    theirs_ref,
    sums_ref,
):
    core = core_ref[0]
    width = second_ref.shape[1]
    turned_second = second_ref[...].T
    grad = grad_ref[...]
    proj = dot(heard_ref[...], grad, NN).astype(BF16)
    sums_ref[:, 4 * width :] = jnp.sum(grad.astype(F32).reshape(-1, 8, width), 0)
    for block in range(4):
        cols = slice(block * width, (block + 1) * width)
        gup = (dot(grad, down_ref[cols, :], NT) * slope_ref[:, cols].astype(F32)).astype(BF16)
        gup_ref[:, cols] = gup
        sums_ref[:, cols] = jnp.sum(gup.astype(F32).reshape(-1, 8, width), 0)
        up = dot(turned_second, gup, NN).astype(BF16)
        down = dot(active_ref[:, cols].T, grad, NN).astype(BF16)
        first = proj[block * 64 : (block + 1) * 64]
        last = proj[256 + block * 64 : 256 + (block + 1) * 64]
        ours_ref[block, :width, :] = jnp.where(core == 0, up, down)
        theirs_ref[block, :width, :] = jnp.where(core == 0, down, up)
        ours_ref[block, width:, :] = jnp.where(core == 0, first, last)
        theirs_ref[block, width:, :] = jnp.where(core == 0, last, first)


def second_grad_kernel(gup_ref, up_ref, gsecond_ref):
    gsecond_ref[...] = dot(gup_ref[...], up_ref[...], NT)


def late_terms_kernel(core_ref, gqkv_ref, first_ref, ours_ref, theirs_ref):
    core = core_ref[0]
    total = jnp.zeros((3 * HEAD, first_ref.shape[2]), F32)
    for block in range(8):
        total = total + dot(gqkv_ref[block], first_ref[block], NN)
    total = jnp.concatenate([total, jnp.zeros((HEAD, total.shape[1]), F32)], 0).T
    half = total.shape[0] // 2
    upper, lower = total[:half].astype(BF16), total[half:].astype(BF16)
    ours_ref[...] = jnp.where(core == 0, upper, lower)
    theirs_ref[...] = jnp.where(core == 0, lower, upper)


def place_ring_kernel(at_ref, *refs):
    at = at_ref[0]
    for sources, target in ((refs[:5], refs[10]), (refs[5:10], refs[11])):
        own, back, ahead, far_a, far_b = sources
        extent, half = own.shape[0], far_a.shape[0]
        for step, source in ((0, own), (3, back), (1, ahead)):
            start = pl.multiple_of(lax.rem(at + step, 4) * extent, 16)
            target[pl.ds(start, extent), :] = source[...]
        start = lax.rem(at + 2, 4) * extent
        target[pl.ds(pl.multiple_of(start, 16), half), :] = far_a[...]
        target[pl.ds(pl.multiple_of(start + half, 16), half), :] = far_b[...]


def split_kernel(count, pieces, at_ref, *refs):
    sources, targets = refs[:count], refs[count:]
    extent = targets[0].shape[0]
    at = at_ref[0]
    for step in range(pieces):
        start = pl.multiple_of(lax.rem(at + step, pieces) * extent, extent)
        total = sources[0][pl.ds(start, extent), :].astype(F32)
        for source in sources[1:]:
            total = total + source[pl.ds(start, extent), :].astype(F32)
        targets[step][...] = total.astype(BF16)


def ring_kernel(at_ref, first_ref, last_ref, own_ref, next_ref, back_ref, far_a_ref, far_b_ref):
    at = at_ref[0]
    extent = own_ref.shape[0]

    def piece(step):
        rows = pl.ds(pl.multiple_of(lax.rem(at + step, 4) * extent, 16), extent)
        return (first_ref[rows, :].astype(F32) + last_ref[rows, :].astype(F32)).astype(BF16)

    own_ref[...] = piece(0)
    next_ref[...] = piece(1)
    back_ref[...] = piece(3)
    far = piece(2)
    far_a_ref[...] = far[: extent // 2]
    far_b_ref[...] = far[extent // 2 :]


def fold_kernel(next_ref, back_ref, far_a_ref, far_b_ref, to_next_ref, to_back_ref):
    half = far_a_ref.shape[0]
    total = next_ref[:half].astype(F32) + far_a_ref[...].astype(F32)
    to_next_ref[:half] = total.astype(BF16)
    to_next_ref[half:] = next_ref[half:]
    to_back_ref[:half] = back_ref[:half]
    total = back_ref[half:].astype(F32) + far_b_ref[...].astype(F32)
    to_back_ref[half:] = total.astype(BF16)


def split_both_kernel(z_ref, dp_ref, *refs):
    split_kernel(3, 4, z_ref, *refs[:3], *refs[5:9])
    split_kernel(2, 4, dp_ref, *refs[3:5], *refs[9:])


def place_kernel(at_ref, *refs):
    sources, target = refs[:-1], refs[-1]
    count, extent, at = len(sources), sources[0].shape[0], at_ref[0]
    for step, source in enumerate(sources):
        start = pl.multiple_of(lax.rem(at + count - step, count) * extent, extent)
        target[pl.ds(start, extent), :] = source[...]


def share_kernel(*refs):
    early, late, small, out_ref = refs[:4], refs[4:8], refs[8:10], refs[10]

    def total(sources):
        made = sources[0][...].astype(F32)
        for source in sources[1:]:
            made = made + source[...].astype(F32)
        return made.astype(BF16)

    made = total(early)
    rows, half = made.shape[0], made.shape[1] // 2
    out_ref[:rows, :] = made[:, :half]
    out_ref[rows : 2 * rows, :] = made[:, half:]
    out_ref[2 * rows : 2 * rows + HEAD, :] = total(late)
    out_ref[2 * rows + HEAD :, :] = total(small)


def out_kernel(
    core_ref,
    a_ref,
    b_ref,
    other_a_ref,
    other_b_ref,
    up_ref,
    down_ref,
    qkv_ref,
    proj_ref,
    gain_ref,
    shift_ref,
    qkv_bias_ref,
    up_bias_ref,
    branch_ref,
    vectors,
):
    core = core_ref[0]
    width = down_ref.shape[1]

    def parts(first_ref, second_ref):
        early, late = [], []
        for z in range(4):
            first = jnp.concatenate([first_ref[0, z, 0], first_ref[0, z, 1]], 1)
            second = jnp.concatenate([second_ref[z, 0, 0, :LAST], second_ref[z, 0, 1, :LAST]], 1)
            early += [first, second]
        for half in range(2):
            late += [second_ref[z, 0, half, LAST : LAST + HEAD] for z in range(4)]
        return jnp.concatenate(early, 0).astype(F32), [v.astype(F32) for v in late]

    mine, late = parts(a_ref, b_ref)
    other, other_late = parts(other_a_ref, other_b_ref)
    low, high = jnp.where(core == 0, mine, other), jnp.where(core == 0, other, mine)
    up_ref[...] = low[:width]
    down_ref[...] = high[:width]
    proj_ref[0] = low[width:]
    proj_ref[1] = high[width:]
    for head in range(HEADS):
        low = jnp.where(core == 0, late[head], other_late[head])
        high = jnp.where(core == 0, other_late[head], late[head])
        for part in range(3):
            at = part * width + head * HEAD
            qkv_ref[0, :, at : at + HEAD] = low[:, part * HEAD : (part + 1) * HEAD]
            qkv_ref[1, :, at : at + HEAD] = high[:, part * HEAD : (part + 1) * HEAD]
    step = pl.program_id(0)

    def vector_sum(ref):
        return sum(ref[z, 0, half, LAST + HEAD :].astype(F32) for z in range(4) for half in range(2))

    low, high = vector_sum(b_ref), vector_sum(other_b_ref)

    @pl.when(step == 0)
    def _():
        vectors[0], vectors[1] = low, high

    @pl.when(step > 0)
    def _():
        vectors[0] += low
        vectors[1] += high

    @pl.when(step == 3)
    def _():
        mine, other = vectors[0], vectors[1]
        first = jnp.where(core == 0, mine, other)
        last = jnp.where(core == 0, other, mine)
        lines = [first[i : i + 1] for i in range(12)] + [last[i : i + 1] for i in range(12)]
        wide = [jnp.concatenate(lines[2 * i : 2 * i + 2], 1) for i in range(12)]
        for row in range(2):
            gain_ref[row : row + 1, :] = wide[row]
            shift_ref[row : row + 1, :] = wide[2 + row]
            branch_ref[row : row + 1, :] = wide[11]
        qkv_bias_ref[...] = jnp.concatenate(wide[4:7], 1)
        up_bias_ref[...] = jnp.concatenate(wide[7:11], 1)


def halves_kernel(at_ref, mine_ref, other_ref, a_ref, b_ref):
    at = at_ref[0]
    early = EARLY
    total = mine_ref[: 2 * early].astype(F32) + other_ref[: 2 * early].astype(F32)
    total = total.astype(BF16)
    for half in range(2):
        a_ref[half * HALF : (half + 1) * HALF] = total[half * early : half * early + HALF]
        b_ref[half * HALF : half * HALF + LAST] = total[half * early + HALF : (half + 1) * early]
    for source, to in ((mine_ref, at), (other_ref, 1 - at)):
        rows = pl.ds(pl.multiple_of(to * HALF + LAST, 16), HALF - LAST)
        b_ref[rows, :] = source[2 * early :, :]


VMEM = pl.BlockSpec(memory_space=pltpu.VMEM)
SMEM = pl.BlockSpec(memory_space=pltpu.SMEM)
MIB = 1024 * 1024


def shaped(shape, dtype):
    return jax.ShapeDtypeStruct(shape, dtype)


def call(kernel, outs, *args, words=0, limit=12, scratch=(), name=None):
    single = not isinstance(outs, tuple)
    shapes = (outs,) if single else outs
    made = pl.pallas_call(
        kernel,
        out_shape=shapes,
        in_specs=[SMEM] * words + [VMEM] * (len(args) - words),
        out_specs=tuple(VMEM for _ in shapes),
        scratch_shapes=list(scratch),
        compiler_params=pltpu.CompilerParams(vmem_limit_bytes=limit * MIB),
        cost_estimate=pl.CostEstimate(flops=0, bytes_accessed=1024, transcendentals=0),
        name=name,
    )(*args)
    return made[0] if single else made


def attend(core, mine, other, low, high):
    return call(
        attend_kernel,
        (shaped((8, HEAD, 2 * SPAN), BF16), shaped((8, TILE), F32)),
        core, mine, other, low, high,
        words=1, limit=10,
        scratch=[pltpu.VMEM((2048, HEAD), BF16), pltpu.VMEM((2048, TILE), F32)],
        name="attend",
    )


def attend_back(core, mine, other, low, high, out, lse, grad):
    return call(
        attend_back_kernel,
        (shaped((8, 3 * HEAD, 2 * SPAN), BF16), shaped((8, 2 * HEAD, 2 * SPAN), BF16)),
        core, mine, other, low, high, out, lse, grad,
        words=1, limit=10,
        scratch=[
            pltpu.VMEM((2048, HEAD), BF16),
            pltpu.VMEM((2048, HEAD), BF16),
            pltpu.VMEM((HEAD, 2048), F32),
            pltpu.VMEM((HEAD, 2048), F32),
        ],
        name="attend_back",
    )


def swap(array, axis):
    return lax.ppermute(array, axis, [(0, 1), (1, 0)])


def word(value):
    return value.astype(jnp.int32).reshape(1)


def spread_from(pieces, axis):
    count = len(pieces)
    return [pieces[0]] + [
        lax.ppermute(pieces[s], axis, [(i, (i + s) % count) for i in range(count)])
        for s in range(1, count)
    ]


def turn(array, axis, by):
    count = lax.axis_size(axis)
    return lax.ppermute(array, axis, [(i, (i + by) % count) for i in range(count)])


def placed(pieces, axis):
    extent, width = pieces[0].shape
    return call(
        place_kernel, shaped((len(pieces) * extent, width), BF16),
        word(lax.axis_index(axis)), *pieces,
        words=1, limit=8, name="place",
    )


def normed_of(hidden):
    centred = hidden - jnp.mean(hidden, -1, keepdims=True)
    inv = lax.rsqrt(jnp.mean(centred * centred, -1, keepdims=True) + EPS)
    return centred * inv, inv


def turned(tile, cosine, sine):
    first, second = tile[:8], tile[8:16]
    return jnp.concatenate(
        [first * cosine - second * sine, second * cosine + first * sine, tile[16:]], 0
    )


def per_device(
    inputs,
    lengths,
    norm_gain,
    norm_bias,
    qkv_weight,
    qkv_bias,
    proj_weight,
    up_weight,
    up_bias,
    down_weight,
    branch_bias,
    cotangent,
):
    section = lax.axis_index("section")
    core = lax.axis_index("core")
    block = lax.axis_index(XZ)
    micros, span, width = inputs.shape
    rows = micros * span
    gains = norm_gain[0].astype(F32)
    shifts = norm_bias[0].astype(F32)
    w_qkv, w_proj, w_up, w_down = qkv_weight[0], proj_weight[0], up_weight[0], down_weight[0]
    b_qkv = qkv_bias.astype(F32)
    b_up = up_bias[0].astype(F32)
    b_branch = jnp.sum(branch_bias[0].astype(F32), 0)
    core_word = word(core)

    one, two, three = [lengths[0][:, i] for i in range(3)]
    ends = jnp.stack([one, one + two, one + two + three], -1)

    def begin_of(row):
        after = row[None, :, None] >= ends[:, None, :]
        return jnp.sum(jnp.where(after, lengths[0][:, None, :], 0), -1)

    heard_rows = (
        (2 * jnp.arange(8, dtype=jnp.int32)[:, None] + core) * span
        + jnp.arange(span, dtype=jnp.int32)[None]
    ).reshape(-1)
    low = begin_of(heard_rows).reshape(8, TILE)
    high = jnp.broadcast_to(heard_rows[None], (micros, 8 * span)).reshape(8, TILE)
    own_rows = (2 * block + core) * span + jnp.arange(span, dtype=jnp.int32)
    position = (own_rows[None] - begin_of(own_rows)).reshape(1, rows).astype(F32)
    ladder = jnp.exp(-math.log(10000.0) * (jnp.arange(8, dtype=F32) * (2.0 / 16)))
    angle = ladder[:, None] * position
    cosine, sine = jnp.cos(angle), jnp.sin(angle)
    heard_position = (heard_rows[None] - begin_of(heard_rows)).reshape(micros, 8, span)
    heard_position = jnp.moveaxis(heard_position, 0, 1).reshape(8, 1, rows).astype(F32)
    heard_angle = ladder[None, :, None] * heard_position
    heard_cosine, heard_sine = jnp.cos(heard_angle), jnp.sin(heard_angle)

    def front(hidden, copies):
        tiles, second, *firsts = call(
            front_kernel,
            (shaped((HEADS, 3 * HEAD, rows), BF16), shaped((rows, width), BF16))
            + (shaped((HEADS, rows, width), BF16),) * copies,
            hidden, gains, shifts, w_qkv, b_qkv, cosine, sine,
            limit=12, name="front",
        )
        mine = lax.all_to_all(tiles, XZ, 0, 0, tiled=True)
        other = swap(mine, "core")
        return firsts, second, mine, other

    def mlp_of(second):
        up = dot(second, w_up, NN) + b_up
        phi = 0.5 * (1.0 + lax.erf(up * (1.0 / math.sqrt(2.0))))
        bell = jnp.exp(-0.5 * up * up) * (1.0 / math.sqrt(2.0 * math.pi))
        active = (up * phi).astype(BF16)
        slope = (phi + up * bell).astype(BF16)
        return active, slope

    def forward(hidden, copies):
        firsts, second, mine, other = front(hidden, copies)
        active, slope = mlp_of(second)
        base = hidden.astype(F32) + dot(active, w_down, NN) + b_branch
        heard, lse = attend(core_word, mine, other, low, high)
        return base, firsts, second, mine, other, active, slope, heard, lse

    def finish(base, heard_rows):
        return (base + dot(heard_rows, w_proj, TN)).astype(BF16)

    def heard_grad(received, own):
        grad_in, ggo = call(
            grad_kernel,
            (shaped((rows, width), BF16), shaped((HEADS, HEAD, rows), BF16)),
            word(section), received, own, w_proj,
            words=1, name="grad",
        )
        return grad_in, lax.all_to_all(ggo, XZ, 0, 0, tiled=True)

    def joined(gmine, gother, *along):
        return call(
            join_kernel, shaped((HEADS, (3 + len(along)) * HEAD, rows), BF16),
            gmine, swap(gother, "core"), heard_cosine, heard_sine, *along, name="join",
        )

    def rows_back(back, hidden, grad_in, gsecond, *early_sums):
        vectors = (shaped((16, width // 2), BF16),) * 2 if early_sums else ()
        return call(
            back_kernel,
            (shaped((rows, width), BF16),) + vectors,
            core_word, back, hidden, grad_in, gsecond, gains, w_qkv, *early_sums,
            words=1, scratch=[pltpu.VMEM((width, rows), BF16)], limit=56, name="back",
        )

    def mlp_back(grad_in, slope):
        gup = (dot(grad_in, w_down, NT) * slope.astype(F32)).astype(BF16)
        return gup, dot(gup, w_up, NT)

    entry = inputs.reshape(rows, width)
    loss_grad = cotangent.reshape(rows, width)
    grad_in, ggo = heard_grad(loss_grad, loss_grad)
    base, *_, heard, _ = forward(entry, 0)
    heard, ggo = lax.optimization_barrier((heard, ggo))
    heard_rows = lax.all_to_all(heard, XZ, 0, 0, tiled=True).reshape(width, rows)
    heard_rows, base = lax.optimization_barrier((heard_rows, base))
    sent = finish(base, heard_rows)
    received = lax.ppermute(sent, "section", [(0, 1)])
    entry = jnp.where(section == 1, received, entry)
    base, (firsts,), second, mine, other, active, slope, heard, lse = forward(entry, 1)
    mine, firsts = lax.optimization_barrier((mine, firsts))
    first_all = lax.all_to_all(firsts, XZ, 0, 0, tiled=True)
    _, gsecond = mlp_back(grad_in, slope)
    gmine, gother = attend_back(core_word, mine, other, low, high, heard, lse, ggo)
    gother, first_all = lax.optimization_barrier((gother, first_all))
    back = lax.all_to_all(joined(gmine, gother, heard), XZ, 0, 0, tiled=True)
    (sent_back,) = rows_back(back, entry, grad_in, gsecond)
    received = lax.ppermute(sent_back, "section", [(1, 0)])
    heard_rows = back[:, 3 * HEAD :].reshape(width, rows)
    result = finish(base, heard_rows)
    received, result, heard_rows = lax.optimization_barrier((received, result, heard_rows))
    grad_in, ggo = heard_grad(received, loss_grad)
    gup, *early, early_sums = call(
        early_terms_kernel,
        (shaped((rows, 4 * width), BF16),)
        + (shaped((4, width + 64, width), BF16),) * 2
        + (shaped((8, 5 * width), F32),),
        core_word, second, slope, active, grad_in, heard_rows, w_down,
        words=1, limit=56, name="early_terms",
    )
    ggo, early = lax.optimization_barrier((ggo, early))
    early = [v.reshape(-1, width) for v in early]
    whole, part = shaped((4 * EARLY, width), BF16), shaped((2 * EARLY, width), BF16)
    pieces = call(
        ring_kernel, (whole, whole, whole, part, part),
        word(lax.axis_index("dp")), early[0], swap(early[1], "core"),
        words=1, limit=56, name="ring",
    )
    ggo, pieces = lax.optimization_barrier((ggo, pieces))
    own, to_next, to_back, far_a, far_b = pieces
    far_a, far_b = turn(far_a, "dp", 1), turn(far_b, "dp", -1)
    gmine, gother = attend_back(core_word, mine, other, low, high, heard, lse, ggo)
    gmine, gother, far_a, far_b = lax.optimization_barrier((gmine, gother, far_a, far_b))
    to_next, to_back = call(fold_kernel, (whole, whole), to_next, to_back, far_a, far_b, name="fold")
    gmine = joined(gmine, gother)
    gmine, to_next, to_back = lax.optimization_barrier((gmine, to_next, to_back))
    pieces = [own, turn(to_next, "dp", 1), turn(to_back, "dp", -1)]
    late = call(
        late_terms_kernel,
        (shaped((width // 2, width // 2), BF16),) * 2,
        core_word, gmine, first_all,
        words=1, limit=56, name="late_terms",
    )
    gsecond = call(second_grad_kernel, shaped((rows, width), F32), gup, w_up, name="second_grad")
    back = lax.all_to_all(gmine, XZ, 0, 0, tiled=True)
    pieces, late, gsecond = lax.optimization_barrier((pieces, late, gsecond))
    made = call(
        split_both_kernel,
        (shaped((EARLY, width), BF16),) * 4 + (shaped((HEAD, width // 2), BF16),) * 4,
        word(lax.axis_index("z")), word(lax.axis_index("dp")),
        *pieces, late[0], swap(late[1], "core"),
        words=2, limit=56, name="split_both",
    )
    pieces, late = spread_from(made[:4], "z"), spread_from(made[4:], "dp")
    back, pieces = lax.optimization_barrier((back, pieces))
    ghidden, *small = rows_back(back, entry, grad_in, gsecond, early_sums)
    share = call(
        share_kernel, shaped((2 * EARLY + HEAD + 16, width // 2), BF16),
        *pieces, *late, small[0], swap(small[1], "core"), name="share",
    )
    share, ghidden = lax.optimization_barrier((share, ghidden))

    a, b = call(
        halves_kernel,
        (shaped((2 * HALF, width // 2), BF16),) * 2,
        word(lax.axis_index("xl")), share, swap(share, "xl"),
        words=1, limit=8, name="halves",
    )
    a_pieces, b_pieces = spread_from([a] * 4, "z"), spread_from([b] * 4, "dp")
    a_pieces, b_pieces = lax.optimization_barrier((a_pieces, b_pieces))
    a, b = lax.optimization_barrier((placed(a_pieces, "z"), placed(b_pieces, "dp")))
    gathers = []
    for array, axis in ((a, "dp"), (b, "z")):
        back, ahead = turn(array, axis, 1), turn(array, axis, -1)
        half = array.shape[0] // 2
        far_a, far_b = turn(back[:half], axis, 1), turn(ahead[half:], axis, -1)
        gathers.append([array, back, ahead, far_a, far_b])
    gathers = [g + [swap(v, "core") for v in g] for g in gathers]
    gathers = lax.optimization_barrier(gathers)
    placed_all = [
        call(
            place_ring_kernel, (shaped((4 * g[0].shape[0], width // 2), BF16),) * 2,
            word(lax.axis_index(axis)), *g, words=1, limit=12, name="place_ring",
        )
        for g, axis in zip(gathers, ("dp", "z"))
    ]
    (a, other_a), (b, other_b) = placed_all
    a_spec = pl.BlockSpec((1, 4, 2, HALF, width // 2), lambda i: (i, 0, 0, 0, 0))
    b_spec = pl.BlockSpec((4, 1, 2, HALF, width // 2), lambda i: (0, i, 0, 0, 0))
    a, other_a, b, other_b = [v.reshape(4, 4, 2, HALF, width // 2) for v in (a, other_a, b, other_b)]
    up, down, qkv, proj, gain, shift, bias_qkv, bias_up, branch = pl.pallas_call(
        out_kernel,
        grid=(4,),
        out_shape=(
            shaped((width, 4 * width), F32),
            shaped((4 * width, width), F32),
            shaped((2, width // 2, 3 * width), F32),
            shaped((2, width // 2, width), F32),
            shaped((2, width), F32),
            shaped((2, width), F32),
            shaped((1, 3 * width), F32),
            shaped((1, 4 * width), F32),
            shaped((2, width), F32),
        ),
        in_specs=[SMEM, a_spec, b_spec, a_spec, b_spec],
        out_specs=(
            pl.BlockSpec((width, width), lambda i: (0, i)),
            pl.BlockSpec((width, width), lambda i: (i, 0)),
            pl.BlockSpec((2, 64, 3 * width), lambda i: (0, i, 0)),
            pl.BlockSpec((2, 64, width), lambda i: (0, i, 0)),
        )
        + tuple(
            pl.BlockSpec(shape, lambda i: (0, 0))
            for shape in ((2, width), (2, width), (1, 3 * width), (1, 4 * width), (2, width))
        ),
        scratch_shapes=[pltpu.VMEM((2, 16, width // 2), F32)],
        compiler_params=pltpu.CompilerParams(vmem_limit_bytes=32 * MIB),
        cost_estimate=pl.CostEstimate(flops=0, bytes_accessed=1024, transcendentals=0),
        name="out",
    )(core_word, a, b, other_a, other_b)
    qkv, proj = qkv.reshape(width, 3 * width), proj.reshape(width, width)
    return (
        result.reshape(1, micros, span, width),
        ghidden.reshape(1, micros, span, width),
        gain[None],
        shift[None],
        qkv[None],
        bias_qkv,
        proj[None],
        up[None],
        bias_up,
        down[None],
        branch[None],
    )


def solution(mesh):
    axes = ("section", "dp", "xl", "z", "core")
    fine = Mesh(mesh.devices.reshape(2, 4, 2, 4, 2), axes)
    spread = P(None, ("dp", "xl", "z", "core"), None)
    three, two = P("section", None, None), P("section", None)
    kept = P("section", None, ("dp", "xl", "z", "core"), None)
    in_specs = (
        spread, P("dp", None, None), three, three, three, two, three, three, two, three, three, spread,
    )
    out_specs = (kept, kept, three, three, three, two, three, three, two, three, three)
    return jax.shard_map(
        per_device, mesh=fine, in_specs=in_specs, out_specs=out_specs, check_vma=False
    )
```

```python
from functools import partial
import math

import jax
import jax.numpy as jnp
from jax import lax
from jax.experimental import pallas as pl
from jax.experimental.pallas import tpu as pltpu
from jax.sharding import Mesh, PartitionSpec as P

HEADS = 8
EPS = 1e-05
F32 = jnp.float32
BF16 = jnp.bfloat16
XZ = ("xl", "z")
LOG2E = math.log2(math.e)
SPAN = 128
HEAD = 64
TILE = 256
SCALE = 1.0 / math.sqrt(HEAD)
LAST = 32
EARLY = 144
HALF = 112


def dot(a, b, dims):
    return lax.dot_general(a, b, (dims, ((), ())), preferred_element_type=F32)


NN = ((1,), (0,))
NT = ((1,), (1,))
TN = ((0,), (0,))


def lanes_of(ref, block, at, lanes):
    return jnp.concatenate(
        [ref[2 * block, at : at + HEAD, lanes], ref[2 * block + 1, at : at + HEAD, lanes]], axis=1
    )


def both_of(mine_ref, other_ref, pair, at, lanes):
    return jnp.concatenate(
        [lanes_of(mine_ref, pair, at, lanes), lanes_of(other_ref, pair, at, lanes)], 1
    )


def lanes_at(micro):
    return pl.ds(pl.multiple_of(micro * SPAN, SPAN), SPAN)


def key_offsets():
    row = lax.broadcasted_iota(jnp.int32, (TILE, TILE), 0)
    return row + jnp.where(row >= SPAN, SPAN, 0)


def allowed_in(offsets, low, high, chunk, core, tile):
    side = core if chunk % 2 == 0 else 1 - core
    base = (chunk // 2) * (2 * TILE) + side * SPAN
    seen = offsets >= low - base
    if chunk // 2 == tile:
        seen = seen & (offsets <= high - base)
    return seen


def attend_kernel(core_ref, mine_ref, other_ref, low_ref, high_ref, out_ref, lse_ref, keys, scores):
    core = core_ref[0]
    offsets = key_offsets()

    def one_micro(micro, carry):
        lanes = lanes_at(micro)
        for chunk in range(8):
            ref, at = (mine_ref if chunk % 2 == 0 else other_ref), HEAD
            keys[chunk * TILE : (chunk + 1) * TILE, :] = lanes_of(ref, chunk // 2, at, lanes).T
        for tile in range(4):
            row = pl.ds(micro * 4 + tile, 1)
            low, high = low_ref[row, :], high_ref[row, :]
            query = lanes_of(mine_ref, tile, 0, lanes)
            top = jnp.full((8, TILE), -1e30, F32)
            for chunk in range(2 * tile + 2):
                rows = slice(chunk * TILE, (chunk + 1) * TILE)
                raw = dot(keys[rows, :], query, NN) * (SCALE * LOG2E)
                raw = jnp.where(allowed_in(offsets, low, high, chunk, core, tile), raw, -1e30)
                scores[rows, :] = raw
                top = jnp.maximum(top, jnp.max(raw.reshape(-1, 8, TILE), axis=0))
            top = jnp.max(top, axis=0, keepdims=True)
            total = jnp.zeros((8, TILE), F32)
            heard = jnp.zeros((HEAD, TILE), F32)
            for pair in range(tile + 1):
                rows = slice(2 * pair * TILE, 2 * (pair + 1) * TILE)
                weight = jnp.exp2(scores[rows, :] - top)
                total = total + jnp.sum(weight.reshape(-1, 8, TILE), axis=0)
                value = both_of(mine_ref, other_ref, pair, 2 * HEAD, lanes)
                heard = heard + dot(value, weight.astype(BF16), NN)
            total = jnp.sum(total, axis=0, keepdims=True)
            heard = (heard / total).astype(BF16)
            out_ref[2 * tile, :, lanes] = heard[:, :SPAN]
            out_ref[2 * tile + 1, :, lanes] = heard[:, SPAN:]
            lse_ref[row, :] = top + jnp.log2(total)
        return carry

    lax.fori_loop(0, 2, one_micro, 0)


def attend_back_kernel(
    core_ref,
    mine_ref,
    other_ref,
    low_ref,
    high_ref,
    out_ref,
    lse_ref,
    grad_ref,
    gmine_ref,
    gother_ref,
    keys,
    values,
    gkeys,
    gvalues,
):
    core = core_ref[0]
    offsets = key_offsets()

    def one_micro(micro, carry):
        lanes = lanes_at(micro)
        for chunk in range(8):
            rows = slice(chunk * TILE, (chunk + 1) * TILE)
            ref, at = (mine_ref if chunk % 2 == 0 else other_ref), HEAD
            keys[rows, :] = lanes_of(ref, chunk // 2, at, lanes).T
            values[rows, :] = lanes_of(ref, chunk // 2, at + HEAD, lanes).T
        for tile in range(4):
            row = pl.ds(micro * 4 + tile, 1)
            low, high, lse = low_ref[row, :], high_ref[row, :], lse_ref[row, :]
            query = lanes_of(mine_ref, tile, 0, lanes)
            grad = lanes_of(grad_ref, tile, 0, lanes)
            heard = lanes_of(out_ref, tile, 0, lanes)
            centre = jnp.sum(grad.astype(F32) * heard.astype(F32), axis=0, keepdims=True)
            gquery = jnp.zeros((HEAD, TILE), F32)
            for pair in range(tile + 1):
                rows = slice(2 * pair * TILE, 2 * (pair + 1) * TILE)
                raw = dot(keys[rows, :], query, NN) * (SCALE * LOG2E) - lse
                raws = [
                    jnp.where(
                        allowed_in(offsets, low, high, 2 * pair + side, core, tile),
                        raw[side * TILE : (side + 1) * TILE],
                        -1e30,
                    )
                    for side in range(2)
                ]
                prob = jnp.exp2(jnp.concatenate(raws, 0))
                gprob = dot(values[rows, :], grad, NN)
                gscore = (prob * (gprob - centre)).astype(BF16)
                gquery = gquery + dot(both_of(mine_ref, other_ref, pair, HEAD, lanes), gscore, NN)
                gkey = dot(query, gscore, NT)
                gvalue = dot(grad, prob.astype(BF16), NT)
                if pair == tile:
                    gkeys[:, rows], gvalues[:, rows] = gkey, gvalue
                else:
                    gkeys[:, rows] += gkey
                    gvalues[:, rows] += gvalue
            gquery = (gquery * SCALE).astype(BF16)
            gmine_ref[2 * tile, :HEAD, lanes] = gquery[:, :SPAN]
            gmine_ref[2 * tile + 1, :HEAD, lanes] = gquery[:, SPAN:]
        for chunk in range(8):
            ref, at = (gmine_ref, HEAD) if chunk % 2 == 0 else (gother_ref, 0)
            for half in range(2):
                cols = slice(chunk * TILE + half * SPAN, chunk * TILE + (half + 1) * SPAN)
                block = 2 * (chunk // 2) + half
                ref[block, at : at + HEAD, lanes] = (gkeys[:, cols] * SCALE).astype(BF16)
                ref[block, at + HEAD : at + 2 * HEAD, lanes] = gvalues[:, cols].astype(BF16)
        return carry

    lax.fori_loop(0, 2, one_micro, 0)


def front_kernel(
    start_ref, length_ref, hidden_ref, gain_ref, shift_ref, weight_ref, bias_ref, tiles_ref, second_ref, *copies
):
    rows, width = hidden_ref.shape
    lane = lax.broadcasted_iota(jnp.int32, (8, rows), 1)
    later = lane >= SPAN
    row = start_ref[0] + lane - jnp.where(later, SPAN, 0)
    first, second = [jnp.where(later, length_ref[0, 1, i], length_ref[0, 0, i]) for i in range(2)]
    begin = jnp.where(row >= first, first, 0) + jnp.where(row >= first + second, second, 0)
    order = lax.broadcasted_iota(jnp.int32, (8, rows), 0).astype(F32)
    ladder = jnp.exp(-math.log(10000.0) * (order * (2.0 / 16)))
    angle = ladder * (row - begin).astype(F32)
    cosine, sine = jnp.cos(angle), jnp.sin(angle)
    gain, shift = gain_ref[0].astype(F32), shift_ref[0].astype(F32)
    bias = bias_ref[...].astype(F32)
    xhat, _ = normed_of(hidden_ref[...].astype(F32))
    first = (xhat * gain[0:1] + shift[0:1]).astype(BF16)
    for copies_ref in copies:
        for block in range(copies_ref.shape[0]):
            copies_ref[block] = first
    second_ref[...] = (xhat * gain[1:2] + shift[1:2]).astype(BF16)
    for part in range(3):
        cols = slice(part * width, (part + 1) * width)
        made = (dot(first, weight_ref[:, cols], NN) + bias[:, cols]).T
        for head in range(HEADS):
            tile = made[head * HEAD : (head + 1) * HEAD]
            if part < 2:
                tile = turned(tile, cosine, sine)
            tiles_ref[head, part * HEAD : (part + 1) * HEAD, :] = tile.astype(BF16)


def back_kernel(
    core_ref, back_ref, hidden_ref, grad_ref, gsecond_ref, gain_ref, weight_ref, *refs
):
    early_refs = refs[: len(refs) - 2 if len(refs) == 2 else 1]
    ghidden_ref, *vector_refs, gqkv = refs[len(early_refs) :]
    width = hidden_ref.shape[1]
    rows = hidden_ref.shape[0]
    gfirst = jnp.zeros((rows, width), F32)
    ones = jnp.ones((8, rows), BF16)
    biases, gains, shifts = [], [], []
    for part in range(3):
        cols = slice(part * width, (part + 1) * width)
        for head in range(HEADS):
            gqkv[head * HEAD : (head + 1) * HEAD, :] = back_ref[head, part * HEAD : (part + 1) * HEAD, :]
        made = gqkv[...]
        gfirst = gfirst + dot(made.T, weight_ref[:, cols], NT)
        biases.append(dot(ones, made, NT)[:1])
    xhat, inv = normed_of(hidden_ref[...].astype(F32))
    gsecond = gsecond_ref[...]
    total = grad_ref[...].astype(F32)
    for which, grad in ((0, gfirst), (1, gsecond)):
        e = grad * gain_ref[which : which + 1, :]
        total = total + inv * (
            e - jnp.mean(e, -1, keepdims=True) - xhat * jnp.mean(e * xhat, -1, keepdims=True)
        )
        gains.append(jnp.sum(grad * xhat, 0, keepdims=True))
        shifts.append(jnp.sum(grad, 0, keepdims=True))
    ghidden_ref[...] = total.astype(BF16)
    if not vector_refs:
        return
    early = jnp.sum(early_refs[0][...], 0, keepdims=True)
    wide = gains + shifts + biases + [early[:, i * width : (i + 1) * width] for i in range(5)]
    lines = [v[:, half * width // 2 : (half + 1) * width // 2] for v in wide for half in range(2)]
    blank = [jnp.zeros((4, width // 2), F32)]
    first = jnp.concatenate(lines[:12] + blank, 0).astype(BF16)
    last = jnp.concatenate(lines[12:] + blank, 0).astype(BF16)
    ours_ref, theirs_ref = vector_refs
    ours_ref[...] = jnp.where(core_ref[0] == 0, first, last)
    theirs_ref[...] = jnp.where(core_ref[0] == 0, last, first)


def join_kernel(mine_ref, other_ref, cos_ref, sin_ref, *refs):
    out_ref = refs[-1]
    for block in range(8):
        if len(refs) > 1:
            out_ref[block, 3 * HEAD :, :] = refs[0][block]
        cosine, sine = cos_ref[block], -sin_ref[block]
        for part in range(3):
            rows = slice(part * HEAD, (part + 1) * HEAD)
            tile = mine_ref[block, rows, :].astype(F32)
            if part > 0:
                at = (part - 1) * HEAD
                tile = tile + other_ref[block, at : at + HEAD, :].astype(F32)
            if part < 2:
                tile = turned(tile, cosine, sine)
            out_ref[block, rows, :] = tile.astype(BF16)


def grad_kernel(section_ref, received_ref, own_ref, weight_ref, grad_ref, heard_ref):
    grad = jnp.where(section_ref[0] == 1, own_ref[...], received_ref[...])
    grad_ref[...] = grad
    made = dot(weight_ref[...], grad, NT).astype(BF16)
    for head in range(HEADS):
        heard_ref[head] = made[head * HEAD : (head + 1) * HEAD]


def early_terms_kernel(
    core_ref,
    second_ref,
    slope_ref,
    active_ref,
    grad_ref,
    heard_ref,
    down_ref,
    gup_ref,
    ours_ref,
    theirs_ref,
    sums_ref,
):
    core = core_ref[0]
    width = second_ref.shape[1]
    turned_second = second_ref[...].T
    grad = grad_ref[...]
    proj = dot(heard_ref[...], grad, NN).astype(BF16)
    sums_ref[:, 4 * width :] = jnp.sum(grad.astype(F32).reshape(-1, 8, width), 0)
    for block in range(4):
        cols = slice(block * width, (block + 1) * width)
        gup = (dot(grad, down_ref[cols, :], NT) * slope_ref[:, cols].astype(F32)).astype(BF16)
        gup_ref[:, cols] = gup
        sums_ref[:, cols] = jnp.sum(gup.astype(F32).reshape(-1, 8, width), 0)
        up = dot(turned_second, gup, NN).astype(BF16)
        down = dot(active_ref[:, cols].T, grad, NN).astype(BF16)
        first = proj[block * 64 : (block + 1) * 64]
        last = proj[256 + block * 64 : 256 + (block + 1) * 64]
        ours_ref[block, :width, :] = jnp.where(core == 0, up, down)
        theirs_ref[block, :width, :] = jnp.where(core == 0, down, up)
        ours_ref[block, width:, :] = jnp.where(core == 0, first, last)
        theirs_ref[block, width:, :] = jnp.where(core == 0, last, first)


def second_grad_kernel(gup_ref, up_ref, gsecond_ref):
    gsecond_ref[...] = dot(gup_ref[...], up_ref[...], NT)


def late_terms_kernel(core_ref, gqkv_ref, first_ref, ours_ref, theirs_ref):
    core = core_ref[0]
    total = jnp.zeros((3 * HEAD, first_ref.shape[2]), F32)
    for block in range(8):
        total = total + dot(gqkv_ref[block], first_ref[block], NN)
    total = jnp.concatenate([total, jnp.zeros((HEAD, total.shape[1]), F32)], 0).T
    half = total.shape[0] // 2
    upper, lower = total[:half].astype(BF16), total[half:].astype(BF16)
    ours_ref[...] = jnp.where(core == 0, upper, lower)
    theirs_ref[...] = jnp.where(core == 0, lower, upper)


def place_ring_kernel(at_ref, *refs):
    at = at_ref[0]
    for sources, target in ((refs[:5], refs[10]), (refs[5:10], refs[11])):
        own, back, ahead, far_a, far_b = sources
        extent, half = own.shape[0], far_a.shape[0]
        for step, source in ((0, own), (3, back), (1, ahead)):
            start = pl.multiple_of(lax.rem(at + step, 4) * extent, 16)
            target[pl.ds(start, extent), :] = source[...]
        start = lax.rem(at + 2, 4) * extent
        target[pl.ds(pl.multiple_of(start, 16), half), :] = far_a[...]
        target[pl.ds(pl.multiple_of(start + half, 16), half), :] = far_b[...]


def split_kernel(count, pieces, at_ref, *refs):
    sources, targets = refs[:count], refs[count:]
    extent = targets[0].shape[0]
    at = at_ref[0]
    for step in range(pieces):
        start = pl.multiple_of(lax.rem(at + step, pieces) * extent, extent)
        total = sources[0][pl.ds(start, extent), :].astype(F32)
        for source in sources[1:]:
            total = total + source[pl.ds(start, extent), :].astype(F32)
        targets[step][...] = total.astype(BF16)


def ring_kernel(at_ref, first_ref, last_ref, own_ref, next_ref, back_ref, far_a_ref, far_b_ref):
    at = at_ref[0]
    extent = own_ref.shape[0]

    def piece(step):
        rows = pl.ds(pl.multiple_of(lax.rem(at + step, 4) * extent, 16), extent)
        return (first_ref[rows, :].astype(F32) + last_ref[rows, :].astype(F32)).astype(BF16)

    own_ref[...] = piece(0)
    next_ref[...] = piece(1)
    back_ref[...] = piece(3)
    far = piece(2)
    far_a_ref[...] = far[: extent // 2]
    far_b_ref[...] = far[extent // 2 :]


def fold_kernel(next_ref, back_ref, far_a_ref, far_b_ref, to_next_ref, to_back_ref):
    half = far_a_ref.shape[0]
    total = next_ref[:half].astype(F32) + far_a_ref[...].astype(F32)
    to_next_ref[:half] = total.astype(BF16)
    to_next_ref[half:] = next_ref[half:]
    to_back_ref[:half] = back_ref[:half]
    total = back_ref[half:].astype(F32) + far_b_ref[...].astype(F32)
    to_back_ref[half:] = total.astype(BF16)


def split_both_kernel(z_ref, dp_ref, *refs):
    split_kernel(3, 4, z_ref, *refs[:3], *refs[5:9])
    split_kernel(2, 4, dp_ref, *refs[3:5], *refs[9:])


def place_kernel(at_ref, *refs):
    sources, target = refs[:-1], refs[-1]
    count, extent, at = len(sources), sources[0].shape[0], at_ref[0]
    for step, source in enumerate(sources):
        start = pl.multiple_of(lax.rem(at + count - step, count) * extent, extent)
        target[pl.ds(start, extent), :] = source[...]


def share_kernel(*refs):
    early, late, small, out_ref = refs[:4], refs[4:8], refs[8:10], refs[10]

    def total(sources):
        made = sources[0][...].astype(F32)
        for source in sources[1:]:
            made = made + source[...].astype(F32)
        return made.astype(BF16)

    made = total(early)
    rows, half = made.shape[0], made.shape[1] // 2
    out_ref[:rows, :] = made[:, :half]
    out_ref[rows : 2 * rows, :] = made[:, half:]
    out_ref[2 * rows : 2 * rows + HEAD, :] = total(late)
    out_ref[2 * rows + HEAD :, :] = total(small)


def out_kernel(
    core_ref,
    a_ref,
    b_ref,
    other_a_ref,
    other_b_ref,
    up_ref,
    down_ref,
    qkv_ref,
    proj_ref,
    gain_ref,
    shift_ref,
    qkv_bias_ref,
    up_bias_ref,
    branch_ref,
    vectors,
):
    core = core_ref[0]
    width = down_ref.shape[1]

    def parts(first_ref, second_ref):
        early, late = [], []
        for z in range(4):
            first = jnp.concatenate([first_ref[0, z, 0], first_ref[0, z, 1]], 1)
            second = jnp.concatenate([second_ref[z, 0, 0, :LAST], second_ref[z, 0, 1, :LAST]], 1)
            early += [first, second]
        for half in range(2):
            late += [second_ref[z, 0, half, LAST : LAST + HEAD] for z in range(4)]
        return jnp.concatenate(early, 0).astype(F32), [v.astype(F32) for v in late]

    mine, late = parts(a_ref, b_ref)
    other, other_late = parts(other_a_ref, other_b_ref)
    low, high = jnp.where(core == 0, mine, other), jnp.where(core == 0, other, mine)
    up_ref[...] = low[:width]
    down_ref[...] = high[:width]
    proj_ref[0] = low[width:]
    proj_ref[1] = high[width:]
    for head in range(HEADS):
        low = jnp.where(core == 0, late[head], other_late[head])
        high = jnp.where(core == 0, other_late[head], late[head])
        for part in range(3):
            at = part * width + head * HEAD
            qkv_ref[0, :, at : at + HEAD] = low[:, part * HEAD : (part + 1) * HEAD]
            qkv_ref[1, :, at : at + HEAD] = high[:, part * HEAD : (part + 1) * HEAD]
    step = pl.program_id(0)

    def vector_sum(ref):
        return sum(ref[z, 0, half, LAST + HEAD :].astype(F32) for z in range(4) for half in range(2))

    low, high = vector_sum(b_ref), vector_sum(other_b_ref)

    @pl.when(step == 0)
    def _():
        vectors[0], vectors[1] = low, high

    @pl.when(step > 0)
    def _():
        vectors[0] += low
        vectors[1] += high

    @pl.when(step == 3)
    def _():
        mine, other = vectors[0], vectors[1]
        first = jnp.where(core == 0, mine, other)
        last = jnp.where(core == 0, other, mine)
        lines = [first[i : i + 1] for i in range(12)] + [last[i : i + 1] for i in range(12)]
        wide = [jnp.concatenate(lines[2 * i : 2 * i + 2], 1) for i in range(12)]
        for row in range(2):
            gain_ref[row : row + 1, :] = wide[row]
            shift_ref[row : row + 1, :] = wide[2 + row]
            branch_ref[row : row + 1, :] = wide[11]
        qkv_bias_ref[...] = jnp.concatenate(wide[4:7], 1)
        up_bias_ref[...] = jnp.concatenate(wide[7:11], 1)


def halves_kernel(at_ref, mine_ref, other_ref, a_ref, b_ref):
    at = at_ref[0]
    early = EARLY
    total = mine_ref[: 2 * early].astype(F32) + other_ref[: 2 * early].astype(F32)
    total = total.astype(BF16)
    for half in range(2):
        a_ref[half * HALF : (half + 1) * HALF] = total[half * early : half * early + HALF]
        b_ref[half * HALF : half * HALF + LAST] = total[half * early + HALF : (half + 1) * early]
    for source, to in ((mine_ref, at), (other_ref, 1 - at)):
        rows = pl.ds(pl.multiple_of(to * HALF + LAST, 16), HALF - LAST)
        b_ref[rows, :] = source[2 * early :, :]


VMEM = pl.BlockSpec(memory_space=pltpu.VMEM)
SMEM = pl.BlockSpec(memory_space=pltpu.SMEM)
MIB = 1024 * 1024


def shaped(shape, dtype):
    return jax.ShapeDtypeStruct(shape, dtype)


def call(kernel, outs, *args, words=0, limit=12, scratch=(), name=None):
    single = not isinstance(outs, tuple)
    shapes = (outs,) if single else outs
    made = pl.pallas_call(
        kernel,
        out_shape=shapes,
        in_specs=[SMEM] * words + [VMEM] * (len(args) - words),
        out_specs=tuple(VMEM for _ in shapes),
        scratch_shapes=list(scratch),
        compiler_params=pltpu.CompilerParams(vmem_limit_bytes=limit * MIB),
        cost_estimate=pl.CostEstimate(flops=0, bytes_accessed=1024, transcendentals=0),
        name=name,
    )(*args)
    return made[0] if single else made


def attend(core, mine, other, low, high):
    return call(
        attend_kernel,
        (shaped((8, HEAD, 2 * SPAN), BF16), shaped((8, TILE), F32)),
        core, mine, other, low, high,
        words=1, limit=10,
        scratch=[pltpu.VMEM((2048, HEAD), BF16), pltpu.VMEM((2048, TILE), F32)],
        name="attend",
    )


def attend_back(core, mine, other, low, high, out, lse, grad):
    return call(
        attend_back_kernel,
        (shaped((8, 3 * HEAD, 2 * SPAN), BF16), shaped((8, 2 * HEAD, 2 * SPAN), BF16)),
        core, mine, other, low, high, out, lse, grad,
        words=1, limit=10,
        scratch=[
            pltpu.VMEM((2048, HEAD), BF16),
            pltpu.VMEM((2048, HEAD), BF16),
            pltpu.VMEM((HEAD, 2048), F32),
            pltpu.VMEM((HEAD, 2048), F32),
        ],
        name="attend_back",
    )


def swap(array, axis):
    return lax.ppermute(array, axis, [(0, 1), (1, 0)])


def word(value):
    return value.astype(jnp.int32).reshape(1)


def spread_from(pieces, axis):
    count = len(pieces)
    return [pieces[0]] + [
        lax.ppermute(pieces[s], axis, [(i, (i + s) % count) for i in range(count)])
        for s in range(1, count)
    ]


def turn(array, axis, by):
    count = lax.axis_size(axis)
    return lax.ppermute(array, axis, [(i, (i + by) % count) for i in range(count)])


def placed(pieces, axis):
    extent, width = pieces[0].shape
    return call(
        place_kernel, shaped((len(pieces) * extent, width), BF16),
        word(lax.axis_index(axis)), *pieces,
        words=1, limit=8, name="place",
    )


def normed_of(hidden):
    centred = hidden - jnp.mean(hidden, -1, keepdims=True)
    inv = lax.rsqrt(jnp.mean(centred * centred, -1, keepdims=True) + EPS)
    return centred * inv, inv


def turned(tile, cosine, sine):
    first, second = tile[:8], tile[8:16]
    return jnp.concatenate(
        [first * cosine - second * sine, second * cosine + first * sine, tile[16:]], 0
    )


def per_device(
    inputs,
    lengths,
    norm_gain,
    norm_bias,
    qkv_weight,
    qkv_bias,
    proj_weight,
    up_weight,
    up_bias,
    down_weight,
    branch_bias,
    cotangent,
):
    section = lax.axis_index("section")
    core = lax.axis_index("core")
    block = lax.axis_index(XZ)
    micros, span, width = inputs.shape
    rows = micros * span
    gains = norm_gain[0].astype(F32)
    w_qkv, w_proj, w_up, w_down = qkv_weight[0], proj_weight[0], up_weight[0], down_weight[0]
    b_up = up_bias[0].astype(F32)
    b_branch = jnp.sum(branch_bias[0].astype(F32), 0)
    core_word = word(core)

    def front(hidden, copies):
        tiles, second, *firsts = call(
            front_kernel,
            (shaped((HEADS, 3 * HEAD, rows), BF16), shaped((rows, width), BF16))
            + (shaped((HEADS, rows, width), BF16),) * copies,
            word((2 * block + core) * span), lengths, hidden, norm_gain, norm_bias, w_qkv, qkv_bias,
            words=2, limit=12 if copies else 56, name="front",
        )
        return firsts, second, tiles

    entry = inputs.reshape(rows, width)
    first_front = front(entry, 0)
    tiles, lengths = lax.optimization_barrier((first_front[-1], lengths))
    first_front = first_front[:-1] + (tiles,)
    one, two, three = [lengths[0][:, i] for i in range(3)]
    ends = jnp.stack([one, one + two, one + two + three], -1)

    def begin_of(row):
        after = row[None, :, None] >= ends[:, None, :]
        return jnp.sum(jnp.where(after, lengths[0][:, None, :], 0), -1)

    heard_rows = (
        (2 * jnp.arange(8, dtype=jnp.int32)[:, None] + core) * span
        + jnp.arange(span, dtype=jnp.int32)[None]
    ).reshape(-1)
    low = begin_of(heard_rows).reshape(8, TILE)
    high = jnp.broadcast_to(heard_rows[None], (micros, 8 * span)).reshape(8, TILE)
    ladder = jnp.exp(-math.log(10000.0) * (jnp.arange(8, dtype=F32) * (2.0 / 16)))
    heard_position = (heard_rows[None] - begin_of(heard_rows)).reshape(micros, 8, span)
    heard_position = jnp.moveaxis(heard_position, 0, 1).reshape(8, 1, rows).astype(F32)
    heard_angle = ladder[None, :, None] * heard_position
    heard_cosine, heard_sine = jnp.cos(heard_angle), jnp.sin(heard_angle)

    def mlp_of(second):
        up = dot(second, w_up, NN) + b_up
        phi = 0.5 * (1.0 + lax.erf(up * (1.0 / math.sqrt(2.0))))
        bell = jnp.exp(-0.5 * up * up) * (1.0 / math.sqrt(2.0 * math.pi))
        active = (up * phi).astype(BF16)
        slope = (phi + up * bell).astype(BF16)
        return active, slope

    def forward(hidden, firsts, second, tiles):
        mine = lax.all_to_all(tiles, XZ, 0, 0, tiled=True)
        other = swap(mine, "core")
        active, slope = mlp_of(second)
        base = hidden.astype(F32) + dot(active, w_down, NN) + b_branch
        heard, lse = attend(core_word, mine, other, low, high)
        return base, firsts, second, mine, other, active, slope, heard, lse

    def finish(base, heard_rows):
        return (base + dot(heard_rows, w_proj, TN)).astype(BF16)

    def heard_grad(received, own):
        grad_in, ggo = call(
            grad_kernel,
            (shaped((rows, width), BF16), shaped((HEADS, HEAD, rows), BF16)),
            word(section), received, own, w_proj,
            words=1, name="grad",
        )
        return grad_in, lax.all_to_all(ggo, XZ, 0, 0, tiled=True)

    def joined(gmine, gother, *along):
        return call(
            join_kernel, shaped((HEADS, (3 + len(along)) * HEAD, rows), BF16),
            gmine, swap(gother, "core"), heard_cosine, heard_sine, *along, name="join",
        )

    def rows_back(back, hidden, grad_in, gsecond, *early_sums):
        vectors = (shaped((16, width // 2), BF16),) * 2 if early_sums else ()
        return call(
            back_kernel,
            (shaped((rows, width), BF16),) + vectors,
            core_word, back, hidden, grad_in, gsecond, gains, w_qkv, *early_sums,
            words=1, scratch=[pltpu.VMEM((width, rows), BF16)], limit=56, name="back",
        )

    def mlp_back(grad_in, slope):
        gup = (dot(grad_in, w_down, NT) * slope.astype(F32)).astype(BF16)
        return gup, dot(gup, w_up, NT)

    loss_grad = cotangent.reshape(rows, width)
    grad_in, ggo = heard_grad(loss_grad, loss_grad)
    base, *_, heard, _ = forward(entry, *first_front)
    heard, ggo = lax.optimization_barrier((heard, ggo))
    heard_rows = lax.all_to_all(heard, XZ, 0, 0, tiled=True).reshape(width, rows)
    heard_rows, base = lax.optimization_barrier((heard_rows, base))
    sent = finish(base, heard_rows)
    received = lax.ppermute(sent, "section", [(0, 1)])
    entry = jnp.where(section == 1, received, entry)
    base, (firsts,), second, mine, other, active, slope, heard, lse = forward(entry, *front(entry, 1))
    mine, firsts = lax.optimization_barrier((mine, firsts))
    first_all = lax.all_to_all(firsts, XZ, 0, 0, tiled=True)
    _, gsecond = mlp_back(grad_in, slope)
    gmine, gother = attend_back(core_word, mine, other, low, high, heard, lse, ggo)
    gother, first_all = lax.optimization_barrier((gother, first_all))
    back = lax.all_to_all(joined(gmine, gother, heard), XZ, 0, 0, tiled=True)
    (sent_back,) = rows_back(back, entry, grad_in, gsecond)
    received = lax.ppermute(sent_back, "section", [(1, 0)])
    heard_rows = back[:, 3 * HEAD :].reshape(width, rows)
    result = finish(base, heard_rows)
    received, result, heard_rows = lax.optimization_barrier((received, result, heard_rows))
    grad_in, ggo = heard_grad(received, loss_grad)
    gup, *early, early_sums = call(
        early_terms_kernel,
        (shaped((rows, 4 * width), BF16),)
        + (shaped((4, width + 64, width), BF16),) * 2
        + (shaped((8, 5 * width), F32),),
        core_word, second, slope, active, grad_in, heard_rows, w_down,
        words=1, limit=56, name="early_terms",
    )
    ggo, early = lax.optimization_barrier((ggo, early))
    early = [v.reshape(-1, width) for v in early]
    whole, part = shaped((4 * EARLY, width), BF16), shaped((2 * EARLY, width), BF16)
    pieces = call(
        ring_kernel, (whole, whole, whole, part, part),
        word(lax.axis_index("dp")), early[0], swap(early[1], "core"),
        words=1, limit=56, name="ring",
    )
    ggo, pieces = lax.optimization_barrier((ggo, pieces))
    own, to_next, to_back, far_a, far_b = pieces
    far_a, far_b = turn(far_a, "dp", 1), turn(far_b, "dp", -1)
    gmine, gother = attend_back(core_word, mine, other, low, high, heard, lse, ggo)
    gmine, gother, far_a, far_b = lax.optimization_barrier((gmine, gother, far_a, far_b))
    to_next, to_back = call(fold_kernel, (whole, whole), to_next, to_back, far_a, far_b, name="fold")
    gmine = joined(gmine, gother)
    gmine, to_next, to_back = lax.optimization_barrier((gmine, to_next, to_back))
    pieces = [own, turn(to_next, "dp", 1), turn(to_back, "dp", -1)]
    late = call(
        late_terms_kernel,
        (shaped((width // 2, width // 2), BF16),) * 2,
        core_word, gmine, first_all,
        words=1, limit=56, name="late_terms",
    )
    gsecond = call(second_grad_kernel, shaped((rows, width), F32), gup, w_up, name="second_grad")
    back = lax.all_to_all(gmine, XZ, 0, 0, tiled=True)
    pieces, late, gsecond = lax.optimization_barrier((pieces, late, gsecond))
    made = call(
        split_both_kernel,
        (shaped((EARLY, width), BF16),) * 4 + (shaped((HEAD, width // 2), BF16),) * 4,
        word(lax.axis_index("z")), word(lax.axis_index("dp")),
        *pieces, late[0], swap(late[1], "core"),
        words=2, limit=56, name="split_both",
    )
    pieces, late = spread_from(made[:4], "z"), spread_from(made[4:], "dp")
    back, pieces = lax.optimization_barrier((back, pieces))
    ghidden, *small = rows_back(back, entry, grad_in, gsecond, early_sums)
    share = call(
        share_kernel, shaped((2 * EARLY + HEAD + 16, width // 2), BF16),
        *pieces, *late, small[0], swap(small[1], "core"), name="share",
    )
    share, ghidden = lax.optimization_barrier((share, ghidden))

    a, b = call(
        halves_kernel,
        (shaped((2 * HALF, width // 2), BF16),) * 2,
        word(lax.axis_index("xl")), share, swap(share, "xl"),
        words=1, limit=8, name="halves",
    )
    a_pieces, b_pieces = spread_from([a] * 4, "z"), spread_from([b] * 4, "dp")
    a_pieces, b_pieces = lax.optimization_barrier((a_pieces, b_pieces))
    a, b = lax.optimization_barrier((placed(a_pieces, "z"), placed(b_pieces, "dp")))
    gathers = []
    for array, axis in ((a, "dp"), (b, "z")):
        back, ahead = turn(array, axis, 1), turn(array, axis, -1)
        half = array.shape[0] // 2
        far_a, far_b = turn(back[:half], axis, 1), turn(ahead[half:], axis, -1)
        gathers.append([array, back, ahead, far_a, far_b])
    gathers = [g + [swap(v, "core") for v in g] for g in gathers]
    gathers = lax.optimization_barrier(gathers)
    placed_all = [
        call(
            place_ring_kernel, (shaped((4 * g[0].shape[0], width // 2), BF16),) * 2,
            word(lax.axis_index(axis)), *g, words=1, limit=12, name="place_ring",
        )
        for g, axis in zip(gathers, ("dp", "z"))
    ]
    (a, other_a), (b, other_b) = placed_all
    a_spec = pl.BlockSpec((1, 4, 2, HALF, width // 2), lambda i: (i, 0, 0, 0, 0))
    b_spec = pl.BlockSpec((4, 1, 2, HALF, width // 2), lambda i: (0, i, 0, 0, 0))
    a, other_a, b, other_b = [v.reshape(4, 4, 2, HALF, width // 2) for v in (a, other_a, b, other_b)]
    up, down, qkv, proj, gain, shift, bias_qkv, bias_up, branch = pl.pallas_call(
        out_kernel,
        grid=(4,),
        out_shape=(
            shaped((width, 4 * width), F32),
            shaped((4 * width, width), F32),
            shaped((2, width // 2, 3 * width), F32),
            shaped((2, width // 2, width), F32),
            shaped((2, width), F32),
            shaped((2, width), F32),
            shaped((1, 3 * width), F32),
            shaped((1, 4 * width), F32),
            shaped((2, width), F32),
        ),
        in_specs=[SMEM, a_spec, b_spec, a_spec, b_spec],
        out_specs=(
            pl.BlockSpec((width, width), lambda i: (0, i)),
            pl.BlockSpec((width, width), lambda i: (i, 0)),
            pl.BlockSpec((2, 64, 3 * width), lambda i: (0, i, 0)),
            pl.BlockSpec((2, 64, width), lambda i: (0, i, 0)),
        )
        + tuple(
            pl.BlockSpec(shape, lambda i: (0, 0))
            for shape in ((2, width), (2, width), (1, 3 * width), (1, 4 * width), (2, width))
        ),
        scratch_shapes=[pltpu.VMEM((2, 16, width // 2), F32)],
        compiler_params=pltpu.CompilerParams(vmem_limit_bytes=32 * MIB),
        cost_estimate=pl.CostEstimate(flops=0, bytes_accessed=1024, transcendentals=0),
        name="out",
    )(core_word, a, b, other_a, other_b)
    qkv, proj = qkv.reshape(width, 3 * width), proj.reshape(width, width)
    return (
        result.reshape(1, micros, span, width),
        ghidden.reshape(1, micros, span, width),
        gain[None],
        shift[None],
        qkv[None],
        bias_qkv,
        proj[None],
        up[None],
        bias_up,
        down[None],
        branch[None],
    )


def solution(mesh):
    axes = ("section", "dp", "xl", "z", "core")
    fine = Mesh(mesh.devices.reshape(2, 4, 2, 4, 2), axes)
    spread = P(None, ("dp", "xl", "z", "core"), None)
    three, two = P("section", None, None), P("section", None)
    kept = P("section", None, ("dp", "xl", "z", "core"), None)
    in_specs = (
        spread, P("dp", None, None), three, three, three, two, three, three, two, three, three, spread,
    )
    out_specs = (kept, kept, three, three, three, two, three, three, two, three, three)
    return jax.shard_map(
        per_device, mesh=fine, in_specs=in_specs, out_specs=out_specs, check_vma=False
    )
```

```python
from functools import partial
import math

import jax
import jax.numpy as jnp
from jax import lax
from jax.experimental import pallas as pl
from jax.experimental.pallas import tpu as pltpu
from jax.sharding import Mesh, PartitionSpec as P

HEADS = 8
EPS = 1e-05
F32 = jnp.float32
BF16 = jnp.bfloat16
XZ = ("xl", "z")
LOG2E = math.log2(math.e)
SPAN = 128
HEAD = 64
TILE = 256
SCALE = 1.0 / math.sqrt(HEAD)
LAST = 32
EARLY = 144
HALF = 112


def dot(a, b, dims):
    return lax.dot_general(a, b, (dims, ((), ())), preferred_element_type=F32)


NN = ((1,), (0,))
NT = ((1,), (1,))
TN = ((0,), (0,))


def lanes_of(ref, block, at, lanes):
    return jnp.concatenate(
        [ref[2 * block, at : at + HEAD, lanes], ref[2 * block + 1, at : at + HEAD, lanes]], axis=1
    )


def both_of(mine_ref, other_ref, pair, at, lanes):
    return jnp.concatenate(
        [lanes_of(mine_ref, pair, at, lanes), lanes_of(other_ref, pair, at, lanes)], 1
    )


def lanes_at(micro):
    return pl.ds(pl.multiple_of(micro * SPAN, SPAN), SPAN)


def key_offsets():
    row = lax.broadcasted_iota(jnp.int32, (TILE, TILE), 0)
    return row + jnp.where(row >= SPAN, SPAN, 0)


def allowed_in(offsets, low, high, chunk, core, tile):
    side = core if chunk % 2 == 0 else 1 - core
    base = (chunk // 2) * (2 * TILE) + side * SPAN
    seen = offsets >= low - base
    if chunk // 2 == tile:
        seen = seen & (offsets <= high - base)
    return seen


def attend_kernel(core_ref, mine_ref, other_ref, low_ref, high_ref, out_ref, lse_ref, keys, scores):
    core = core_ref[0]
    offsets = key_offsets()

    def one_micro(micro, carry):
        lanes = lanes_at(micro)
        for chunk in range(8):
            ref, at = (mine_ref if chunk % 2 == 0 else other_ref), HEAD
            keys[chunk * TILE : (chunk + 1) * TILE, :] = lanes_of(ref, chunk // 2, at, lanes).T
        for tile in range(4):
            row = pl.ds(micro * 4 + tile, 1)
            low, high = low_ref[row, :], high_ref[row, :]
            query = lanes_of(mine_ref, tile, 0, lanes)
            top = jnp.full((8, TILE), -1e30, F32)
            for chunk in range(2 * tile + 2):
                rows = slice(chunk * TILE, (chunk + 1) * TILE)
                raw = dot(keys[rows, :], query, NN) * (SCALE * LOG2E)
                raw = jnp.where(allowed_in(offsets, low, high, chunk, core, tile), raw, -1e30)
                scores[rows, :] = raw
                top = jnp.maximum(top, jnp.max(raw.reshape(-1, 8, TILE), axis=0))
            top = jnp.max(top, axis=0, keepdims=True)
            total = jnp.zeros((8, TILE), F32)
            heard = jnp.zeros((HEAD, TILE), F32)
            for pair in range(tile + 1):
                rows = slice(2 * pair * TILE, 2 * (pair + 1) * TILE)
                weight = jnp.exp2(scores[rows, :] - top)
                total = total + jnp.sum(weight.reshape(-1, 8, TILE), axis=0)
                value = both_of(mine_ref, other_ref, pair, 2 * HEAD, lanes)
                heard = heard + dot(value, weight.astype(BF16), NN)
            total = jnp.sum(total, axis=0, keepdims=True)
            heard = (heard / total).astype(BF16)
            out_ref[2 * tile, :, lanes] = heard[:, :SPAN]
            out_ref[2 * tile + 1, :, lanes] = heard[:, SPAN:]
            lse_ref[row, :] = top + jnp.log2(total)
        return carry

    lax.fori_loop(0, 2, one_micro, 0)


def attend_back_kernel(
    core_ref,
    mine_ref,
    other_ref,
    low_ref,
    high_ref,
    out_ref,
    lse_ref,
    grad_ref,
    gmine_ref,
    gother_ref,
    keys,
    values,
    gkeys,
    gvalues,
):
    core = core_ref[0]
    offsets = key_offsets()

    def one_micro(micro, carry):
        lanes = lanes_at(micro)
        for chunk in range(8):
            rows = slice(chunk * TILE, (chunk + 1) * TILE)
            ref, at = (mine_ref if chunk % 2 == 0 else other_ref), HEAD
            keys[rows, :] = lanes_of(ref, chunk // 2, at, lanes).T
            values[rows, :] = lanes_of(ref, chunk // 2, at + HEAD, lanes).T
        for tile in range(4):
            row = pl.ds(micro * 4 + tile, 1)
            low, high, lse = low_ref[row, :], high_ref[row, :], lse_ref[row, :]
            query = lanes_of(mine_ref, tile, 0, lanes)
            grad = lanes_of(grad_ref, tile, 0, lanes)
            heard = lanes_of(out_ref, tile, 0, lanes)
            centre = jnp.sum(grad.astype(F32) * heard.astype(F32), axis=0, keepdims=True)
            gquery = jnp.zeros((HEAD, TILE), F32)
            for pair in range(tile + 1):
                rows = slice(2 * pair * TILE, 2 * (pair + 1) * TILE)
                raw = dot(keys[rows, :], query, NN) * (SCALE * LOG2E) - lse
                raws = [
                    jnp.where(
                        allowed_in(offsets, low, high, 2 * pair + side, core, tile),
                        raw[side * TILE : (side + 1) * TILE],
                        -1e30,
                    )
                    for side in range(2)
                ]
                prob = jnp.exp2(jnp.concatenate(raws, 0))
                gprob = dot(values[rows, :], grad, NN)
                gscore = (prob * (gprob - centre)).astype(BF16)
                gquery = gquery + dot(both_of(mine_ref, other_ref, pair, HEAD, lanes), gscore, NN)
                gkey = dot(query, gscore, NT)
                gvalue = dot(grad, prob.astype(BF16), NT)
                if pair == tile:
                    gkeys[:, rows], gvalues[:, rows] = gkey, gvalue
                else:
                    gkeys[:, rows] += gkey
                    gvalues[:, rows] += gvalue
            gquery = (gquery * SCALE).astype(BF16)
            gmine_ref[2 * tile, :HEAD, lanes] = gquery[:, :SPAN]
            gmine_ref[2 * tile + 1, :HEAD, lanes] = gquery[:, SPAN:]
        for chunk in range(8):
            ref, at = (gmine_ref, HEAD) if chunk % 2 == 0 else (gother_ref, 0)
            for half in range(2):
                cols = slice(chunk * TILE + half * SPAN, chunk * TILE + (half + 1) * SPAN)
                block = 2 * (chunk // 2) + half
                ref[block, at : at + HEAD, lanes] = (gkeys[:, cols] * SCALE).astype(BF16)
                ref[block, at + HEAD : at + 2 * HEAD, lanes] = gvalues[:, cols].astype(BF16)
        return carry

    lax.fori_loop(0, 2, one_micro, 0)


def front_kernel(
    start_ref, length_ref, hidden_ref, gain_ref, shift_ref, weight_ref, bias_ref, tiles_ref, second_ref, *copies
):
    rows, width = hidden_ref.shape
    lane = lax.broadcasted_iota(jnp.int32, (8, rows), 1)
    later = lane >= SPAN
    row = start_ref[0] + lane - jnp.where(later, SPAN, 0)
    first, second = [jnp.where(later, length_ref[0, 1, i], length_ref[0, 0, i]) for i in range(2)]
    begin = jnp.where(row >= first, first, 0) + jnp.where(row >= first + second, second, 0)
    order = lax.broadcasted_iota(jnp.int32, (8, rows), 0).astype(F32)
    ladder = jnp.exp(-math.log(10000.0) * (order * (2.0 / 16)))
    angle = ladder * (row - begin).astype(F32)
    cosine, sine = jnp.cos(angle), jnp.sin(angle)
    gain, shift = gain_ref[0].astype(F32), shift_ref[0].astype(F32)
    bias = bias_ref[...].astype(F32)
    xhat, _ = normed_of(hidden_ref[...].astype(F32))
    first = (xhat * gain[0:1] + shift[0:1]).astype(BF16)
    for copies_ref in copies:
        for block in range(copies_ref.shape[0]):
            copies_ref[block] = first
    second_ref[...] = (xhat * gain[1:2] + shift[1:2]).astype(BF16)
    for part in range(3):
        cols = slice(part * width, (part + 1) * width)
        made = (dot(first, weight_ref[:, cols], NN) + bias[:, cols]).T
        for head in range(HEADS):
            tile = made[head * HEAD : (head + 1) * HEAD]
            if part < 2:
                tile = turned(tile, cosine, sine)
            tiles_ref[head, part * HEAD : (part + 1) * HEAD, :] = tile.astype(BF16)


def back_kernel(
    core_ref, back_ref, hidden_ref, grad_ref, gsecond_ref, gain_ref, weight_ref, *refs
):
    early_refs = refs[: len(refs) - 2 if len(refs) == 2 else 1]
    ghidden_ref, *vector_refs, gqkv = refs[len(early_refs) :]
    width = hidden_ref.shape[1]
    rows = hidden_ref.shape[0]
    gfirst = jnp.zeros((rows, width), F32)
    ones = jnp.ones((8, rows), BF16)
    biases, gains, shifts = [], [], []
    for part in range(3):
        cols = slice(part * width, (part + 1) * width)
        for head in range(HEADS):
            gqkv[head * HEAD : (head + 1) * HEAD, :] = back_ref[head, part * HEAD : (part + 1) * HEAD, :]
        made = gqkv[...]
        gfirst = gfirst + dot(made.T, weight_ref[:, cols], NT)
        biases.append(dot(ones, made, NT)[:1])
    xhat, inv = normed_of(hidden_ref[...].astype(F32))
    gsecond = gsecond_ref[...]
    total = grad_ref[...].astype(F32)
    for which, grad in ((0, gfirst), (1, gsecond)):
        e = grad * gain_ref[which : which + 1, :]
        total = total + inv * (
            e - jnp.mean(e, -1, keepdims=True) - xhat * jnp.mean(e * xhat, -1, keepdims=True)
        )
        gains.append(jnp.sum(grad * xhat, 0, keepdims=True))
        shifts.append(jnp.sum(grad, 0, keepdims=True))
    ghidden_ref[...] = total.astype(BF16)
    if not vector_refs:
        return
    early = jnp.sum(early_refs[0][...], 0, keepdims=True)
    wide = gains + shifts + biases + [early[:, i * width : (i + 1) * width] for i in range(5)]
    lines = [v[:, half * width // 2 : (half + 1) * width // 2] for v in wide for half in range(2)]
    blank = [jnp.zeros((4, width // 2), F32)]
    first = jnp.concatenate(lines[:12] + blank, 0).astype(BF16)
    last = jnp.concatenate(lines[12:] + blank, 0).astype(BF16)
    ours_ref, theirs_ref = vector_refs
    ours_ref[...] = jnp.where(core_ref[0] == 0, first, last)
    theirs_ref[...] = jnp.where(core_ref[0] == 0, last, first)


def join_kernel(mine_ref, other_ref, cos_ref, sin_ref, *refs):
    out_ref = refs[-1]
    for block in range(8):
        if len(refs) > 1:
            out_ref[block, 3 * HEAD :, :] = refs[0][block]
        cosine, sine = cos_ref[block], -sin_ref[block]
        for part in range(3):
            rows = slice(part * HEAD, (part + 1) * HEAD)
            tile = mine_ref[block, rows, :].astype(F32)
            if part > 0:
                at = (part - 1) * HEAD
                tile = tile + other_ref[block, at : at + HEAD, :].astype(F32)
            if part < 2:
                tile = turned(tile, cosine, sine)
            out_ref[block, rows, :] = tile.astype(BF16)


def grad_kernel(section_ref, received_ref, own_ref, weight_ref, grad_ref, heard_ref):
    grad = jnp.where(section_ref[0] == 1, own_ref[...], received_ref[...])
    grad_ref[...] = grad
    made = dot(weight_ref[...], grad, NT).astype(BF16)
    for head in range(HEADS):
        heard_ref[head] = made[head * HEAD : (head + 1) * HEAD]


def early_terms_kernel(
    core_ref,
    second_ref,
    slope_ref,
    active_ref,
    grad_ref,
    heard_ref,
    down_ref,
    gup_ref,
    ours_ref,
    theirs_ref,
    sums_ref,
):
    core = core_ref[0]
    width = second_ref.shape[1]
    turned_second = second_ref[...].T
    grad = grad_ref[...]
    proj = dot(heard_ref[...], grad, NN).astype(BF16)
    sums_ref[:, 4 * width :] = jnp.sum(grad.astype(F32).reshape(-1, 8, width), 0)
    for block in range(4):
        cols = slice(block * width, (block + 1) * width)
        gup = (dot(grad, down_ref[cols, :], NT) * slope_ref[:, cols].astype(F32)).astype(BF16)
        gup_ref[:, cols] = gup
        sums_ref[:, cols] = jnp.sum(gup.astype(F32).reshape(-1, 8, width), 0)
        up = dot(turned_second, gup, NN).astype(BF16)
        down = dot(active_ref[:, cols].T, grad, NN).astype(BF16)
        first = proj[block * 64 : (block + 1) * 64]
        last = proj[256 + block * 64 : 256 + (block + 1) * 64]
        ours_ref[block, :width, :] = jnp.where(core == 0, up, down)
        theirs_ref[block, :width, :] = jnp.where(core == 0, down, up)
        ours_ref[block, width:, :] = jnp.where(core == 0, first, last)
        theirs_ref[block, width:, :] = jnp.where(core == 0, last, first)


def second_grad_kernel(gup_ref, up_ref, gsecond_ref):
    gsecond_ref[...] = dot(gup_ref[...], up_ref[...], NT)


def late_terms_kernel(core_ref, gqkv_ref, first_ref, ours_ref, theirs_ref):
    core = core_ref[0]
    total = jnp.zeros((3 * HEAD, first_ref.shape[2]), F32)
    for block in range(8):
        total = total + dot(gqkv_ref[block], first_ref[block], NN)
    total = jnp.concatenate([total, jnp.zeros((HEAD, total.shape[1]), F32)], 0).T
    half = total.shape[0] // 2
    upper, lower = total[:half].astype(BF16), total[half:].astype(BF16)
    ours_ref[...] = jnp.where(core == 0, upper, lower)
    theirs_ref[...] = jnp.where(core == 0, lower, upper)


def place_ring_kernel(at_ref, *refs):
    at = at_ref[0]
    for sources, target in ((refs[:5], refs[10]), (refs[5:10], refs[11])):
        own, back, ahead, far_a, far_b = sources
        extent, half = own.shape[0], far_a.shape[0]
        for step, source in ((0, own), (3, back), (1, ahead)):
            start = pl.multiple_of(lax.rem(at + step, 4) * extent, 16)
            target[pl.ds(start, extent), :] = source[...]
        start = lax.rem(at + 2, 4) * extent
        target[pl.ds(pl.multiple_of(start, 16), half), :] = far_a[...]
        target[pl.ds(pl.multiple_of(start + half, 16), half), :] = far_b[...]


def split_kernel(count, pieces, at_ref, *refs):
    sources, targets = refs[:count], refs[count:]
    extent = targets[0].shape[0]
    at = at_ref[0]
    for step in range(pieces):
        start = pl.multiple_of(lax.rem(at + step, pieces) * extent, extent)
        total = sources[0][pl.ds(start, extent), :].astype(F32)
        for source in sources[1:]:
            total = total + source[pl.ds(start, extent), :].astype(F32)
        targets[step][...] = total.astype(BF16)


def ring_kernel(at_ref, first_ref, last_ref, own_ref, next_ref, back_ref, far_a_ref, far_b_ref):
    at = at_ref[0]
    extent = own_ref.shape[0]

    def piece(step):
        rows = pl.ds(pl.multiple_of(lax.rem(at + step, 4) * extent, 16), extent)
        return (first_ref[rows, :].astype(F32) + last_ref[rows, :].astype(F32)).astype(BF16)

    own_ref[...] = piece(0)
    next_ref[...] = piece(1)
    back_ref[...] = piece(3)
    far = piece(2)
    far_a_ref[...] = far[: extent // 2]
    far_b_ref[...] = far[extent // 2 :]


def fold_kernel(next_ref, back_ref, far_a_ref, far_b_ref, to_next_ref, to_back_ref):
    half = far_a_ref.shape[0]
    total = next_ref[:half].astype(F32) + far_a_ref[...].astype(F32)
    to_next_ref[:half] = total.astype(BF16)
    to_next_ref[half:] = next_ref[half:]
    to_back_ref[:half] = back_ref[:half]
    total = back_ref[half:].astype(F32) + far_b_ref[...].astype(F32)
    to_back_ref[half:] = total.astype(BF16)


def split_both_kernel(z_ref, dp_ref, *refs):
    split_kernel(3, 4, z_ref, *refs[:3], *refs[5:9])
    split_kernel(2, 4, dp_ref, *refs[3:5], *refs[9:])


def place_kernel(at_ref, *refs):
    sources, target = refs[:-1], refs[-1]
    count, extent, at = len(sources), sources[0].shape[0], at_ref[0]
    for step, source in enumerate(sources):
        start = pl.multiple_of(lax.rem(at + count - step, count) * extent, extent)
        target[pl.ds(start, extent), :] = source[...]


def share_kernel(*refs):
    early, late, small, out_ref = refs[:4], refs[4:8], refs[8:10], refs[10]

    def total(sources):
        made = sources[0][...].astype(F32)
        for source in sources[1:]:
            made = made + source[...].astype(F32)
        return made.astype(BF16)

    made = total(early)
    rows, half = made.shape[0], made.shape[1] // 2
    out_ref[:rows, :] = made[:, :half]
    out_ref[rows : 2 * rows, :] = made[:, half:]
    out_ref[2 * rows : 2 * rows + HEAD, :] = total(late)
    out_ref[2 * rows + HEAD :, :] = total(small)


def out_kernel(
    core_ref,
    a_ref,
    b_ref,
    other_a_ref,
    other_b_ref,
    up_ref,
    down_ref,
    qkv_ref,
    proj_ref,
    gain_ref,
    shift_ref,
    qkv_bias_ref,
    up_bias_ref,
    branch_ref,
    vectors,
):
    core = core_ref[0]
    width = down_ref.shape[1]

    def parts(first_ref, second_ref):
        early, late = [], []
        for z in range(4):
            first = jnp.concatenate([first_ref[0, z, 0], first_ref[0, z, 1]], 1)
            second = jnp.concatenate([second_ref[z, 0, 0, :LAST], second_ref[z, 0, 1, :LAST]], 1)
            early += [first, second]
        for half in range(2):
            late += [second_ref[z, 0, half, LAST : LAST + HEAD] for z in range(4)]
        return jnp.concatenate(early, 0).astype(F32), [v.astype(F32) for v in late]

    mine, late = parts(a_ref, b_ref)
    other, other_late = parts(other_a_ref, other_b_ref)
    low, high = jnp.where(core == 0, mine, other), jnp.where(core == 0, other, mine)
    up_ref[...] = low[:width]
    down_ref[...] = high[:width]
    proj_ref[0] = low[width:]
    proj_ref[1] = high[width:]
    for head in range(HEADS):
        low = jnp.where(core == 0, late[head], other_late[head])
        high = jnp.where(core == 0, other_late[head], late[head])
        for part in range(3):
            at = part * width + head * HEAD
            qkv_ref[0, :, at : at + HEAD] = low[:, part * HEAD : (part + 1) * HEAD]
            qkv_ref[1, :, at : at + HEAD] = high[:, part * HEAD : (part + 1) * HEAD]
    step = pl.program_id(0)

    def vector_sum(ref):
        return sum(ref[z, 0, half, LAST + HEAD :].astype(F32) for z in range(4) for half in range(2))

    low, high = vector_sum(b_ref), vector_sum(other_b_ref)

    @pl.when(step == 0)
    def _():
        vectors[0], vectors[1] = low, high

    @pl.when(step > 0)
    def _():
        vectors[0] += low
        vectors[1] += high

    @pl.when(step == 3)
    def _():
        mine, other = vectors[0], vectors[1]
        first = jnp.where(core == 0, mine, other)
        last = jnp.where(core == 0, other, mine)
        lines = [first[i : i + 1] for i in range(12)] + [last[i : i + 1] for i in range(12)]
        wide = [jnp.concatenate(lines[2 * i : 2 * i + 2], 1) for i in range(12)]
        for row in range(2):
            gain_ref[row : row + 1, :] = wide[row]
            shift_ref[row : row + 1, :] = wide[2 + row]
            branch_ref[row : row + 1, :] = wide[11]
        qkv_bias_ref[...] = jnp.concatenate(wide[4:7], 1)
        up_bias_ref[...] = jnp.concatenate(wide[7:11], 1)


def halves_kernel(at_ref, mine_ref, other_ref, a_ref, b_ref):
    at = at_ref[0]
    early = EARLY
    total = mine_ref[: 2 * early].astype(F32) + other_ref[: 2 * early].astype(F32)
    total = total.astype(BF16)
    for half in range(2):
        a_ref[half * HALF : (half + 1) * HALF] = total[half * early : half * early + HALF]
        b_ref[half * HALF : half * HALF + LAST] = total[half * early + HALF : (half + 1) * early]
    for source, to in ((mine_ref, at), (other_ref, 1 - at)):
        rows = pl.ds(pl.multiple_of(to * HALF + LAST, 16), HALF - LAST)
        b_ref[rows, :] = source[2 * early :, :]


VMEM = pl.BlockSpec(memory_space=pltpu.VMEM)
SMEM = pl.BlockSpec(memory_space=pltpu.SMEM)
MIB = 1024 * 1024


def shaped(shape, dtype):
    return jax.ShapeDtypeStruct(shape, dtype)


def call(kernel, outs, *args, words=0, limit=12, scratch=(), name=None):
    single = not isinstance(outs, tuple)
    shapes = (outs,) if single else outs
    made = pl.pallas_call(
        kernel,
        out_shape=shapes,
        in_specs=[SMEM] * words + [VMEM] * (len(args) - words),
        out_specs=tuple(VMEM for _ in shapes),
        scratch_shapes=list(scratch),
        compiler_params=pltpu.CompilerParams(vmem_limit_bytes=limit * MIB),
        cost_estimate=pl.CostEstimate(flops=0, bytes_accessed=1024, transcendentals=0),
        name=name,
    )(*args)
    return made[0] if single else made


def attend(core, mine, other, low, high):
    return call(
        attend_kernel,
        (shaped((8, HEAD, 2 * SPAN), BF16), shaped((8, TILE), F32)),
        core, mine, other, low, high,
        words=1, limit=10,
        scratch=[pltpu.VMEM((2048, HEAD), BF16), pltpu.VMEM((2048, TILE), F32)],
        name="attend",
    )


def attend_back(core, mine, other, low, high, out, lse, grad):
    return call(
        attend_back_kernel,
        (shaped((8, 3 * HEAD, 2 * SPAN), BF16), shaped((8, 2 * HEAD, 2 * SPAN), BF16)),
        core, mine, other, low, high, out, lse, grad,
        words=1, limit=10,
        scratch=[
            pltpu.VMEM((2048, HEAD), BF16),
            pltpu.VMEM((2048, HEAD), BF16),
            pltpu.VMEM((HEAD, 2048), F32),
            pltpu.VMEM((HEAD, 2048), F32),
        ],
        name="attend_back",
    )


def swap(array, axis):
    return lax.ppermute(array, axis, [(0, 1), (1, 0)])


def word(value):
    return value.astype(jnp.int32).reshape(1)


def spread_from(pieces, axis):
    count = len(pieces)
    return [pieces[0]] + [
        lax.ppermute(pieces[s], axis, [(i, (i + s) % count) for i in range(count)])
        for s in range(1, count)
    ]


def turn(array, axis, by):
    count = lax.axis_size(axis)
    return lax.ppermute(array, axis, [(i, (i + by) % count) for i in range(count)])


def placed(pieces, axis):
    extent, width = pieces[0].shape
    return call(
        place_kernel, shaped((len(pieces) * extent, width), BF16),
        word(lax.axis_index(axis)), *pieces,
        words=1, limit=8, name="place",
    )


def normed_of(hidden):
    centred = hidden - jnp.mean(hidden, -1, keepdims=True)
    inv = lax.rsqrt(jnp.mean(centred * centred, -1, keepdims=True) + EPS)
    return centred * inv, inv


def turned(tile, cosine, sine):
    first, second = tile[:8], tile[8:16]
    return jnp.concatenate(
        [first * cosine - second * sine, second * cosine + first * sine, tile[16:]], 0
    )


def per_device(
    inputs,
    lengths,
    norm_gain,
    norm_bias,
    qkv_weight,
    qkv_bias,
    proj_weight,
    up_weight,
    up_bias,
    down_weight,
    branch_bias,
    cotangent,
):
    section = lax.axis_index("section")
    core = lax.axis_index("core")
    block = lax.axis_index(XZ)
    micros, span, width = inputs.shape
    rows = micros * span
    gains = norm_gain[0].astype(F32)
    w_qkv, w_proj, w_up, w_down = qkv_weight[0], proj_weight[0], up_weight[0], down_weight[0]
    b_up = up_bias[0].astype(F32)
    b_branch = jnp.sum(branch_bias[0].astype(F32), 0)
    core_word = word(core)

    def front(hidden, copies):
        tiles, second, *firsts = call(
            front_kernel,
            (shaped((HEADS, 3 * HEAD, rows), BF16), shaped((rows, width), BF16))
            + (shaped((HEADS, rows, width), BF16),) * copies,
            word((2 * block + core) * span), lengths, hidden, norm_gain, norm_bias, w_qkv, qkv_bias,
            words=2, limit=12 if copies else 56, name="front",
        )
        return firsts, second, tiles

    entry = inputs.reshape(rows, width)
    first_front = front(entry, 0)
    tiles, lengths = lax.optimization_barrier((first_front[-1], lengths))
    first_front = first_front[:-1] + (tiles,)
    one, two, three = [lengths[0][:, i] for i in range(3)]
    ends = jnp.stack([one, one + two, one + two + three], -1)

    def begin_of(row):
        after = row[None, :, None] >= ends[:, None, :]
        return jnp.sum(jnp.where(after, lengths[0][:, None, :], 0), -1)

    heard_rows = (
        (2 * jnp.arange(8, dtype=jnp.int32)[:, None] + core) * span
        + jnp.arange(span, dtype=jnp.int32)[None]
    ).reshape(-1)
    low = begin_of(heard_rows).reshape(8, TILE)
    high = jnp.broadcast_to(heard_rows[None], (micros, 8 * span)).reshape(8, TILE)
    ladder = jnp.exp(-math.log(10000.0) * (jnp.arange(8, dtype=F32) * (2.0 / 16)))
    heard_position = (heard_rows[None] - begin_of(heard_rows)).reshape(micros, 8, span)
    heard_position = jnp.moveaxis(heard_position, 0, 1).reshape(8, 1, rows).astype(F32)
    heard_angle = ladder[None, :, None] * heard_position
    heard_cosine, heard_sine = jnp.cos(heard_angle), jnp.sin(heard_angle)

    def mlp_of(second):
        up = dot(second, w_up, NN) + b_up
        phi = 0.5 * (1.0 + lax.erf(up * (1.0 / math.sqrt(2.0))))
        bell = jnp.exp(-0.5 * up * up) * (1.0 / math.sqrt(2.0 * math.pi))
        active = (up * phi).astype(BF16)
        slope = (phi + up * bell).astype(BF16)
        return active, slope

    def forward(hidden, firsts, second, tiles):
        mine = lax.all_to_all(tiles, XZ, 0, 0, tiled=True)
        other = swap(mine, "core")
        active, slope = mlp_of(second)
        base = hidden.astype(F32) + dot(active, w_down, NN) + b_branch
        heard, lse = attend(core_word, mine, other, low, high)
        return base, firsts, second, mine, other, active, slope, heard, lse

    def finish(base, heard_rows):
        return (base + dot(heard_rows, w_proj, TN)).astype(BF16)

    def heard_grad(received, own):
        grad_in, ggo = call(
            grad_kernel,
            (shaped((rows, width), BF16), shaped((HEADS, HEAD, rows), BF16)),
            word(section), received, own, w_proj,
            words=1, name="grad",
        )
        return grad_in, lax.all_to_all(ggo, XZ, 0, 0, tiled=True)

    def joined(gmine, gother, *along):
        return call(
            join_kernel, shaped((HEADS, (3 + len(along)) * HEAD, rows), BF16),
            gmine, swap(gother, "core"), heard_cosine, heard_sine, *along, name="join",
        )

    def rows_back(back, hidden, grad_in, gsecond, *early_sums):
        vectors = (shaped((16, width // 2), BF16),) * 2 if early_sums else ()
        return call(
            back_kernel,
            (shaped((rows, width), BF16),) + vectors,
            core_word, back, hidden, grad_in, gsecond, gains, w_qkv, *early_sums,
            words=1, scratch=[pltpu.VMEM((width, rows), BF16)], limit=56, name="back",
        )

    def mlp_back(grad_in, slope):
        gup = (dot(grad_in, w_down, NT) * slope.astype(F32)).astype(BF16)
        return gup, dot(gup, w_up, NT)

    loss_grad = cotangent.reshape(rows, width)
    grad_in, ggo = heard_grad(loss_grad, loss_grad)
    base, *_, heard, _ = forward(entry, *first_front)
    heard, ggo = lax.optimization_barrier((heard, ggo))
    heard_rows = lax.all_to_all(heard, XZ, 0, 0, tiled=True).reshape(width, rows)
    heard_rows, base = lax.optimization_barrier((heard_rows, base))
    sent = finish(base, heard_rows)
    received = lax.ppermute(sent, "section", [(0, 1)])
    entry = jnp.where(section == 1, received, entry)
    base, (firsts,), second, mine, other, active, slope, heard, lse = forward(entry, *front(entry, 1))
    mine, firsts = lax.optimization_barrier((mine, firsts))
    first_all = lax.all_to_all(firsts, XZ, 0, 0, tiled=True)
    _, gsecond = mlp_back(grad_in, slope)
    gmine, gother = attend_back(core_word, mine, other, low, high, heard, lse, ggo)
    back, first_all = lax.optimization_barrier((joined(gmine, gother, heard), first_all))
    back = lax.all_to_all(back, XZ, 0, 0, tiled=True)
    (sent_back,) = rows_back(back, entry, grad_in, gsecond)
    received = lax.ppermute(sent_back, "section", [(1, 0)])
    _, back = lax.optimization_barrier((sent_back, back))
    heard_rows = back[:, 3 * HEAD :].reshape(width, rows)
    result = finish(base, heard_rows)
    received, result, heard_rows = lax.optimization_barrier((received, result, heard_rows))
    grad_in, ggo = heard_grad(received, loss_grad)
    gup, *early, early_sums = call(
        early_terms_kernel,
        (shaped((rows, 4 * width), BF16),)
        + (shaped((4, width + 64, width), BF16),) * 2
        + (shaped((8, 5 * width), F32),),
        core_word, second, slope, active, grad_in, heard_rows, w_down,
        words=1, limit=56, name="early_terms",
    )
    ggo, early = lax.optimization_barrier((ggo, early))
    early = [v.reshape(-1, width) for v in early]
    whole, part = shaped((4 * EARLY, width), BF16), shaped((2 * EARLY, width), BF16)
    pieces = call(
        ring_kernel, (whole, whole, whole, part, part),
        word(lax.axis_index("dp")), early[0], swap(early[1], "core"),
        words=1, limit=56, name="ring",
    )
    ggo, pieces = lax.optimization_barrier((ggo, pieces))
    own, to_next, to_back, far_a, far_b = pieces
    far_a, far_b = turn(far_a, "dp", 1), turn(far_b, "dp", -1)
    gmine, gother = attend_back(core_word, mine, other, low, high, heard, lse, ggo)
    gmine, gother, far_a, far_b = lax.optimization_barrier((gmine, gother, far_a, far_b))
    to_next, to_back = call(fold_kernel, (whole, whole), to_next, to_back, far_a, far_b, name="fold")
    gmine = joined(gmine, gother)
    gmine, to_next, to_back = lax.optimization_barrier((gmine, to_next, to_back))
    pieces = [own, turn(to_next, "dp", 1), turn(to_back, "dp", -1)]
    late = call(
        late_terms_kernel,
        (shaped((width // 2, width // 2), BF16),) * 2,
        core_word, gmine, first_all,
        words=1, limit=56, name="late_terms",
    )
    late, gup = lax.optimization_barrier((late, gup))
    gsecond = call(second_grad_kernel, shaped((rows, width), F32), gup, w_up, name="second_grad")
    back = lax.all_to_all(gmine, XZ, 0, 0, tiled=True)
    pieces, late, gsecond = lax.optimization_barrier((pieces, late, gsecond))
    made = call(
        split_both_kernel,
        (shaped((EARLY, width), BF16),) * 4 + (shaped((HEAD, width // 2), BF16),) * 4,
        word(lax.axis_index("z")), word(lax.axis_index("dp")),
        *pieces, late[0], swap(late[1], "core"),
        words=2, limit=56, name="split_both",
    )
    pieces, late = spread_from(made[:4], "z"), spread_from(made[4:], "dp")
    back, pieces = lax.optimization_barrier((back, pieces))
    ghidden, *small = rows_back(back, entry, grad_in, gsecond, early_sums)
    share = call(
        share_kernel, shaped((2 * EARLY + HEAD + 16, width // 2), BF16),
        *pieces, *late, small[0], swap(small[1], "core"), name="share",
    )
    share, ghidden = lax.optimization_barrier((share, ghidden))

    a, b = call(
        halves_kernel,
        (shaped((2 * HALF, width // 2), BF16),) * 2,
        word(lax.axis_index("xl")), share, swap(share, "xl"),
        words=1, limit=8, name="halves",
    )
    a_pieces, b_pieces = spread_from([a] * 4, "z"), spread_from([b] * 4, "dp")
    a_pieces, b_pieces = lax.optimization_barrier((a_pieces, b_pieces))
    a, b = lax.optimization_barrier((placed(a_pieces, "z"), placed(b_pieces, "dp")))
    gathers = []
    for array, axis in ((a, "dp"), (b, "z")):
        back, ahead = turn(array, axis, 1), turn(array, axis, -1)
        half = array.shape[0] // 2
        far_a, far_b = turn(back[:half], axis, 1), turn(ahead[half:], axis, -1)
        gathers.append([array, back, ahead, far_a, far_b])
    gathers = [g + [swap(v, "core") for v in g] for g in gathers]
    gathers = lax.optimization_barrier(gathers)
    placed_all = [
        call(
            place_ring_kernel, (shaped((4 * g[0].shape[0], width // 2), BF16),) * 2,
            word(lax.axis_index(axis)), *g, words=1, limit=12, name="place_ring",
        )
        for g, axis in zip(gathers, ("dp", "z"))
    ]
    (a, other_a), (b, other_b) = placed_all
    a_spec = pl.BlockSpec((1, 4, 2, HALF, width // 2), lambda i: (i, 0, 0, 0, 0))
    b_spec = pl.BlockSpec((4, 1, 2, HALF, width // 2), lambda i: (0, i, 0, 0, 0))
    a, other_a, b, other_b = [v.reshape(4, 4, 2, HALF, width // 2) for v in (a, other_a, b, other_b)]
    up, down, qkv, proj, gain, shift, bias_qkv, bias_up, branch = pl.pallas_call(
        out_kernel,
        grid=(4,),
        out_shape=(
            shaped((width, 4 * width), F32),
            shaped((4 * width, width), F32),
            shaped((2, width // 2, 3 * width), F32),
            shaped((2, width // 2, width), F32),
            shaped((2, width), F32),
            shaped((2, width), F32),
            shaped((1, 3 * width), F32),
            shaped((1, 4 * width), F32),
            shaped((2, width), F32),
        ),
        in_specs=[SMEM, a_spec, b_spec, a_spec, b_spec],
        out_specs=(
            pl.BlockSpec((width, width), lambda i: (0, i)),
            pl.BlockSpec((width, width), lambda i: (i, 0)),
            pl.BlockSpec((2, 64, 3 * width), lambda i: (0, i, 0)),
            pl.BlockSpec((2, 64, width), lambda i: (0, i, 0)),
        )
        + tuple(
            pl.BlockSpec(shape, lambda i: (0, 0))
            for shape in ((2, width), (2, width), (1, 3 * width), (1, 4 * width), (2, width))
        ),
        scratch_shapes=[pltpu.VMEM((2, 16, width // 2), F32)],
        compiler_params=pltpu.CompilerParams(vmem_limit_bytes=32 * MIB),
        cost_estimate=pl.CostEstimate(flops=0, bytes_accessed=1024, transcendentals=0),
        name="out",
    )(core_word, a, b, other_a, other_b)
    qkv, proj = qkv.reshape(width, 3 * width), proj.reshape(width, width)
    return (
        result.reshape(1, micros, span, width),
        ghidden.reshape(1, micros, span, width),
        gain[None],
        shift[None],
        qkv[None],
        bias_qkv,
        proj[None],
        up[None],
        bias_up,
        down[None],
        branch[None],
    )


def solution(mesh):
    axes = ("section", "dp", "xl", "z", "core")
    fine = Mesh(mesh.devices.reshape(2, 4, 2, 4, 2), axes)
    spread = P(None, ("dp", "xl", "z", "core"), None)
    three, two = P("section", None, None), P("section", None)
    kept = P("section", None, ("dp", "xl", "z", "core"), None)
    in_specs = (
        spread, P("dp", None, None), three, three, three, two, three, three, two, three, three, spread,
    )
    out_specs = (kept, kept, three, three, three, two, three, three, two, three, three)
    return jax.shard_map(
        per_device, mesh=fine, in_specs=in_specs, out_specs=out_specs, check_vma=False
    )
```

```python
from functools import partial
import math

import jax
import jax.numpy as jnp
from jax import lax
from jax.experimental import pallas as pl
from jax.experimental.pallas import tpu as pltpu
from jax.sharding import Mesh, PartitionSpec as P

HEADS = 8
EPS = 1e-05
F32 = jnp.float32
BF16 = jnp.bfloat16
XZ = ("xl", "z")
LOG2E = math.log2(math.e)
SPAN = 128
HEAD = 64
TILE = 256
SCALE = 1.0 / math.sqrt(HEAD)
LAST = 32
EARLY = 144
HALF = 112


def dot(a, b, dims):
    return lax.dot_general(a, b, (dims, ((), ())), preferred_element_type=F32)


NN = ((1,), (0,))
NT = ((1,), (1,))
TN = ((0,), (0,))


def lanes_of(ref, block, at, lanes):
    return jnp.concatenate(
        [ref[2 * block, at : at + HEAD, lanes], ref[2 * block + 1, at : at + HEAD, lanes]], axis=1
    )


def both_of(mine_ref, other_ref, pair, at, lanes):
    return jnp.concatenate(
        [lanes_of(mine_ref, pair, at, lanes), lanes_of(other_ref, pair, at, lanes)], 1
    )


def lanes_at(micro):
    return pl.ds(pl.multiple_of(micro * SPAN, SPAN), SPAN)


def key_offsets():
    row = lax.broadcasted_iota(jnp.int32, (TILE, TILE), 0)
    return row + jnp.where(row >= SPAN, SPAN, 0)


def allowed_in(offsets, low, high, chunk, core, tile):
    side = core if chunk % 2 == 0 else 1 - core
    base = (chunk // 2) * (2 * TILE) + side * SPAN
    seen = offsets >= low - base
    if chunk // 2 == tile:
        seen = seen & (offsets <= high - base)
    return seen


def attend_kernel(core_ref, mine_ref, other_ref, low_ref, high_ref, out_ref, lse_ref, keys, scores):
    core = core_ref[0]
    offsets = key_offsets()

    def one_micro(micro, carry):
        lanes = lanes_at(micro)
        for chunk in range(8):
            ref, at = (mine_ref if chunk % 2 == 0 else other_ref), HEAD
            keys[chunk * TILE : (chunk + 1) * TILE, :] = lanes_of(ref, chunk // 2, at, lanes).T
        for tile in range(4):
            row = pl.ds(micro * 4 + tile, 1)
            low, high = low_ref[row, :], high_ref[row, :]
            query = lanes_of(mine_ref, tile, 0, lanes)
            top = jnp.full((8, TILE), -1e30, F32)
            for chunk in range(2 * tile + 2):
                rows = slice(chunk * TILE, (chunk + 1) * TILE)
                raw = dot(keys[rows, :], query, NN) * (SCALE * LOG2E)
                raw = jnp.where(allowed_in(offsets, low, high, chunk, core, tile), raw, -1e30)
                scores[rows, :] = raw
                top = jnp.maximum(top, jnp.max(raw.reshape(-1, 8, TILE), axis=0))
            top = jnp.max(top, axis=0, keepdims=True)
            total = jnp.zeros((8, TILE), F32)
            heard = jnp.zeros((HEAD, TILE), F32)
            for pair in range(tile + 1):
                rows = slice(2 * pair * TILE, 2 * (pair + 1) * TILE)
                weight = jnp.exp2(scores[rows, :] - top)
                total = total + jnp.sum(weight.reshape(-1, 8, TILE), axis=0)
                value = both_of(mine_ref, other_ref, pair, 2 * HEAD, lanes)
                heard = heard + dot(value, weight.astype(BF16), NN)
            total = jnp.sum(total, axis=0, keepdims=True)
            heard = (heard / total).astype(BF16)
            out_ref[2 * tile, :, lanes] = heard[:, :SPAN]
            out_ref[2 * tile + 1, :, lanes] = heard[:, SPAN:]
            lse_ref[row, :] = top + jnp.log2(total)
        return carry

    lax.fori_loop(0, 2, one_micro, 0)


def attend_back_kernel(
    core_ref,
    mine_ref,
    other_ref,
    low_ref,
    high_ref,
    out_ref,
    lse_ref,
    grad_ref,
    gmine_ref,
    gother_ref,
    keys,
    values,
    gkeys,
    gvalues,
):
    core = core_ref[0]
    offsets = key_offsets()

    def one_micro(micro, carry):
        lanes = lanes_at(micro)
        for chunk in range(8):
            rows = slice(chunk * TILE, (chunk + 1) * TILE)
            ref, at = (mine_ref if chunk % 2 == 0 else other_ref), HEAD
            keys[rows, :] = lanes_of(ref, chunk // 2, at, lanes).T
            values[rows, :] = lanes_of(ref, chunk // 2, at + HEAD, lanes).T
        for tile in range(4):
            row = pl.ds(micro * 4 + tile, 1)
            low, high, lse = low_ref[row, :], high_ref[row, :], lse_ref[row, :]
            query = lanes_of(mine_ref, tile, 0, lanes)
            grad = lanes_of(grad_ref, tile, 0, lanes)
            heard = lanes_of(out_ref, tile, 0, lanes)
            centre = jnp.sum(grad.astype(F32) * heard.astype(F32), axis=0, keepdims=True)
            gquery = jnp.zeros((HEAD, TILE), F32)
            for pair in range(tile + 1):
                rows = slice(2 * pair * TILE, 2 * (pair + 1) * TILE)
                raw = dot(keys[rows, :], query, NN) * (SCALE * LOG2E) - lse
                raws = [
                    jnp.where(
                        allowed_in(offsets, low, high, 2 * pair + side, core, tile),
                        raw[side * TILE : (side + 1) * TILE],
                        -1e30,
                    )
                    for side in range(2)
                ]
                prob = jnp.exp2(jnp.concatenate(raws, 0))
                gprob = dot(values[rows, :], grad, NN)
                gscore = (prob * (gprob - centre)).astype(BF16)
                gquery = gquery + dot(both_of(mine_ref, other_ref, pair, HEAD, lanes), gscore, NN)
                gkey = dot(query, gscore, NT)
                gvalue = dot(grad, prob.astype(BF16), NT)
                if pair == tile:
                    gkeys[:, rows], gvalues[:, rows] = gkey, gvalue
                else:
                    gkeys[:, rows] += gkey
                    gvalues[:, rows] += gvalue
            gquery = (gquery * SCALE).astype(BF16)
            gmine_ref[2 * tile, :HEAD, lanes] = gquery[:, :SPAN]
            gmine_ref[2 * tile + 1, :HEAD, lanes] = gquery[:, SPAN:]
        for chunk in range(8):
            ref, at = (gmine_ref, HEAD) if chunk % 2 == 0 else (gother_ref, 0)
            for half in range(2):
                cols = slice(chunk * TILE + half * SPAN, chunk * TILE + (half + 1) * SPAN)
                block = 2 * (chunk // 2) + half
                ref[block, at : at + HEAD, lanes] = (gkeys[:, cols] * SCALE).astype(BF16)
                ref[block, at + HEAD : at + 2 * HEAD, lanes] = gvalues[:, cols].astype(BF16)
        return carry

    lax.fori_loop(0, 2, one_micro, 0)


def front_kernel(
    start_ref, length_ref, hidden_ref, gain_ref, shift_ref, weight_ref, bias_ref, tiles_ref, second_ref, *copies
):
    rows, width = hidden_ref.shape
    lane = lax.broadcasted_iota(jnp.int32, (8, rows), 1)
    later = lane >= SPAN
    row = start_ref[0] + lane - jnp.where(later, SPAN, 0)
    first, second = [jnp.where(later, length_ref[0, 1, i], length_ref[0, 0, i]) for i in range(2)]
    begin = jnp.where(row >= first, first, 0) + jnp.where(row >= first + second, second, 0)
    order = lax.broadcasted_iota(jnp.int32, (8, rows), 0).astype(F32)
    ladder = jnp.exp(-math.log(10000.0) * (order * (2.0 / 16)))
    angle = ladder * (row - begin).astype(F32)
    cosine, sine = jnp.cos(angle), jnp.sin(angle)
    gain, shift = gain_ref[0].astype(F32), shift_ref[0].astype(F32)
    bias = bias_ref[...].astype(F32)
    xhat, _ = normed_of(hidden_ref[...].astype(F32))
    first = (xhat * gain[0:1] + shift[0:1]).astype(BF16)
    for copies_ref in copies:
        for block in range(copies_ref.shape[0]):
            copies_ref[block] = first
    second_ref[...] = (xhat * gain[1:2] + shift[1:2]).astype(BF16)
    for part in range(3):
        cols = slice(part * width, (part + 1) * width)
        made = (dot(first, weight_ref[:, cols], NN) + bias[:, cols]).T
        for head in range(HEADS):
            tile = made[head * HEAD : (head + 1) * HEAD]
            if part < 2:
                tile = turned(tile, cosine, sine)
            tiles_ref[head, part * HEAD : (part + 1) * HEAD, :] = tile.astype(BF16)


def back_kernel(
    core_ref, back_ref, hidden_ref, grad_ref, gsecond_ref, gain_ref, weight_ref, *refs
):
    early_refs = refs[: len(refs) - 2 if len(refs) == 2 else 1]
    ghidden_ref, *vector_refs, gqkv = refs[len(early_refs) :]
    width = hidden_ref.shape[1]
    rows = hidden_ref.shape[0]
    gfirst = jnp.zeros((rows, width), F32)
    ones = jnp.ones((8, rows), BF16)
    biases, gains, shifts = [], [], []
    for part in range(3):
        cols = slice(part * width, (part + 1) * width)
        for head in range(HEADS):
            gqkv[head * HEAD : (head + 1) * HEAD, :] = back_ref[head, part * HEAD : (part + 1) * HEAD, :]
        made = gqkv[...]
        gfirst = gfirst + dot(made.T, weight_ref[:, cols], NT)
        biases.append(dot(ones, made, NT)[:1])
    xhat, inv = normed_of(hidden_ref[...].astype(F32))
    gsecond = gsecond_ref[...]
    total = grad_ref[...].astype(F32)
    for which, grad in ((0, gfirst), (1, gsecond)):
        e = grad * gain_ref[which : which + 1, :]
        total = total + inv * (
            e - jnp.mean(e, -1, keepdims=True) - xhat * jnp.mean(e * xhat, -1, keepdims=True)
        )
        gains.append(jnp.sum(grad * xhat, 0, keepdims=True))
        shifts.append(jnp.sum(grad, 0, keepdims=True))
    ghidden_ref[...] = total.astype(BF16)
    if not vector_refs:
        return
    early = jnp.sum(early_refs[0][...], 0, keepdims=True)
    wide = gains + shifts + biases + [early[:, i * width : (i + 1) * width] for i in range(5)]
    lines = [v[:, half * width // 2 : (half + 1) * width // 2] for v in wide for half in range(2)]
    blank = [jnp.zeros((4, width // 2), F32)]
    first = jnp.concatenate(lines[:12] + blank, 0).astype(BF16)
    last = jnp.concatenate(lines[12:] + blank, 0).astype(BF16)
    ours_ref, theirs_ref = vector_refs
    ours_ref[...] = jnp.where(core_ref[0] == 0, first, last)
    theirs_ref[...] = jnp.where(core_ref[0] == 0, last, first)


def join_kernel(mine_ref, other_ref, cos_ref, sin_ref, *refs):
    out_ref = refs[-1]
    for block in range(8):
        if len(refs) > 1:
            out_ref[block, 3 * HEAD :, :] = refs[0][block]
        cosine, sine = cos_ref[block], -sin_ref[block]
        for part in range(3):
            rows = slice(part * HEAD, (part + 1) * HEAD)
            tile = mine_ref[block, rows, :].astype(F32)
            if part > 0:
                at = (part - 1) * HEAD
                tile = tile + other_ref[block, at : at + HEAD, :].astype(F32)
            if part < 2:
                tile = turned(tile, cosine, sine)
            out_ref[block, rows, :] = tile.astype(BF16)


def grad_kernel(section_ref, received_ref, own_ref, weight_ref, grad_ref, heard_ref):
    grad = jnp.where(section_ref[0] == 1, own_ref[...], received_ref[...])
    grad_ref[...] = grad
    made = dot(weight_ref[...], grad, NT).astype(BF16)
    for head in range(HEADS):
        heard_ref[head] = made[head * HEAD : (head + 1) * HEAD]


def early_terms_kernel(
    core_ref,
    second_ref,
    slope_ref,
    active_ref,
    grad_ref,
    heard_ref,
    down_ref,
    gup_ref,
    ours_ref,
    theirs_ref,
    sums_ref,
):
    core = core_ref[0]
    width = second_ref.shape[1]
    turned_second = second_ref[...].T
    grad = grad_ref[...]
    proj = dot(heard_ref[...], grad, NN).astype(BF16)
    sums_ref[:, 4 * width :] = jnp.sum(grad.astype(F32).reshape(-1, 8, width), 0)
    for block in range(4):
        cols = slice(block * width, (block + 1) * width)
        gup = (dot(grad, down_ref[cols, :], NT) * slope_ref[:, cols].astype(F32)).astype(BF16)
        gup_ref[:, cols] = gup
        sums_ref[:, cols] = jnp.sum(gup.astype(F32).reshape(-1, 8, width), 0)
        up = dot(turned_second, gup, NN).astype(BF16)
        down = dot(active_ref[:, cols].T, grad, NN).astype(BF16)
        first = proj[block * 64 : (block + 1) * 64]
        last = proj[256 + block * 64 : 256 + (block + 1) * 64]
        ours_ref[block, :width, :] = jnp.where(core == 0, up, down)
        theirs_ref[block, :width, :] = jnp.where(core == 0, down, up)
        ours_ref[block, width:, :] = jnp.where(core == 0, first, last)
        theirs_ref[block, width:, :] = jnp.where(core == 0, last, first)


def second_grad_kernel(gup_ref, up_ref, gsecond_ref):
    gsecond_ref[...] = dot(gup_ref[...], up_ref[...], NT)


def late_terms_kernel(core_ref, gqkv_ref, first_ref, ours_ref, theirs_ref):
    core = core_ref[0]
    total = jnp.zeros((3 * HEAD, first_ref.shape[2]), F32)
    for block in range(8):
        total = total + dot(gqkv_ref[block], first_ref[block], NN)
    total = jnp.concatenate([total, jnp.zeros((HEAD, total.shape[1]), F32)], 0).T
    half = total.shape[0] // 2
    upper, lower = total[:half].astype(BF16), total[half:].astype(BF16)
    ours_ref[...] = jnp.where(core == 0, upper, lower)
    theirs_ref[...] = jnp.where(core == 0, lower, upper)


def place_ring_kernel(dp_ref, z_ref, *refs):
    for group, at_ref in enumerate((dp_ref, dp_ref, z_ref, z_ref)):
        own, back, ahead = refs[3 * group : 3 * group + 3]
        far, target = refs[12 + group % 2], refs[14 + group]
        at, extent = at_ref[0], own.shape[0]
        for step, source in ((0, own), (3, back), (1, ahead)):
            start = pl.multiple_of(lax.rem(at + step, 4) * extent, 16)
            target[pl.ds(start, extent), :] = source[...]
        start = pl.multiple_of(lax.rem(at + 2, 4) * extent, 16)
        target[pl.ds(start, extent), :] = far[(group // 2) * extent : (group // 2 + 1) * extent]


def split_kernel(count, pieces, at_ref, *refs):
    sources, targets = refs[:count], refs[count:]
    extent = targets[0].shape[0]
    at = at_ref[0]
    for step in range(pieces):
        start = pl.multiple_of(lax.rem(at + step, pieces) * extent, extent)
        total = sources[0][pl.ds(start, extent), :].astype(F32)
        for source in sources[1:]:
            total = total + source[pl.ds(start, extent), :].astype(F32)
        targets[step][...] = total.astype(BF16)


def ring_kernel(at_ref, first_ref, last_ref, own_ref, next_ref, back_ref, far_a_ref, far_b_ref):
    at = at_ref[0]
    extent = own_ref.shape[0]

    def piece(step):
        rows = pl.ds(pl.multiple_of(lax.rem(at + step, 4) * extent, 16), extent)
        return (first_ref[rows, :].astype(F32) + last_ref[rows, :].astype(F32)).astype(BF16)

    own_ref[...] = piece(0)
    next_ref[...] = piece(1)
    back_ref[...] = piece(3)
    far = piece(2)
    far_a_ref[...] = far[: extent // 2]
    far_b_ref[...] = far[extent // 2 :]


def fold_kernel(next_ref, back_ref, far_a_ref, far_b_ref, to_next_ref, to_back_ref):
    half = far_a_ref.shape[0]
    total = next_ref[:half].astype(F32) + far_a_ref[...].astype(F32)
    to_next_ref[:half] = total.astype(BF16)
    to_next_ref[half:] = next_ref[half:]
    to_back_ref[:half] = back_ref[:half]
    total = back_ref[half:].astype(F32) + far_b_ref[...].astype(F32)
    to_back_ref[half:] = total.astype(BF16)


def split_both_kernel(z_ref, dp_ref, *refs):
    split_kernel(3, 4, z_ref, *refs[:3], *refs[5:9])
    split_kernel(2, 4, dp_ref, *refs[3:5], *refs[9:])


def place_kernel(at_ref, *refs):
    sources, target = refs[:-1], refs[-1]
    count, extent, at = len(sources), sources[0].shape[0], at_ref[0]
    for step, source in enumerate(sources):
        start = pl.multiple_of(lax.rem(at + count - step, count) * extent, extent)
        target[pl.ds(start, extent), :] = source[...]


def share_kernel(*refs):
    early, late, small, out_ref = refs[:4], refs[4:8], refs[8:10], refs[10]

    def total(sources):
        made = sources[0][...].astype(F32)
        for source in sources[1:]:
            made = made + source[...].astype(F32)
        return made.astype(BF16)

    made = total(early)
    rows, half = made.shape[0], made.shape[1] // 2
    out_ref[:rows, :] = made[:, :half]
    out_ref[rows : 2 * rows, :] = made[:, half:]
    out_ref[2 * rows : 2 * rows + HEAD, :] = total(late)
    out_ref[2 * rows + HEAD :, :] = total(small)


def out_kernel(
    core_ref,
    a_ref,
    b_ref,
    other_a_ref,
    other_b_ref,
    up_ref,
    down_ref,
    qkv_ref,
    proj_ref,
    gain_ref,
    shift_ref,
    qkv_bias_ref,
    up_bias_ref,
    branch_ref,
    vectors,
):
    core = core_ref[0]
    width = down_ref.shape[1]

    def parts(first_ref, second_ref):
        early, late = [], []
        for z in range(4):
            first = jnp.concatenate([first_ref[0, z, 0], first_ref[0, z, 1]], 1)
            second = jnp.concatenate([second_ref[z, 0, 0, :LAST], second_ref[z, 0, 1, :LAST]], 1)
            early += [first, second]
        for half in range(2):
            late += [second_ref[z, 0, half, LAST : LAST + HEAD] for z in range(4)]
        return jnp.concatenate(early, 0).astype(F32), [v.astype(F32) for v in late]

    mine, late = parts(a_ref, b_ref)
    other, other_late = parts(other_a_ref, other_b_ref)
    low, high = jnp.where(core == 0, mine, other), jnp.where(core == 0, other, mine)
    up_ref[...] = low[:width]
    down_ref[...] = high[:width]
    proj_ref[0] = low[width:]
    proj_ref[1] = high[width:]
    for head in range(HEADS):
        low = jnp.where(core == 0, late[head], other_late[head])
        high = jnp.where(core == 0, other_late[head], late[head])
        for part in range(3):
            at = part * width + head * HEAD
            qkv_ref[0, :, at : at + HEAD] = low[:, part * HEAD : (part + 1) * HEAD]
            qkv_ref[1, :, at : at + HEAD] = high[:, part * HEAD : (part + 1) * HEAD]
    step = pl.program_id(0)

    def vector_sum(ref):
        return sum(ref[z, 0, half, LAST + HEAD :].astype(F32) for z in range(4) for half in range(2))

    low, high = vector_sum(b_ref), vector_sum(other_b_ref)

    @pl.when(step == 0)
    def _():
        vectors[0], vectors[1] = low, high

    @pl.when(step > 0)
    def _():
        vectors[0] += low
        vectors[1] += high

    @pl.when(step == 3)
    def _():
        mine, other = vectors[0], vectors[1]
        first = jnp.where(core == 0, mine, other)
        last = jnp.where(core == 0, other, mine)
        lines = [first[i : i + 1] for i in range(12)] + [last[i : i + 1] for i in range(12)]
        wide = [jnp.concatenate(lines[2 * i : 2 * i + 2], 1) for i in range(12)]
        for row in range(2):
            gain_ref[row : row + 1, :] = wide[row]
            shift_ref[row : row + 1, :] = wide[2 + row]
            branch_ref[row : row + 1, :] = wide[11]
        qkv_bias_ref[...] = jnp.concatenate(wide[4:7], 1)
        up_bias_ref[...] = jnp.concatenate(wide[7:11], 1)


def halves_kernel(at_ref, mine_ref, other_ref, a_ref, b_ref):
    at = at_ref[0]
    early = EARLY
    total = mine_ref[: 2 * early].astype(F32) + other_ref[: 2 * early].astype(F32)
    total = total.astype(BF16)
    for half in range(2):
        a_ref[half * HALF : (half + 1) * HALF] = total[half * early : half * early + HALF]
        b_ref[half * HALF : half * HALF + LAST] = total[half * early + HALF : (half + 1) * early]
    for source, to in ((mine_ref, at), (other_ref, 1 - at)):
        rows = pl.ds(pl.multiple_of(to * HALF + LAST, 16), HALF - LAST)
        b_ref[rows, :] = source[2 * early :, :]


VMEM = pl.BlockSpec(memory_space=pltpu.VMEM)
SMEM = pl.BlockSpec(memory_space=pltpu.SMEM)
MIB = 1024 * 1024


def shaped(shape, dtype):
    return jax.ShapeDtypeStruct(shape, dtype)


def call(kernel, outs, *args, words=0, limit=12, scratch=(), name=None):
    single = not isinstance(outs, tuple)
    shapes = (outs,) if single else outs
    made = pl.pallas_call(
        kernel,
        out_shape=shapes,
        in_specs=[SMEM] * words + [VMEM] * (len(args) - words),
        out_specs=tuple(VMEM for _ in shapes),
        scratch_shapes=list(scratch),
        compiler_params=pltpu.CompilerParams(vmem_limit_bytes=limit * MIB),
        cost_estimate=pl.CostEstimate(flops=0, bytes_accessed=1024, transcendentals=0),
        name=name,
    )(*args)
    return made[0] if single else made


def attend(core, mine, other, low, high):
    return call(
        attend_kernel,
        (shaped((8, HEAD, 2 * SPAN), BF16), shaped((8, TILE), F32)),
        core, mine, other, low, high,
        words=1, limit=10,
        scratch=[pltpu.VMEM((2048, HEAD), BF16), pltpu.VMEM((2048, TILE), F32)],
        name="attend",
    )


def attend_back(core, mine, other, low, high, out, lse, grad):
    return call(
        attend_back_kernel,
        (shaped((8, 3 * HEAD, 2 * SPAN), BF16), shaped((8, 2 * HEAD, 2 * SPAN), BF16)),
        core, mine, other, low, high, out, lse, grad,
        words=1, limit=10,
        scratch=[
            pltpu.VMEM((2048, HEAD), BF16),
            pltpu.VMEM((2048, HEAD), BF16),
            pltpu.VMEM((HEAD, 2048), F32),
            pltpu.VMEM((HEAD, 2048), F32),
        ],
        name="attend_back",
    )


def swap(array, axis):
    return lax.ppermute(array, axis, [(0, 1), (1, 0)])


def word(value):
    return value.astype(jnp.int32).reshape(1)


def spread_from(pieces, axis):
    count = len(pieces)
    return [pieces[0]] + [
        lax.ppermute(pieces[s], axis, [(i, (i + s) % count) for i in range(count)])
        for s in range(1, count)
    ]


def turn(array, axis, by):
    count = lax.axis_size(axis)
    return lax.ppermute(array, axis, [(i, (i + by) % count) for i in range(count)])


def placed(pieces, axis):
    extent, width = pieces[0].shape
    return call(
        place_kernel, shaped((len(pieces) * extent, width), BF16),
        word(lax.axis_index(axis)), *pieces,
        words=1, limit=8, name="place",
    )


def normed_of(hidden):
    centred = hidden - jnp.mean(hidden, -1, keepdims=True)
    inv = lax.rsqrt(jnp.mean(centred * centred, -1, keepdims=True) + EPS)
    return centred * inv, inv


def turned(tile, cosine, sine):
    first, second = tile[:8], tile[8:16]
    return jnp.concatenate(
        [first * cosine - second * sine, second * cosine + first * sine, tile[16:]], 0
    )


def per_device(
    inputs,
    lengths,
    norm_gain,
    norm_bias,
    qkv_weight,
    qkv_bias,
    proj_weight,
    up_weight,
    up_bias,
    down_weight,
    branch_bias,
    cotangent,
):
    section = lax.axis_index("section")
    core = lax.axis_index("core")
    block = lax.axis_index(XZ)
    micros, span, width = inputs.shape
    rows = micros * span
    gains = norm_gain[0].astype(F32)
    w_qkv, w_proj, w_up, w_down = qkv_weight[0], proj_weight[0], up_weight[0], down_weight[0]
    b_up = up_bias[0].astype(F32)
    b_branch = jnp.sum(branch_bias[0].astype(F32), 0)
    core_word = word(core)

    def front(hidden, copies):
        tiles, second, *firsts = call(
            front_kernel,
            (shaped((HEADS, 3 * HEAD, rows), BF16), shaped((rows, width), BF16))
            + (shaped((HEADS, rows, width), BF16),) * copies,
            word((2 * block + core) * span), lengths, hidden, norm_gain, norm_bias, w_qkv, qkv_bias,
            words=2, limit=12 if copies else 56, name="front",
        )
        return firsts, second, tiles

    entry = inputs.reshape(rows, width)
    first_front = front(entry, 0)
    tiles, lengths = lax.optimization_barrier((first_front[-1], lengths))
    first_front = first_front[:-1] + (tiles,)
    one, two, three = [lengths[0][:, i] for i in range(3)]
    ends = jnp.stack([one, one + two, one + two + three], -1)

    def begin_of(row):
        after = row[None, :, None] >= ends[:, None, :]
        return jnp.sum(jnp.where(after, lengths[0][:, None, :], 0), -1)

    heard_rows = (
        (2 * jnp.arange(8, dtype=jnp.int32)[:, None] + core) * span
        + jnp.arange(span, dtype=jnp.int32)[None]
    ).reshape(-1)
    low = begin_of(heard_rows).reshape(8, TILE)
    high = jnp.broadcast_to(heard_rows[None], (micros, 8 * span)).reshape(8, TILE)
    ladder = jnp.exp(-math.log(10000.0) * (jnp.arange(8, dtype=F32) * (2.0 / 16)))
    heard_position = (heard_rows[None] - begin_of(heard_rows)).reshape(micros, 8, span)
    heard_position = jnp.moveaxis(heard_position, 0, 1).reshape(8, 1, rows).astype(F32)
    heard_angle = ladder[None, :, None] * heard_position
    heard_cosine, heard_sine = jnp.cos(heard_angle), jnp.sin(heard_angle)

    def mlp_of(second):
        up = dot(second, w_up, NN) + b_up
        phi = 0.5 * (1.0 + lax.erf(up * (1.0 / math.sqrt(2.0))))
        bell = jnp.exp(-0.5 * up * up) * (1.0 / math.sqrt(2.0 * math.pi))
        active = (up * phi).astype(BF16)
        slope = (phi + up * bell).astype(BF16)
        return active, slope

    def forward(hidden, firsts, second, tiles):
        mine = lax.all_to_all(tiles, XZ, 0, 0, tiled=True)
        other = swap(mine, "core")
        active, slope = mlp_of(second)
        base = hidden.astype(F32) + dot(active, w_down, NN) + b_branch
        heard, lse = attend(core_word, mine, other, low, high)
        return base, firsts, second, mine, other, active, slope, heard, lse

    def finish(base, heard_rows):
        return (base + dot(heard_rows, w_proj, TN)).astype(BF16)

    def heard_grad(received, own):
        grad_in, ggo = call(
            grad_kernel,
            (shaped((rows, width), BF16), shaped((HEADS, HEAD, rows), BF16)),
            word(section), received, own, w_proj,
            words=1, name="grad",
        )
        return grad_in, lax.all_to_all(ggo, XZ, 0, 0, tiled=True)

    def joined(gmine, gother, *along):
        return call(
            join_kernel, shaped((HEADS, (3 + len(along)) * HEAD, rows), BF16),
            gmine, swap(gother, "core"), heard_cosine, heard_sine, *along, name="join",
        )

    def rows_back(back, hidden, grad_in, gsecond, *early_sums):
        vectors = (shaped((16, width // 2), BF16),) * 2 if early_sums else ()
        return call(
            back_kernel,
            (shaped((rows, width), BF16),) + vectors,
            core_word, back, hidden, grad_in, gsecond, gains, w_qkv, *early_sums,
            words=1, scratch=[pltpu.VMEM((width, rows), BF16)], limit=56, name="back",
        )

    def mlp_back(grad_in, slope):
        gup = (dot(grad_in, w_down, NT) * slope.astype(F32)).astype(BF16)
        return gup, dot(gup, w_up, NT)

    loss_grad = cotangent.reshape(rows, width)
    grad_in, ggo = heard_grad(loss_grad, loss_grad)
    base, *_, heard, _ = forward(entry, *first_front)
    heard, ggo = lax.optimization_barrier((heard, ggo))
    heard_rows = lax.all_to_all(heard, XZ, 0, 0, tiled=True).reshape(width, rows)
    heard_rows, base = lax.optimization_barrier((heard_rows, base))
    sent = finish(base, heard_rows)
    received = lax.ppermute(sent, "section", [(0, 1)])
    entry = jnp.where(section == 1, received, entry)
    base, (firsts,), second, mine, other, active, slope, heard, lse = forward(entry, *front(entry, 1))
    mine, firsts = lax.optimization_barrier((mine, firsts))
    first_all = lax.all_to_all(firsts, XZ, 0, 0, tiled=True)
    _, gsecond = mlp_back(grad_in, slope)
    gmine, gother = attend_back(core_word, mine, other, low, high, heard, lse, ggo)
    back, first_all = lax.optimization_barrier((joined(gmine, gother, heard), first_all))
    back = lax.all_to_all(back, XZ, 0, 0, tiled=True)
    (sent_back,) = rows_back(back, entry, grad_in, gsecond)
    received = lax.ppermute(sent_back, "section", [(1, 0)])
    _, back = lax.optimization_barrier((sent_back, back))
    heard_rows = back[:, 3 * HEAD :].reshape(width, rows)
    result = finish(base, heard_rows)
    received, result, heard_rows = lax.optimization_barrier((received, result, heard_rows))
    grad_in, ggo = heard_grad(received, loss_grad)
    gup, *early, early_sums = call(
        early_terms_kernel,
        (shaped((rows, 4 * width), BF16),)
        + (shaped((4, width + 64, width), BF16),) * 2
        + (shaped((8, 5 * width), F32),),
        core_word, second, slope, active, grad_in, heard_rows, w_down,
        words=1, limit=56, name="early_terms",
    )
    ggo, early = lax.optimization_barrier((ggo, early))
    early = [v.reshape(-1, width) for v in early]
    whole, part = shaped((4 * EARLY, width), BF16), shaped((2 * EARLY, width), BF16)
    pieces = call(
        ring_kernel, (whole, whole, whole, part, part),
        word(lax.axis_index("dp")), early[0], swap(early[1], "core"),
        words=1, limit=56, name="ring",
    )
    ggo, pieces = lax.optimization_barrier((ggo, pieces))
    own, to_next, to_back, far_a, far_b = pieces
    far_a, far_b = turn(far_a, "dp", 1), turn(far_b, "dp", -1)
    gmine, gother = attend_back(core_word, mine, other, low, high, heard, lse, ggo)
    gmine, gother, far_a, far_b = lax.optimization_barrier((gmine, gother, far_a, far_b))
    to_next, to_back = call(fold_kernel, (whole, whole), to_next, to_back, far_a, far_b, name="fold")
    gmine = joined(gmine, gother)
    gmine, to_next, to_back = lax.optimization_barrier((gmine, to_next, to_back))
    pieces = [own, turn(to_next, "dp", 1), turn(to_back, "dp", -1)]
    late = call(
        late_terms_kernel,
        (shaped((width // 2, width // 2), BF16),) * 2,
        core_word, gmine, first_all,
        words=1, limit=56, name="late_terms",
    )
    late, gup = lax.optimization_barrier((late, gup))
    gsecond = call(second_grad_kernel, shaped((rows, width), F32), gup, w_up, name="second_grad")
    back = lax.all_to_all(gmine, XZ, 0, 0, tiled=True)
    pieces, late, gsecond = lax.optimization_barrier((pieces, late, gsecond))
    made = call(
        split_both_kernel,
        (shaped((EARLY, width), BF16),) * 4 + (shaped((HEAD, width // 2), BF16),) * 4,
        word(lax.axis_index("z")), word(lax.axis_index("dp")),
        *pieces, late[0], swap(late[1], "core"),
        words=2, limit=56, name="split_both",
    )
    pieces, late = spread_from(made[:4], "z"), spread_from(made[4:], "dp")
    back, pieces = lax.optimization_barrier((back, pieces))
    ghidden, *small = rows_back(back, entry, grad_in, gsecond, early_sums)
    share = call(
        share_kernel, shaped((2 * EARLY + HEAD + 16, width // 2), BF16),
        *pieces, *late, small[0], swap(small[1], "core"), name="share",
    )
    share, ghidden = lax.optimization_barrier((share, ghidden))

    a, b = call(
        halves_kernel,
        (shaped((2 * HALF, width // 2), BF16),) * 2,
        word(lax.axis_index("xl")), share, swap(share, "xl"),
        words=1, limit=8, name="halves",
    )
    a_pieces, b_pieces = spread_from([a] * 4, "z"), spread_from([b] * 4, "dp")
    a_pieces, b_pieces = lax.optimization_barrier((a_pieces, b_pieces))
    a, b = lax.optimization_barrier((placed(a_pieces, "z"), placed(b_pieces, "dp")))
    gathers, fars = [], []
    for array, axis in ((a, "dp"), (b, "z")):
        back, ahead = turn(array, axis, 1), turn(array, axis, -1)
        half = array.shape[0] // 2
        far_a, far_b = turn(back[:half], axis, 1), turn(ahead[half:], axis, -1)
        gathers.append([array, back, ahead])
        fars += [far_a, far_b]
    fars = jnp.concatenate(fars)
    gathers = [g + [swap(v, "core") for v in g] for g in gathers]
    gathers, fars = lax.optimization_barrier((gathers, fars))
    a, other_a, b, other_b = call(
        place_ring_kernel, (shaped((4 * a.shape[0], width // 2), BF16),) * 4,
        word(lax.axis_index("dp")), word(lax.axis_index("z")),
        *gathers[0], *gathers[1], fars, swap(fars, "core"),
        words=2, limit=24, name="place_ring",
    )
    a_spec = pl.BlockSpec((1, 4, 2, HALF, width // 2), lambda i: (i, 0, 0, 0, 0))
    b_spec = pl.BlockSpec((4, 1, 2, HALF, width // 2), lambda i: (0, i, 0, 0, 0))
    a, other_a, b, other_b = [v.reshape(4, 4, 2, HALF, width // 2) for v in (a, other_a, b, other_b)]
    up, down, qkv, proj, gain, shift, bias_qkv, bias_up, branch = pl.pallas_call(
        out_kernel,
        grid=(4,),
        out_shape=(
            shaped((width, 4 * width), F32),
            shaped((4 * width, width), F32),
            shaped((2, width // 2, 3 * width), F32),
            shaped((2, width // 2, width), F32),
            shaped((2, width), F32),
            shaped((2, width), F32),
            shaped((1, 3 * width), F32),
            shaped((1, 4 * width), F32),
            shaped((2, width), F32),
        ),
        in_specs=[SMEM, a_spec, b_spec, a_spec, b_spec],
        out_specs=(
            pl.BlockSpec((width, width), lambda i: (0, i)),
            pl.BlockSpec((width, width), lambda i: (i, 0)),
            pl.BlockSpec((2, 64, 3 * width), lambda i: (0, i, 0)),
            pl.BlockSpec((2, 64, width), lambda i: (0, i, 0)),
        )
        + tuple(
            pl.BlockSpec(shape, lambda i: (0, 0))
            for shape in ((2, width), (2, width), (1, 3 * width), (1, 4 * width), (2, width))
        ),
        scratch_shapes=[pltpu.VMEM((2, 16, width // 2), F32)],
        compiler_params=pltpu.CompilerParams(vmem_limit_bytes=32 * MIB),
        cost_estimate=pl.CostEstimate(flops=0, bytes_accessed=1024, transcendentals=0),
        name="out",
    )(core_word, a, b, other_a, other_b)
    qkv, proj = qkv.reshape(width, 3 * width), proj.reshape(width, width)
    return (
        result.reshape(1, micros, span, width),
        ghidden.reshape(1, micros, span, width),
        gain[None],
        shift[None],
        qkv[None],
        bias_qkv,
        proj[None],
        up[None],
        bias_up,
        down[None],
        branch[None],
    )


def solution(mesh):
    axes = ("section", "dp", "xl", "z", "core")
    fine = Mesh(mesh.devices.reshape(2, 4, 2, 4, 2), axes)
    spread = P(None, ("dp", "xl", "z", "core"), None)
    three, two = P("section", None, None), P("section", None)
    kept = P("section", None, ("dp", "xl", "z", "core"), None)
    in_specs = (
        spread, P("dp", None, None), three, three, three, two, three, three, two, three, three, spread,
    )
    out_specs = (kept, kept, three, three, three, two, three, three, two, three, three)
    return jax.shard_map(
        per_device, mesh=fine, in_specs=in_specs, out_specs=out_specs, check_vma=False
    )
```

```python
from functools import partial
import math

import jax
import jax.numpy as jnp
from jax import lax
from jax.experimental import pallas as pl
from jax.experimental.pallas import tpu as pltpu
from jax.sharding import Mesh, PartitionSpec as P

HEADS = 8
EPS = 1e-05
F32 = jnp.float32
BF16 = jnp.bfloat16
XZ = ("xl", "z")
LOG2E = math.log2(math.e)
SPAN = 128
HEAD = 64
TILE = 256
SCALE = 1.0 / math.sqrt(HEAD)
LAST = 32
EARLY = 144
HALF = 112


def dot(a, b, dims):
    return lax.dot_general(a, b, (dims, ((), ())), preferred_element_type=F32)


NN = ((1,), (0,))
NT = ((1,), (1,))
TN = ((0,), (0,))


def lanes_of(ref, block, at, lanes):
    return jnp.concatenate(
        [ref[2 * block, at : at + HEAD, lanes], ref[2 * block + 1, at : at + HEAD, lanes]], axis=1
    )


def both_of(mine_ref, other_ref, pair, at, lanes):
    return jnp.concatenate(
        [lanes_of(mine_ref, pair, at, lanes), lanes_of(other_ref, pair, at, lanes)], 1
    )


def lanes_at(micro):
    return pl.ds(pl.multiple_of(micro * SPAN, SPAN), SPAN)


def key_offsets():
    row = lax.broadcasted_iota(jnp.int32, (TILE, TILE), 0)
    return row + jnp.where(row >= SPAN, SPAN, 0)


def allowed_in(offsets, low, high, chunk, core, tile):
    side = core if chunk % 2 == 0 else 1 - core
    base = (chunk // 2) * (2 * TILE) + side * SPAN
    seen = offsets >= low - base
    if chunk // 2 == tile:
        seen = seen & (offsets <= high - base)
    return seen


def attend_kernel(core_ref, mine_ref, other_ref, low_ref, high_ref, out_ref, lse_ref, keys, scores):
    core = core_ref[0]
    offsets = key_offsets()

    def one_micro(micro, carry):
        lanes = lanes_at(micro)
        for chunk in range(8):
            ref, at = (mine_ref if chunk % 2 == 0 else other_ref), HEAD
            keys[chunk * TILE : (chunk + 1) * TILE, :] = lanes_of(ref, chunk // 2, at, lanes).T
        for tile in range(4):
            row = pl.ds(micro * 4 + tile, 1)
            low, high = low_ref[row, :], high_ref[row, :]
            query = lanes_of(mine_ref, tile, 0, lanes)
            top = jnp.full((8, TILE), -1e30, F32)
            for chunk in range(2 * tile + 2):
                rows = slice(chunk * TILE, (chunk + 1) * TILE)
                raw = dot(keys[rows, :], query, NN) * (SCALE * LOG2E)
                raw = jnp.where(allowed_in(offsets, low, high, chunk, core, tile), raw, -1e30)
                scores[rows, :] = raw
                top = jnp.maximum(top, jnp.max(raw.reshape(-1, 8, TILE), axis=0))
            top = jnp.max(top, axis=0, keepdims=True)
            total = jnp.zeros((8, TILE), F32)
            heard = jnp.zeros((HEAD, TILE), F32)
            for pair in range(tile + 1):
                rows = slice(2 * pair * TILE, 2 * (pair + 1) * TILE)
                weight = jnp.exp2(scores[rows, :] - top)
                total = total + jnp.sum(weight.reshape(-1, 8, TILE), axis=0)
                value = both_of(mine_ref, other_ref, pair, 2 * HEAD, lanes)
                heard = heard + dot(value, weight.astype(BF16), NN)
            total = jnp.sum(total, axis=0, keepdims=True)
            heard = (heard / total).astype(BF16)
            out_ref[2 * tile, :, lanes] = heard[:, :SPAN]
            out_ref[2 * tile + 1, :, lanes] = heard[:, SPAN:]
            lse_ref[row, :] = top + jnp.log2(total)
        return carry

    lax.fori_loop(0, 2, one_micro, 0)


def attend_back_kernel(
    core_ref,
    mine_ref,
    other_ref,
    low_ref,
    high_ref,
    out_ref,
    lse_ref,
    grad_ref,
    gmine_ref,
    gother_ref,
    keys,
    values,
    gkeys,
    gvalues,
):
    core = core_ref[0]
    offsets = key_offsets()

    def one_micro(micro, carry):
        lanes = lanes_at(micro)
        for chunk in range(8):
            rows = slice(chunk * TILE, (chunk + 1) * TILE)
            ref, at = (mine_ref if chunk % 2 == 0 else other_ref), HEAD
            keys[rows, :] = lanes_of(ref, chunk // 2, at, lanes).T
            values[rows, :] = lanes_of(ref, chunk // 2, at + HEAD, lanes).T
        for tile in range(4):
            row = pl.ds(micro * 4 + tile, 1)
            low, high, lse = low_ref[row, :], high_ref[row, :], lse_ref[row, :]
            query = lanes_of(mine_ref, tile, 0, lanes)
            grad = lanes_of(grad_ref, tile, 0, lanes)
            heard = lanes_of(out_ref, tile, 0, lanes)
            centre = jnp.sum(grad.astype(F32) * heard.astype(F32), axis=0, keepdims=True)
            gquery = jnp.zeros((HEAD, TILE), F32)
            for pair in range(tile + 1):
                rows = slice(2 * pair * TILE, 2 * (pair + 1) * TILE)
                raw = dot(keys[rows, :], query, NN) * (SCALE * LOG2E) - lse
                raws = [
                    jnp.where(
                        allowed_in(offsets, low, high, 2 * pair + side, core, tile),
                        raw[side * TILE : (side + 1) * TILE],
                        -1e30,
                    )
                    for side in range(2)
                ]
                prob = jnp.exp2(jnp.concatenate(raws, 0))
                gprob = dot(values[rows, :], grad, NN)
                gscore = (prob * (gprob - centre)).astype(BF16)
                gquery = gquery + dot(both_of(mine_ref, other_ref, pair, HEAD, lanes), gscore, NN)
                gkey = dot(query, gscore, NT)
                gvalue = dot(grad, prob.astype(BF16), NT)
                if pair == tile:
                    gkeys[:, rows], gvalues[:, rows] = gkey, gvalue
                else:
                    gkeys[:, rows] += gkey
                    gvalues[:, rows] += gvalue
            gquery = (gquery * SCALE).astype(BF16)
            gmine_ref[2 * tile, :HEAD, lanes] = gquery[:, :SPAN]
            gmine_ref[2 * tile + 1, :HEAD, lanes] = gquery[:, SPAN:]
        for chunk in range(8):
            ref, at = (gmine_ref, HEAD) if chunk % 2 == 0 else (gother_ref, 0)
            for half in range(2):
                cols = slice(chunk * TILE + half * SPAN, chunk * TILE + (half + 1) * SPAN)
                block = 2 * (chunk // 2) + half
                ref[block, at : at + HEAD, lanes] = (gkeys[:, cols] * SCALE).astype(BF16)
                ref[block, at + HEAD : at + 2 * HEAD, lanes] = gvalues[:, cols].astype(BF16)
        return carry

    lax.fori_loop(0, 2, one_micro, 0)


def front_kernel(
    start_ref, length_ref, hidden_ref, gain_ref, shift_ref, weight_ref, bias_ref, tiles_ref, second_ref, *copies
):
    rows, width = hidden_ref.shape
    lane = lax.broadcasted_iota(jnp.int32, (8, rows), 1)
    later = lane >= SPAN
    row = start_ref[0] + lane - jnp.where(later, SPAN, 0)
    first, second = [jnp.where(later, length_ref[0, 1, i], length_ref[0, 0, i]) for i in range(2)]
    begin = jnp.where(row >= first, first, 0) + jnp.where(row >= first + second, second, 0)
    order = lax.broadcasted_iota(jnp.int32, (8, rows), 0).astype(F32)
    ladder = jnp.exp(-math.log(10000.0) * (order * (2.0 / 16)))
    angle = ladder * (row - begin).astype(F32)
    cosine, sine = jnp.cos(angle), jnp.sin(angle)
    gain, shift = gain_ref[0].astype(F32), shift_ref[0].astype(F32)
    bias = bias_ref[...].astype(F32)
    xhat, _ = normed_of(hidden_ref[...].astype(F32))
    first = (xhat * gain[0:1] + shift[0:1]).astype(BF16)
    for copies_ref in copies:
        for block in range(copies_ref.shape[0]):
            copies_ref[block] = first
    second_ref[...] = (xhat * gain[1:2] + shift[1:2]).astype(BF16)
    for part in range(3):
        cols = slice(part * width, (part + 1) * width)
        made = (dot(first, weight_ref[:, cols], NN) + bias[:, cols]).T
        for head in range(HEADS):
            tile = made[head * HEAD : (head + 1) * HEAD]
            if part < 2:
                tile = turned(tile, cosine, sine)
            tiles_ref[head, part * HEAD : (part + 1) * HEAD, :] = tile.astype(BF16)


def back_kernel(
    core_ref, back_ref, hidden_ref, grad_ref, gsecond_ref, gain_ref, weight_ref, *refs
):
    early_refs = refs[: len(refs) - 2 if len(refs) == 2 else 1]
    ghidden_ref, *vector_refs, gqkv = refs[len(early_refs) :]
    width = hidden_ref.shape[1]
    rows = hidden_ref.shape[0]
    gfirst = jnp.zeros((rows, width), F32)
    ones = jnp.ones((8, rows), BF16)
    biases, gains, shifts = [], [], []
    for part in range(3):
        cols = slice(part * width, (part + 1) * width)
        for head in range(HEADS):
            gqkv[head * HEAD : (head + 1) * HEAD, :] = back_ref[head, part * HEAD : (part + 1) * HEAD, :]
        made = gqkv[...]
        gfirst = gfirst + dot(made.T, weight_ref[:, cols], NT)
        biases.append(dot(ones, made, NT)[:1])
    xhat, inv = normed_of(hidden_ref[...].astype(F32))
    gsecond = gsecond_ref[...]
    total = grad_ref[...].astype(F32)
    for which, grad in ((0, gfirst), (1, gsecond)):
        e = grad * gain_ref[which : which + 1, :]
        total = total + inv * (
            e - jnp.mean(e, -1, keepdims=True) - xhat * jnp.mean(e * xhat, -1, keepdims=True)
        )
        gains.append(jnp.sum(grad * xhat, 0, keepdims=True))
        shifts.append(jnp.sum(grad, 0, keepdims=True))
    ghidden_ref[...] = total.astype(BF16)
    if not vector_refs:
        return
    early = jnp.sum(early_refs[0][...], 0, keepdims=True)
    wide = gains + shifts + biases + [early[:, i * width : (i + 1) * width] for i in range(5)]
    lines = [v[:, half * width // 2 : (half + 1) * width // 2] for v in wide for half in range(2)]
    blank = [jnp.zeros((4, width // 2), F32)]
    first = jnp.concatenate(lines[:12] + blank, 0).astype(BF16)
    last = jnp.concatenate(lines[12:] + blank, 0).astype(BF16)
    ours_ref, theirs_ref = vector_refs
    ours_ref[...] = jnp.where(core_ref[0] == 0, first, last)
    theirs_ref[...] = jnp.where(core_ref[0] == 0, last, first)


def join_kernel(mine_ref, other_ref, cos_ref, sin_ref, *refs):
    out_ref = refs[-1]
    for block in range(8):
        if len(refs) > 1:
            out_ref[block, 3 * HEAD :, :] = refs[0][block]
        cosine, sine = cos_ref[block], -sin_ref[block]
        for part in range(3):
            rows = slice(part * HEAD, (part + 1) * HEAD)
            tile = mine_ref[block, rows, :].astype(F32)
            if part > 0:
                at = (part - 1) * HEAD
                tile = tile + other_ref[block, at : at + HEAD, :].astype(F32)
            if part < 2:
                tile = turned(tile, cosine, sine)
            out_ref[block, rows, :] = tile.astype(BF16)


def grad_kernel(section_ref, received_ref, own_ref, weight_ref, grad_ref, heard_ref):
    grad = jnp.where(section_ref[0] == 1, own_ref[...], received_ref[...])
    grad_ref[...] = grad
    made = dot(weight_ref[...], grad, NT).astype(BF16)
    for head in range(HEADS):
        heard_ref[head] = made[head * HEAD : (head + 1) * HEAD]


def early_terms_kernel(
    core_ref,
    second_ref,
    slope_ref,
    active_ref,
    grad_ref,
    heard_ref,
    down_ref,
    gup_ref,
    ours_ref,
    theirs_ref,
    sums_ref,
):
    core = core_ref[0]
    width = second_ref.shape[1]
    turned_second = second_ref[...].T
    grad = grad_ref[...]
    proj = dot(heard_ref[...], grad, NN).astype(BF16)
    sums_ref[:, 4 * width :] = jnp.sum(grad.astype(F32).reshape(-1, 8, width), 0)
    for block in range(4):
        cols = slice(block * width, (block + 1) * width)
        gup = (dot(grad, down_ref[cols, :], NT) * slope_ref[:, cols].astype(F32)).astype(BF16)
        gup_ref[:, cols] = gup
        sums_ref[:, cols] = jnp.sum(gup.astype(F32).reshape(-1, 8, width), 0)
        up = dot(turned_second, gup, NN).astype(BF16)
        down = dot(active_ref[:, cols].T, grad, NN).astype(BF16)
        first = proj[block * 64 : (block + 1) * 64]
        last = proj[256 + block * 64 : 256 + (block + 1) * 64]
        ours_ref[block, :width, :] = jnp.where(core == 0, up, down)
        theirs_ref[block, :width, :] = jnp.where(core == 0, down, up)
        ours_ref[block, width:, :] = jnp.where(core == 0, first, last)
        theirs_ref[block, width:, :] = jnp.where(core == 0, last, first)


def second_grad_kernel(gup_ref, up_ref, gsecond_ref):
    gsecond_ref[...] = dot(gup_ref[...], up_ref[...], NT)


def late_terms_kernel(core_ref, gqkv_ref, first_ref, ours_ref, theirs_ref):
    core = core_ref[0]
    total = jnp.zeros((3 * HEAD, first_ref.shape[2]), F32)
    for block in range(8):
        total = total + dot(gqkv_ref[block], first_ref[block], NN)
    total = jnp.concatenate([total, jnp.zeros((HEAD, total.shape[1]), F32)], 0).T
    half = total.shape[0] // 2
    upper, lower = total[:half].astype(BF16), total[half:].astype(BF16)
    ours_ref[...] = jnp.where(core == 0, upper, lower)
    theirs_ref[...] = jnp.where(core == 0, lower, upper)


def place_ring_kernel(dp_ref, z_ref, *refs):
    for group, at_ref in enumerate((dp_ref, dp_ref, z_ref, z_ref)):
        own, back, ahead = refs[3 * group : 3 * group + 3]
        far, target = refs[12 + group % 2], refs[14 + group]
        at, extent = at_ref[0], own.shape[0]
        for step, source in ((0, own), (3, back), (1, ahead)):
            start = pl.multiple_of(lax.rem(at + step, 4) * extent, 16)
            target[pl.ds(start, extent), :] = source[...]
        start = pl.multiple_of(lax.rem(at + 2, 4) * extent, 16)
        target[pl.ds(start, extent), :] = far[(group // 2) * extent : (group // 2 + 1) * extent]


def split_kernel(count, pieces, at_ref, *refs):
    sources, targets = refs[:count], refs[count:]
    extent = targets[0].shape[0]
    at = at_ref[0]
    for step in range(pieces):
        start = pl.multiple_of(lax.rem(at + step, pieces) * extent, extent)
        total = sources[0][pl.ds(start, extent), :].astype(F32)
        for source in sources[1:]:
            total = total + source[pl.ds(start, extent), :].astype(F32)
        targets[step][...] = total.astype(BF16)


def ring_kernel(at_ref, first_ref, last_ref, own_ref, next_ref, back_ref, far_a_ref, far_b_ref):
    at = at_ref[0]
    extent = own_ref.shape[0]

    def piece(step):
        rows = pl.ds(pl.multiple_of(lax.rem(at + step, 4) * extent, 16), extent)
        return (first_ref[rows, :].astype(F32) + last_ref[rows, :].astype(F32)).astype(BF16)

    own_ref[...] = piece(0)
    next_ref[...] = piece(1)
    back_ref[...] = piece(3)
    far = piece(2)
    far_a_ref[...] = far[: extent // 2]
    far_b_ref[...] = far[extent // 2 :]


def fold_kernel(next_ref, back_ref, far_a_ref, far_b_ref, to_next_ref, to_back_ref):
    half = far_a_ref.shape[0]
    total = next_ref[:half].astype(F32) + far_a_ref[...].astype(F32)
    to_next_ref[:half] = total.astype(BF16)
    to_next_ref[half:] = next_ref[half:]
    to_back_ref[:half] = back_ref[:half]
    total = back_ref[half:].astype(F32) + far_b_ref[...].astype(F32)
    to_back_ref[half:] = total.astype(BF16)


def split_both_kernel(z_ref, dp_ref, *refs):
    split_kernel(3, 4, z_ref, *refs[:3], *refs[5:9])
    split_kernel(2, 4, dp_ref, *refs[3:5], *refs[9:])


def place_kernel(at_ref, *refs):
    sources, target = refs[:-1], refs[-1]
    count, extent, at = len(sources), sources[0].shape[0], at_ref[0]
    for step, source in enumerate(sources):
        start = pl.multiple_of(lax.rem(at + count - step, count) * extent, extent)
        target[pl.ds(start, extent), :] = source[...]


def share_kernel(*refs):
    early, late, small, out_ref = refs[:4], refs[4:8], refs[8:10], refs[10]

    def total(sources):
        made = sources[0][...].astype(F32)
        for source in sources[1:]:
            made = made + source[...].astype(F32)
        return made.astype(BF16)

    made = total(early)
    rows, half = made.shape[0], made.shape[1] // 2
    out_ref[:rows, :] = made[:, :half]
    out_ref[rows : 2 * rows, :] = made[:, half:]
    out_ref[2 * rows : 2 * rows + HEAD, :] = total(late)
    out_ref[2 * rows + HEAD :, :] = total(small)


def out_kernel(
    core_ref,
    a_ref,
    b_ref,
    other_a_ref,
    other_b_ref,
    up_ref,
    down_ref,
    qkv_ref,
    proj_ref,
    gain_ref,
    shift_ref,
    qkv_bias_ref,
    up_bias_ref,
    branch_ref,
    vectors,
):
    core = core_ref[0]
    width = down_ref.shape[1]

    def parts(first_ref, second_ref):
        early, late = [], []
        for z in range(4):
            first = jnp.concatenate([first_ref[0, z, 0], first_ref[0, z, 1]], 1)
            second = jnp.concatenate([second_ref[z, 0, 0, :LAST], second_ref[z, 0, 1, :LAST]], 1)
            early += [first, second]
        for half in range(2):
            late += [second_ref[z, 0, half, LAST : LAST + HEAD] for z in range(4)]
        return jnp.concatenate(early, 0).astype(F32), [v.astype(F32) for v in late]

    mine, late = parts(a_ref, b_ref)
    other, other_late = parts(other_a_ref, other_b_ref)
    low, high = jnp.where(core == 0, mine, other), jnp.where(core == 0, other, mine)
    up_ref[...] = low[:width]
    down_ref[...] = high[:width]
    proj_ref[0] = low[width:]
    proj_ref[1] = high[width:]
    for head in range(HEADS):
        low = jnp.where(core == 0, late[head], other_late[head])
        high = jnp.where(core == 0, other_late[head], late[head])
        for part in range(3):
            at = part * width + head * HEAD
            qkv_ref[0, :, at : at + HEAD] = low[:, part * HEAD : (part + 1) * HEAD]
            qkv_ref[1, :, at : at + HEAD] = high[:, part * HEAD : (part + 1) * HEAD]
    step = pl.program_id(0)

    def vector_sum(ref):
        return sum(ref[z, 0, half, LAST + HEAD :].astype(F32) for z in range(4) for half in range(2))

    low, high = vector_sum(b_ref), vector_sum(other_b_ref)

    @pl.when(step == 0)
    def _():
        vectors[0], vectors[1] = low, high

    @pl.when(step > 0)
    def _():
        vectors[0] += low
        vectors[1] += high

    @pl.when(step == 3)
    def _():
        mine, other = vectors[0], vectors[1]
        first = jnp.where(core == 0, mine, other)
        last = jnp.where(core == 0, other, mine)
        lines = [first[i : i + 1] for i in range(12)] + [last[i : i + 1] for i in range(12)]
        wide = [jnp.concatenate(lines[2 * i : 2 * i + 2], 1) for i in range(12)]
        for row in range(2):
            gain_ref[row : row + 1, :] = wide[row]
            shift_ref[row : row + 1, :] = wide[2 + row]
            branch_ref[row : row + 1, :] = wide[11]
        qkv_bias_ref[...] = jnp.concatenate(wide[4:7], 1)
        up_bias_ref[...] = jnp.concatenate(wide[7:11], 1)


def halves_kernel(at_ref, mine_ref, other_ref, a_ref, b_ref):
    at = at_ref[0]
    early = EARLY
    total = mine_ref[: 2 * early].astype(F32) + other_ref[: 2 * early].astype(F32)
    total = total.astype(BF16)
    for half in range(2):
        a_ref[half * HALF : (half + 1) * HALF] = total[half * early : half * early + HALF]
        b_ref[half * HALF : half * HALF + LAST] = total[half * early + HALF : (half + 1) * early]
    for source, to in ((mine_ref, at), (other_ref, 1 - at)):
        rows = pl.ds(pl.multiple_of(to * HALF + LAST, 16), HALF - LAST)
        b_ref[rows, :] = source[2 * early :, :]


VMEM = pl.BlockSpec(memory_space=pltpu.VMEM)
SMEM = pl.BlockSpec(memory_space=pltpu.SMEM)
MIB = 1024 * 1024


def shaped(shape, dtype):
    return jax.ShapeDtypeStruct(shape, dtype)


def call(kernel, outs, *args, words=0, limit=12, scratch=(), name=None):
    single = not isinstance(outs, tuple)
    shapes = (outs,) if single else outs
    made = pl.pallas_call(
        kernel,
        out_shape=shapes,
        in_specs=[SMEM] * words + [VMEM] * (len(args) - words),
        out_specs=tuple(VMEM for _ in shapes),
        scratch_shapes=list(scratch),
        compiler_params=pltpu.CompilerParams(vmem_limit_bytes=limit * MIB),
        cost_estimate=pl.CostEstimate(flops=0, bytes_accessed=1024, transcendentals=0),
        name=name,
    )(*args)
    return made[0] if single else made


def attend(core, mine, other, low, high):
    return call(
        attend_kernel,
        (shaped((8, HEAD, 2 * SPAN), BF16), shaped((8, TILE), F32)),
        core, mine, other, low, high,
        words=1, limit=10,
        scratch=[pltpu.VMEM((2048, HEAD), BF16), pltpu.VMEM((2048, TILE), F32)],
        name="attend",
    )


def attend_back(core, mine, other, low, high, out, lse, grad):
    return call(
        attend_back_kernel,
        (shaped((8, 3 * HEAD, 2 * SPAN), BF16), shaped((8, 2 * HEAD, 2 * SPAN), BF16)),
        core, mine, other, low, high, out, lse, grad,
        words=1, limit=10,
        scratch=[
            pltpu.VMEM((2048, HEAD), BF16),
            pltpu.VMEM((2048, HEAD), BF16),
            pltpu.VMEM((HEAD, 2048), F32),
            pltpu.VMEM((HEAD, 2048), F32),
        ],
        name="attend_back",
    )


def swap(array, axis):
    return lax.ppermute(array, axis, [(0, 1), (1, 0)])


def word(value):
    return value.astype(jnp.int32).reshape(1)


def spread_from(pieces, axis):
    count = len(pieces)
    return [pieces[0]] + [
        lax.ppermute(pieces[s], axis, [(i, (i + s) % count) for i in range(count)])
        for s in range(1, count)
    ]


def turn(array, axis, by):
    count = lax.axis_size(axis)
    return lax.ppermute(array, axis, [(i, (i + by) % count) for i in range(count)])


def placed(pieces, axis):
    extent, width = pieces[0].shape
    return call(
        place_kernel, shaped((len(pieces) * extent, width), BF16),
        word(lax.axis_index(axis)), *pieces,
        words=1, limit=8, name="place",
    )


def normed_of(hidden):
    centred = hidden - jnp.mean(hidden, -1, keepdims=True)
    inv = lax.rsqrt(jnp.mean(centred * centred, -1, keepdims=True) + EPS)
    return centred * inv, inv


def turned(tile, cosine, sine):
    first, second = tile[:8], tile[8:16]
    return jnp.concatenate(
        [first * cosine - second * sine, second * cosine + first * sine, tile[16:]], 0
    )


def per_device(
    inputs,
    lengths,
    norm_gain,
    norm_bias,
    qkv_weight,
    qkv_bias,
    proj_weight,
    up_weight,
    up_bias,
    down_weight,
    branch_bias,
    cotangent,
):
    section = lax.axis_index("section")
    core = lax.axis_index("core")
    block = lax.axis_index(XZ)
    micros, span, width = inputs.shape
    rows = micros * span
    gains = norm_gain[0].astype(F32)
    w_qkv, w_proj, w_up, w_down = qkv_weight[0], proj_weight[0], up_weight[0], down_weight[0]
    b_up = up_bias[0].astype(F32)
    b_branch = jnp.sum(branch_bias[0].astype(F32), 0)
    core_word = word(core)

    def front(hidden, copies):
        tiles, second, *firsts = call(
            front_kernel,
            (shaped((HEADS, 3 * HEAD, rows), BF16), shaped((rows, width), BF16))
            + (shaped((HEADS, rows, width), BF16),) * copies,
            word((2 * block + core) * span), lengths, hidden, norm_gain, norm_bias, w_qkv, qkv_bias,
            words=2, limit=12 if copies else 56, name="front",
        )
        return firsts, second, tiles

    entry = inputs.reshape(rows, width)
    first_front = front(entry, 0)
    tiles, lengths = lax.optimization_barrier((first_front[-1], lengths))
    first_front = first_front[:-1] + (tiles,)
    one, two, three = [lengths[0][:, i] for i in range(3)]
    ends = jnp.stack([one, one + two, one + two + three], -1)

    def begin_of(row):
        after = row[None, :, None] >= ends[:, None, :]
        return jnp.sum(jnp.where(after, lengths[0][:, None, :], 0), -1)

    heard_rows = (
        (2 * jnp.arange(8, dtype=jnp.int32)[:, None] + core) * span
        + jnp.arange(span, dtype=jnp.int32)[None]
    ).reshape(-1)
    low = begin_of(heard_rows).reshape(8, TILE)
    high = jnp.broadcast_to(heard_rows[None], (micros, 8 * span)).reshape(8, TILE)
    ladder = jnp.exp(-math.log(10000.0) * (jnp.arange(8, dtype=F32) * (2.0 / 16)))
    heard_position = (heard_rows[None] - begin_of(heard_rows)).reshape(micros, 8, span)
    heard_position = jnp.moveaxis(heard_position, 0, 1).reshape(8, 1, rows).astype(F32)
    heard_angle = ladder[None, :, None] * heard_position
    heard_cosine, heard_sine = jnp.cos(heard_angle), jnp.sin(heard_angle)

    def mlp_of(second):
        up = dot(second, w_up, NN) + b_up
        phi = 0.5 * (1.0 + lax.erf(up * (1.0 / math.sqrt(2.0))))
        bell = jnp.exp(-0.5 * up * up) * (1.0 / math.sqrt(2.0 * math.pi))
        active = (up * phi).astype(BF16)
        slope = (phi + up * bell).astype(BF16)
        return active, slope

    def forward(hidden, firsts, second, tiles):
        mine = lax.all_to_all(tiles, XZ, 0, 0, tiled=True)
        other = swap(mine, "core")
        active, slope = mlp_of(second)
        base = hidden.astype(F32) + dot(active, w_down, NN) + b_branch
        heard, lse = attend(core_word, mine, other, low, high)
        return base, firsts, second, mine, other, active, slope, heard, lse

    def finish(base, heard_rows):
        return (base + dot(heard_rows, w_proj, TN)).astype(BF16)

    def heard_grad(received, own):
        grad_in, ggo = call(
            grad_kernel,
            (shaped((rows, width), BF16), shaped((HEADS, HEAD, rows), BF16)),
            word(section), received, own, w_proj,
            words=1, name="grad",
        )
        return grad_in, lax.all_to_all(ggo, XZ, 0, 0, tiled=True)

    def joined(gmine, gother, *along):
        return call(
            join_kernel, shaped((HEADS, (3 + len(along)) * HEAD, rows), BF16),
            gmine, swap(gother, "core"), heard_cosine, heard_sine, *along, name="join",
        )

    def rows_back(back, hidden, grad_in, gsecond, *early_sums):
        vectors = (shaped((16, width // 2), BF16),) * 2 if early_sums else ()
        return call(
            back_kernel,
            (shaped((rows, width), BF16),) + vectors,
            core_word, back, hidden, grad_in, gsecond, gains, w_qkv, *early_sums,
            words=1, scratch=[pltpu.VMEM((width, rows), BF16)], limit=56, name="back",
        )

    def mlp_back(grad_in, slope):
        gup = (dot(grad_in, w_down, NT) * slope.astype(F32)).astype(BF16)
        return gup, dot(gup, w_up, NT)

    loss_grad = cotangent.reshape(rows, width)
    grad_in, ggo = heard_grad(loss_grad, loss_grad)
    base, *_, heard, _ = forward(entry, *first_front)
    heard_rows = lax.all_to_all(heard, XZ, 0, 0, tiled=True).reshape(width, rows)
    heard_rows, base = lax.optimization_barrier((heard_rows, base))
    sent = finish(base, heard_rows)
    received = lax.ppermute(sent, "section", [(0, 1)])
    received, ggo = lax.optimization_barrier((received, ggo))
    entry = jnp.where(section == 1, received, entry)
    base, (firsts,), second, mine, other, active, slope, heard, lse = forward(entry, *front(entry, 1))
    mine, firsts = lax.optimization_barrier((mine, firsts))
    first_all = lax.all_to_all(firsts, XZ, 0, 0, tiled=True)
    _, gsecond = mlp_back(grad_in, slope)
    gmine, gother = attend_back(core_word, mine, other, low, high, heard, lse, ggo)
    back, first_all = lax.optimization_barrier((joined(gmine, gother, heard), first_all))
    back = lax.all_to_all(back, XZ, 0, 0, tiled=True)
    (sent_back,) = rows_back(back, entry, grad_in, gsecond)
    received = lax.ppermute(sent_back, "section", [(1, 0)])
    _, back = lax.optimization_barrier((sent_back, back))
    heard_rows = back[:, 3 * HEAD :].reshape(width, rows)
    result = finish(base, heard_rows)
    received, result, heard_rows = lax.optimization_barrier((received, result, heard_rows))
    grad_in, ggo = heard_grad(received, loss_grad)
    gup, *early, early_sums = call(
        early_terms_kernel,
        (shaped((rows, 4 * width), BF16),)
        + (shaped((4, width + 64, width), BF16),) * 2
        + (shaped((8, 5 * width), F32),),
        core_word, second, slope, active, grad_in, heard_rows, w_down,
        words=1, limit=56, name="early_terms",
    )
    ggo, early = lax.optimization_barrier((ggo, early))
    early = [v.reshape(-1, width) for v in early]
    whole, part = shaped((4 * EARLY, width), BF16), shaped((2 * EARLY, width), BF16)
    pieces = call(
        ring_kernel, (whole, whole, whole, part, part),
        word(lax.axis_index("dp")), early[0], swap(early[1], "core"),
        words=1, limit=56, name="ring",
    )
    ggo, pieces = lax.optimization_barrier((ggo, pieces))
    own, to_next, to_back, far_a, far_b = pieces
    far_a, far_b = turn(far_a, "dp", 1), turn(far_b, "dp", -1)
    gmine, gother = attend_back(core_word, mine, other, low, high, heard, lse, ggo)
    gmine, gother, far_a, far_b = lax.optimization_barrier((gmine, gother, far_a, far_b))
    to_next, to_back = call(fold_kernel, (whole, whole), to_next, to_back, far_a, far_b, name="fold")
    gmine = joined(gmine, gother)
    gmine, to_next, to_back = lax.optimization_barrier((gmine, to_next, to_back))
    pieces = [own, turn(to_next, "dp", 1), turn(to_back, "dp", -1)]
    late = call(
        late_terms_kernel,
        (shaped((width // 2, width // 2), BF16),) * 2,
        core_word, gmine, first_all,
        words=1, limit=56, name="late_terms",
    )
    late, gup = lax.optimization_barrier((late, gup))
    gsecond = call(second_grad_kernel, shaped((rows, width), F32), gup, w_up, name="second_grad")
    back = lax.all_to_all(gmine, XZ, 0, 0, tiled=True)
    pieces, late, gsecond = lax.optimization_barrier((pieces, late, gsecond))
    made = call(
        split_both_kernel,
        (shaped((EARLY, width), BF16),) * 4 + (shaped((HEAD, width // 2), BF16),) * 4,
        word(lax.axis_index("z")), word(lax.axis_index("dp")),
        *pieces, late[0], swap(late[1], "core"),
        words=2, limit=56, name="split_both",
    )
    pieces, late = spread_from(made[:4], "z"), spread_from(made[4:], "dp")
    back, pieces = lax.optimization_barrier((back, pieces))
    ghidden, *small = rows_back(back, entry, grad_in, gsecond, early_sums)
    share = call(
        share_kernel, shaped((2 * EARLY + HEAD + 16, width // 2), BF16),
        *pieces, *late, small[0], swap(small[1], "core"), name="share",
    )
    share, ghidden = lax.optimization_barrier((share, ghidden))

    a, b = call(
        halves_kernel,
        (shaped((2 * HALF, width // 2), BF16),) * 2,
        word(lax.axis_index("xl")), share, swap(share, "xl"),
        words=1, limit=8, name="halves",
    )
    a_pieces, b_pieces = spread_from([a] * 4, "z"), spread_from([b] * 4, "dp")
    a_pieces, b_pieces = lax.optimization_barrier((a_pieces, b_pieces))
    a, b = lax.optimization_barrier((placed(a_pieces, "z"), placed(b_pieces, "dp")))
    gathers, fars = [], []
    for array, axis in ((a, "dp"), (b, "z")):
        back, ahead = turn(array, axis, 1), turn(array, axis, -1)
        half = array.shape[0] // 2
        far_a, far_b = turn(back[:half], axis, 1), turn(ahead[half:], axis, -1)
        gathers.append([array, back, ahead])
        fars += [far_a, far_b]
    fars = jnp.concatenate(fars)
    gathers = [g + [swap(v, "core") for v in g] for g in gathers]
    gathers, fars = lax.optimization_barrier((gathers, fars))
    a, other_a, b, other_b = call(
        place_ring_kernel, (shaped((4 * a.shape[0], width // 2), BF16),) * 4,
        word(lax.axis_index("dp")), word(lax.axis_index("z")),
        *gathers[0], *gathers[1], fars, swap(fars, "core"),
        words=2, limit=24, name="place_ring",
    )
    a_spec = pl.BlockSpec((1, 4, 2, HALF, width // 2), lambda i: (i, 0, 0, 0, 0))
    b_spec = pl.BlockSpec((4, 1, 2, HALF, width // 2), lambda i: (0, i, 0, 0, 0))
    a, other_a, b, other_b = [v.reshape(4, 4, 2, HALF, width // 2) for v in (a, other_a, b, other_b)]
    up, down, qkv, proj, gain, shift, bias_qkv, bias_up, branch = pl.pallas_call(
        out_kernel,
        grid=(4,),
        out_shape=(
            shaped((width, 4 * width), F32),
            shaped((4 * width, width), F32),
            shaped((2, width // 2, 3 * width), F32),
            shaped((2, width // 2, width), F32),
            shaped((2, width), F32),
            shaped((2, width), F32),
            shaped((1, 3 * width), F32),
            shaped((1, 4 * width), F32),
            shaped((2, width), F32),
        ),
        in_specs=[SMEM, a_spec, b_spec, a_spec, b_spec],
        out_specs=(
            pl.BlockSpec((width, width), lambda i: (0, i)),
            pl.BlockSpec((width, width), lambda i: (i, 0)),
            pl.BlockSpec((2, 64, 3 * width), lambda i: (0, i, 0)),
            pl.BlockSpec((2, 64, width), lambda i: (0, i, 0)),
        )
        + tuple(
            pl.BlockSpec(shape, lambda i: (0, 0))
            for shape in ((2, width), (2, width), (1, 3 * width), (1, 4 * width), (2, width))
        ),
        scratch_shapes=[pltpu.VMEM((2, 16, width // 2), F32)],
        compiler_params=pltpu.CompilerParams(vmem_limit_bytes=32 * MIB),
        cost_estimate=pl.CostEstimate(flops=0, bytes_accessed=1024, transcendentals=0),
        name="out",
    )(core_word, a, b, other_a, other_b)
    qkv, proj = qkv.reshape(width, 3 * width), proj.reshape(width, width)
    return (
        result.reshape(1, micros, span, width),
        ghidden.reshape(1, micros, span, width),
        gain[None],
        shift[None],
        qkv[None],
        bias_qkv,
        proj[None],
        up[None],
        bias_up,
        down[None],
        branch[None],
    )


def solution(mesh):
    axes = ("section", "dp", "xl", "z", "core")
    fine = Mesh(mesh.devices.reshape(2, 4, 2, 4, 2), axes)
    spread = P(None, ("dp", "xl", "z", "core"), None)
    three, two = P("section", None, None), P("section", None)
    kept = P("section", None, ("dp", "xl", "z", "core"), None)
    in_specs = (
        spread, P("dp", None, None), three, three, three, two, three, three, two, three, three, spread,
    )
    out_specs = (kept, kept, three, three, three, two, three, three, two, three, three)
    return jax.shard_map(
        per_device, mesh=fine, in_specs=in_specs, out_specs=out_specs, check_vma=False
    )
```
